32 devices in a mesh: dp: 4 (over z), fsdp: 8 (over y, x, core).
Axes of the slice: x: 2, y: 2, z: 4, core: 2. Of those that a mesh axis runs over, the one named last changes fastest.
Arguments:
- features: bfloat16 [12544, 512], P(('dp', 'fsdp')), may hold values from -6 to 6
- shortcut: bfloat16 [12544, 2048], P(('dp', 'fsdp')), may hold values from -6 to 6
- conv_weight: bfloat16 [2048, 512], P('fsdp'), may hold values from -0.25 to 0.25
- proj_weight: bfloat16 [2048, 256], P('fsdp'), may hold values from -0.125 to 0.125
- partner: int32 [256], P(('dp', 'fsdp')), may hold values from 0 to 31, as said below
Outputs:
- grad_conv: float32 [2048, 512], P('fsdp')
- grad_proj: float32 [2048, 256], P('fsdp')
- group_loss: float32 [8], P('fsdp')
The draws below stay inside these ranges and needn't reach their ends.
Inputs may be any that keep to these rules, and one draw needn't show every extreme that they name: Each image's partner is another image of its group, given as its member index, and the pairing is mutual: the partner of the partner is the image itself.
All inputs are finite; a program needn't handle non-finite values.
Results may differ from the reference program's by a relative error of at most 0.035.
Values may be sent and summed in bfloat16 or wider, within the bound.
No kernel may reach another device: no remote copies, remote signals or barrier semaphores. Data moves between devices by JAX's collectives and lax.ppermute only.
A program may use at most 64 MiB of HBM per device.

```python
import jax
import jax.numpy as jnp
from jax import lax

C_IN = 512
C_OUT = 2048
EMB = 256
POS = 49
IMG_DEV = 8
ROWS = 392
GROUP = 32
IMAGES = 256
N_DP = 4
N_FSDP = 8


def draw_partner(key, part):
    key_list = jax.random.split(key, N_FSDP)

    def one_group(group_key):
        shuffled = jax.random.permutation(group_key, GROUP)
        couples = shuffled.reshape(GROUP // 2, 2).astype(jnp.int32)
        partner_of = jnp.zeros((GROUP,), jnp.int32)
        partner_of = partner_of.at[couples[:, 0]].set(couples[:, 1])
        partner_of = partner_of.at[couples[:, 1]].set(couples[:, 0])
        return partner_of
    grouped = jax.vmap(one_group)(key_list)
    return grouped.reshape(N_FSDP, N_DP, IMG_DEV).transpose(1, 0, 2).reshape(N_DP * N_FSDP * IMG_DEV)


def level_of(stream_key, dims, cuts, low, high):
    level, own = 1.0, jax.random.fold_in(stream_key, 6)
    for position, parts in cuts:
        steps = jnp.exp(jax.random.uniform(jax.random.fold_in(own, position), (parts,), jnp.float32, low / len(cuts), high / len(cuts)))
        level = level * jnp.repeat(steps, dims[position] // parts).reshape([-1 if axis == position else 1 for axis in range(len(dims))])
    return level


def normal_values(key, shape, scale, bound, shards=(), kind=jnp.bfloat16):
    array = scale * jax.random.normal(key, shape, jnp.float32)
    if shards:
        array = array * level_of(key, shape, shards, -0.22, 0.18)
    return jnp.clip(array, -bound, bound).astype(kind)


def setup_inputs(seed: int = 0) -> dict:
    keys = jax.random.split(jax.random.key(seed), 6)
    features = normal_values(keys[0], (IMAGES * POS, C_IN), 1.0, 6.0, ((0, 32),))
    shortcut = normal_values(keys[1], (IMAGES * POS, C_OUT), 1.0, 6.0, ((0, 32),))
    conv_weight = normal_values(keys[2], (C_OUT, C_IN), C_IN ** -0.5, 0.25, ((0, 8),))
    proj_weight = normal_values(keys[3], (C_OUT, EMB), C_OUT ** -0.5, 0.125, ((0, 8),))
    partner = draw_partner(jax.random.fold_in(keys[5], 71), 0)
    return {"features": features, "shortcut": shortcut, "conv_weight": conv_weight, "proj_weight": proj_weight, "partner": partner}


gamma_weight = 3.0
epsilon = 1e-06

def conv_preact(feat_block, short_block, conv_weight):
    return lax.dot_general(feat_block, conv_weight, (((1,), (1,)), ((), ())), preferred_element_type=jnp.float32) + short_block.astype(jnp.float32)

def pool_rows(hidden):
    return lax.optimization_barrier(jnp.mean(hidden.reshape(IMG_DEV, POS, hidden.shape[-1]), axis=1))

def group_terms(embed_group, partner_group):
    count = embed_group.shape[0]
    center = lax.optimization_barrier(jnp.mean(embed_group, axis=0))
    spread = 2.0 * jnp.mean(lax.optimization_barrier(jnp.sum((embed_group - center) ** 2, axis=1)))
    squares = lax.optimization_barrier(jnp.sum(embed_group * embed_group, axis=1))
    inner = jnp.dot(embed_group, embed_group.T, precision=lax.Precision.HIGHEST)
    kernel = jnp.exp(-(squares[:, None] + squares[None, :] - 2.0 * inner) / (2.0 * spread))
    row_mean = lax.optimization_barrier(jnp.mean(kernel, axis=1))
    total_mean = jnp.mean(row_mean)
    centered = kernel - row_mean[:, None] - row_mean[None, :] + total_mean
    scale_sq = float(count - 1) ** 2
    root = jnp.sqrt(jnp.sum(centered * centered) / scale_sq + epsilon)
    onehot = (partner_group[:, None] == jnp.arange(count, dtype=jnp.int32)[None, :]).astype(jnp.float32)
    positive = jnp.sum(kernel * onehot) / count
    loss_value = -(positive - total_mean) + gamma_weight * root
    coeff = (-onehot / count + 1.0 / (count * count) + gamma_weight * centered / (scale_sq * root)) / N_FSDP
    weighted = coeff * kernel
    grad_embed = -(2.0 / spread) * (lax.optimization_barrier(jnp.sum(weighted, axis=1))[:, None] * embed_group - jnp.dot(weighted, embed_group, precision=lax.Precision.HIGHEST))
    return (loss_value, grad_embed)

def reference(features, shortcut, conv_weight, proj_weight, partner):
    blocks = N_DP * N_FSDP
    feat_blocks = features.reshape(blocks, ROWS, C_IN)
    short_blocks = shortcut.reshape(blocks, ROWS, C_OUT)

    def forward_block(operands):
        feat_block, short_block = operands
        hidden = jnp.maximum(conv_preact(feat_block, short_block, conv_weight), 0.0)
        return pool_rows(hidden).astype(jnp.bfloat16)
    pooled = lax.map(forward_block, (feat_blocks, short_blocks))
    embed = jnp.dot(pooled.reshape(IMAGES, C_OUT), proj_weight, preferred_element_type=jnp.float32)
    embed_groups = embed.reshape(N_DP, N_FSDP, IMG_DEV, EMB).transpose(1, 0, 2, 3).reshape(N_FSDP, GROUP, EMB)
    partner_groups = partner.reshape(N_DP, N_FSDP, IMG_DEV).transpose(1, 0, 2).reshape(N_FSDP, GROUP)
    losses, grad_groups = lax.map(lambda operands: group_terms(operands[0], operands[1]), (embed_groups, partner_groups))
    grad_embed = grad_groups.reshape(N_FSDP, N_DP, IMG_DEV, EMB).transpose(1, 0, 2, 3).astype(jnp.bfloat16)
    feat_grid = features.reshape(N_DP, N_FSDP, ROWS, C_IN)
    short_grid = shortcut.reshape(N_DP, N_FSDP, ROWS, C_OUT)
    pooled_grid = pooled.reshape(N_DP, N_FSDP, IMG_DEV, C_OUT)

    def device_term(operands):
        feat_block, short_block, pooled_block, grad_block = operands
        preact = conv_preact(feat_block, short_block, conv_weight)
        grad_pool = jnp.dot(grad_block, proj_weight.T, preferred_element_type=jnp.float32) / POS
        spread_rows = jnp.repeat(grad_pool, POS, axis=0)
        grad_hidden = jnp.where(preact > 0, spread_rows, 0.0).astype(jnp.bfloat16)
        conv_part = lax.dot_general(grad_hidden, feat_block, (((0,), (0,)), ((), ())), preferred_element_type=jnp.float32)
        proj_part = lax.dot_general(pooled_block, grad_block, (((0,), (0,)), ((), ())), preferred_element_type=jnp.float32)
        return jnp.concatenate([conv_part, proj_part], axis=1).astype(jnp.bfloat16)

    def add_slab(running, slab):
        terms = lax.map(device_term, slab)
        return (running + lax.optimization_barrier(jnp.sum(terms.astype(jnp.float32), axis=0)), None)
    start_total = jnp.zeros((C_OUT, C_IN + EMB), jnp.float32)
    total, _ = lax.scan(add_slab, start_total, (feat_grid, short_grid, pooled_grid, grad_embed))
    return (total[:, :C_IN], total[:, C_IN:], losses.astype(jnp.float32))
```

```python
import functools

import jax
import jax.numpy as jnp
from jax import lax
from jax.experimental import pallas as pl
from jax.experimental.pallas import tpu as pltpu
from jax.sharding import PartitionSpec as P

POS = 49
GAMMA = 3.0
EPSILON = 1e-06
BF = jnp.bfloat16
F32 = jnp.float32
NT = (((1,), (1,)), ((), ()))
TN = (((0,), (0,)), ((), ()))
VMEM_LIMIT = 24 * 1024 * 1024


def dot(a, b, dims=(((1,), (0,)), ((), ()))):
    return lax.dot_general(a, b, dims, preferred_element_type=F32)


def vspec():
    return pl.BlockSpec(memory_space=pltpu.VMEM)


def params():
    return pltpu.CompilerParams(vmem_limit_bytes=VMEM_LIMIT)


def image_of_row(shape, row_dim, image_dim):
    row = lax.broadcasted_iota(jnp.int32, shape, row_dim)
    first = lax.broadcasted_iota(jnp.int32, shape, image_dim) * POS
    return jnp.where((row >= first) & (row < first + POS), 1.0, 0.0).astype(BF)


def forward_block(feat, short, conv, pick):
    hidden = jnp.maximum(dot(feat, conv, NT) + short.astype(F32), 0.0)
    mask = jnp.where(hidden > 0, 1.0, 0.0).astype(BF)
    pooled = dot(pick, hidden.astype(BF)) / POS
    return mask, pooled


def forward_kernel(blocks, images, cols_ref, f_own, f_sib, *refs):
    shorts, convs = refs[: 2 * blocks], refs[2 * blocks : 3 * blocks]
    outs = refs[3 * blocks :]
    pick = image_of_row((images, f_own.shape[0]), 1, 0)
    for j in range(blocks):
        conv = convs[j][...]
        m_own, p_own = forward_block(f_own[...], shorts[2 * j][...], conv, pick)
        m_sib, p_sib = forward_block(f_sib[...], shorts[2 * j + 1][...], conv, pick)
        outs[3 * j][...] = m_own
        outs[3 * j + 1][...] = m_sib
        outs[3 * j + 2][...] = jnp.concatenate([p_own, p_sib], axis=0).astype(BF)


def last_forward_kernel(total, images, cols_ref, f_own, f_sib, s_own, s_sib, conv_ref, partner, *refs):
    pooled, projs = refs[: total - 1], refs[total - 1 : 2 * total - 1]
    m_own_ref, m_sib_ref, pooled_ref, mine_ref, send_ref = refs[2 * total - 1 :]
    pick = image_of_row((images, f_own.shape[0]), 1, 0)
    embed = jnp.zeros((2 * images, projs[0].shape[1]), F32)
    for j in range(total - 1):
        embed = embed + dot(pooled[j][...], projs[j][...])
    conv = conv_ref[...]
    m_own, p_own = forward_block(f_own[...], s_own[...], conv, pick)
    m_sib, p_sib = forward_block(f_sib[...], s_sib[...], conv, pick)
    m_own_ref[...] = m_own
    m_sib_ref[...] = m_sib
    last = jnp.concatenate([p_own, p_sib], axis=0).astype(BF)
    pooled_ref[...] = last
    embed = embed + dot(last, projs[total - 1][...])
    half = embed.shape[1] // 2
    whole = jnp.broadcast_to(partner[...], (images, half))
    none = jnp.zeros((images, half), F32)
    mine_ref[0 : 2 * images] = embed
    mine_ref[2 * images :] = jnp.concatenate([whole, none], axis=1)
    send_ref[0:images] = embed[images:]
    send_ref[images : 2 * images] = embed[:images]
    send_ref[2 * images :] = jnp.concatenate([none, whole], axis=1)


def column_block(j, side, i, cols):
    return (0, cols[j])


def forward_specs(rows, width, count, picks):
    return [pl.BlockSpec((rows, width), lambda i, cols: (0, 0))] * 2, [
        pl.BlockSpec((rows, count), functools.partial(column_block, j, side))
        for j in picks
        for side in (0, 1)
    ]


def whole_spec(shape):
    return pl.BlockSpec(shape, lambda i, cols: (0,) * len(shape))


def forward(cols, f_own, f_sib, s_own, s_sib, convs, images):
    rows, width = f_own.shape
    count = convs[0].shape[0]
    blocks = len(convs)
    feat_specs, short_specs = forward_specs(rows, width, count, range(blocks))
    shapes = [(rows, count), (rows, count), (2 * images, count)] * blocks
    outs = pl.pallas_call(
        functools.partial(forward_kernel, blocks, images),
        grid_spec=pltpu.PrefetchScalarGridSpec(
            num_scalar_prefetch=1,
            grid=(1,),
            in_specs=feat_specs + short_specs + [whole_spec(c.shape) for c in convs],
            out_specs=[whole_spec(s) for s in shapes],
        ),
        out_shape=[jax.ShapeDtypeStruct(s, BF) for s in shapes],
        compiler_params=params(),
        cost_estimate=pl.CostEstimate(
            flops=4 * blocks * rows * width * count, bytes_accessed=8 * blocks * rows * count, transcendentals=0
        ),
        name="forward_blocks",
    )(cols, f_own, f_sib, *([s_own, s_sib] * blocks), *convs)
    return [outs[3 * j : 3 * j + 3] for j in range(blocks)]


def last_forward(cols, f_own, f_sib, s_own, s_sib, conv, partner, pooled, projs, images):
    rows, width = f_own.shape
    count = conv.shape[0]
    total = len(projs)
    embed = projs[0].shape[1]
    feat_specs, short_specs = forward_specs(rows, width, count, [total - 1])
    shapes = [(rows, count), (rows, count), (2 * images, count)]
    packed = (3 * images, embed)
    return pl.pallas_call(
        functools.partial(last_forward_kernel, total, images),
        grid_spec=pltpu.PrefetchScalarGridSpec(
            num_scalar_prefetch=1,
            grid=(1,),
            in_specs=feat_specs
            + short_specs
            + [whole_spec(a.shape) for a in (conv, partner, *pooled, *projs)],
            out_specs=[whole_spec(s) for s in shapes] + [whole_spec(packed)] * 2,
        ),
        out_shape=[jax.ShapeDtypeStruct(s, BF) for s in shapes] + [jax.ShapeDtypeStruct(packed, F32)] * 2,
        compiler_params=params(),
        cost_estimate=pl.CostEstimate(
            flops=4 * rows * width * count, bytes_accessed=8 * rows * count, transcendentals=0
        ),
        name="forward_last",
    )(cols, f_own, f_sib, s_own, s_sib, conv, partner, *pooled, *projs)


def group_terms(z, partner, groups):
    count = z.shape[0]
    z = z - jnp.mean(z, axis=0, keepdims=True)
    squares = jnp.sum(z * z, axis=1, keepdims=True)
    spread = 2.0 * jnp.mean(squares)
    inner = lax.dot_general(z, z, NT, precision=lax.Precision.HIGHEST, preferred_element_type=F32)
    row = lax.broadcasted_iota(jnp.int32, (count, count), 0)
    col = lax.broadcasted_iota(jnp.int32, (count, count), 1)
    across = jnp.sum(jnp.where(row == col, squares, 0.0), axis=0, keepdims=True)
    kernel = jnp.exp(-(squares + across - 2.0 * inner) / (2.0 * spread))
    r_col = jnp.mean(kernel, axis=1, keepdims=True)
    r_row = jnp.mean(kernel, axis=0, keepdims=True)
    t = jnp.mean(r_col)
    centered = kernel - r_col - r_row + t
    scale_sq = float(count - 1) ** 2
    root = jnp.sqrt(jnp.sum(centered * centered, keepdims=True) / scale_sq + EPSILON)
    onehot = jnp.where(partner == col.astype(F32), 1.0, 0.0)
    positive = jnp.sum(kernel * onehot, keepdims=True) / count
    loss = -(positive - t) + GAMMA * root
    coeff = (-onehot / count + 1.0 / (count * count) + GAMMA * centered / (scale_sq * root)) / groups
    weighted = coeff * kernel
    moved = lax.dot_general(
        weighted, z, (((1,), (0,)), ((), ())), precision=lax.Precision.HIGHEST, preferred_element_type=F32
    )
    return loss, -(2.0 / spread) * (jnp.sum(weighted, axis=1, keepdims=True) * z - moved)


def hsic_kernel(slabs, images, groups, place_ref, *refs):
    chunks = refs[:-4]
    ge_ref, loss_ref, z_ref, p_ref = refs[-4:]
    place = place_ref[0]
    count = slabs * images
    half = z_ref.shape[1] // 2
    for g in (0, 1):
        for j in range(slabs):
            if len(chunks) == 1:
                block = chunks[0].at[j]
            else:
                block = chunks[j]
            at = pl.ds(pl.multiple_of((place ^ j) * images, images), images)
            z_ref[at] = block[g * images : (g + 1) * images]
            p_ref[at] = block[2 * images :, g * half : g * half + 128]
        partner = jnp.max(p_ref[...], axis=1, keepdims=True)
        loss, grad = group_terms(z_ref[...], partner, groups)
        if g == 0:
            loss_ref[...] = loss
        z_ref[...] = grad
        for j in range(slabs):
            at = pl.ds(pl.multiple_of((place ^ j) * images, images), images)
            ge_ref[j, g * images : (g + 1) * images] = z_ref[at]


def hsic(place, chunks, slabs, images, groups):
    embed = chunks[0].shape[-1]
    return pl.pallas_call(
        functools.partial(hsic_kernel, slabs, images, groups),
        in_specs=[pl.BlockSpec(memory_space=pltpu.SMEM)] + [vspec()] * len(chunks),
        out_specs=[vspec()] * 2,
        out_shape=[
            jax.ShapeDtypeStruct((slabs, 2 * images, embed), F32),
            jax.ShapeDtypeStruct((1, 1), F32),
        ],
        scratch_shapes=[pltpu.VMEM((slabs * images, embed), F32), pltpu.VMEM((slabs * images, 128), F32)],
        compiler_params=params(),
        name="hsic_groups",
    )(place, *chunks)


def backward_kernel(blocks, images, packed, f_own, f_sib, ge_ref, *refs):
    ins, outs = refs[: 4 * blocks], refs[4 * blocks :]
    spread = image_of_row((f_own.shape[0], images), 0, 1)
    mine = ge_ref[0].astype(BF)
    for j in range(blocks):
        m_own, m_sib, pooled, proj = ins[4 * j : 4 * j + 4]
        out = outs[j]
        count, width = proj.shape[0], f_own.shape[1]
        grad_pool = dot(mine, proj[...], NT) / POS
        total = jnp.zeros((count, width), F32)
        for mask, feat, part in (
            (m_own, f_own, grad_pool[:images]),
            (m_sib, f_sib, grad_pool[images:]),
        ):
            grad_hidden = dot(spread, part.astype(BF)).astype(BF) * mask[...]
            total = total + dot(grad_hidden, feat[...], TN)
        out[0:count] = total.astype(out.dtype)
        if packed:
            slabs = ge_ref.shape[0]
            flat = ge_ref[...].reshape(slabs * 2 * images, ge_ref.shape[2]).astype(BF)
            half = slabs * images
            out[count : count + half] = jnp.concatenate([flat[:half], flat[half:]], axis=1)
            extra = pooled[...]
            rest = jnp.zeros((2 * images, width - extra.shape[1]), BF)
            out[count + half :] = jnp.concatenate([extra, rest], axis=1)


def backward(f_own, f_sib, ge, blocks, images, packed):
    width = f_own.shape[1]
    rows = f_own.shape[0]
    count = blocks[0][3].shape[0]
    high = count + (ge.shape[0] + 2) * images if packed else count
    return pl.pallas_call(
        functools.partial(backward_kernel, len(blocks), images, packed),
        in_specs=[vspec()] * (3 + 4 * len(blocks)),
        out_specs=[vspec()] * len(blocks),
        out_shape=[jax.ShapeDtypeStruct((high, width), BF if packed else F32)] * len(blocks),
        compiler_params=params(),
        cost_estimate=pl.CostEstimate(
            flops=4 * len(blocks) * rows * width * count,
            bytes_accessed=4 * len(blocks) * rows * count,
            transcendentals=0,
        ),
        name="backward_blocks",
    )(f_own, f_sib, ge, *[a for block in blocks for a in block])


def proj_kernel(peers, slabs, images, count, own_ge, *refs):
    msgs, pooled, out = refs[: peers - 1], refs[peers - 1 : -1], refs[-1]
    embed = own_ge.shape[2]
    half = slabs * images
    parts = []
    for j in range(slabs):
        rows = [own_ge[j].astype(BF)]
        start, left = j * 2 * images, 0
        if start >= half:
            start, left = start - half, embed
        for msg in msgs:
            rows.append(msg[count + start : count + start + 2 * images, left : left + embed])
        slab = pooled[0][j] if len(pooled) == 1 else pooled[j][...]
        parts.append(dot(slab, jnp.concatenate(rows, axis=0), TN))
    while len(parts) > 1:
        parts = [parts[k] + parts[k + 1] for k in range(0, len(parts), 2)]
    out[...] = parts[0]


def proj_grad(own_ge, msgs, pooled, slabs, images, count):
    embed = own_ge.shape[2]
    return pl.pallas_call(
        functools.partial(proj_kernel, len(msgs) + 1, slabs, images, count),
        in_specs=[vspec()] * (1 + len(msgs) + len(pooled)),
        out_specs=vspec(),
        out_shape=jax.ShapeDtypeStruct((count, embed), F32),
        compiler_params=params(),
        name="proj_grad",
    )(own_ge, *msgs, *pooled)


def swap(x, axis, bit):
    size = lax.axis_size(axis)
    return lax.ppermute(x, axis, [(i, i ^ bit) for i in range(size)])


def gather_slabs(x, slabs):
    if slabs <= 4:
        return [x] + [swap(x, "dp", j) for j in range(1, slabs)]
    whole = lax.all_gather(x, "dp", axis=0, tiled=False)
    return [jnp.take(whole, lax.axis_index("dp") ^ jnp.arange(slabs), axis=0)]


def local(features, shortcut, conv_weight, proj_weight, partner):
    slabs, groups = lax.axis_size("dp"), lax.axis_size("fsdp")
    peers = groups // 2
    images = features.shape[0] // POS
    count, width = conv_weight.shape
    place = lax.axis_index("dp").astype(jnp.int32)
    index = lax.axis_index("fsdp").astype(jnp.int32)
    cols = index ^ (2 * jnp.arange(peers, dtype=jnp.int32))

    convs, projs = [conv_weight], [proj_weight]
    if peers == 4:
        conv_y, conv_x = swap(conv_weight, "fsdp", 4), swap(conv_weight, "fsdp", 2)
        proj_x, proj_y = swap(proj_weight, "fsdp", 2), swap(proj_weight, "fsdp", 4)
        convs += [conv_x, conv_y, swap(conv_y, "fsdp", 2)]
        projs += [proj_x, proj_y, swap(proj_x, "fsdp", 4)]
    else:
        convs += [swap(conv_weight, "fsdp", 2 * j) for j in range(1, peers)]
        projs += [swap(proj_weight, "fsdp", 2 * j) for j in range(1, peers)]
    f_sib = swap(features, "fsdp", 1)
    s_sib = swap(shortcut, "fsdp", 1)

    blocks = forward(cols, features, f_sib, shortcut, s_sib, convs[:-1], images)
    member = partner.astype(F32).reshape(images, 1)
    *last, mine, send = last_forward(
        cols, features, f_sib, shortcut, s_sib, convs[-1], member, [b[2] for b in blocks], projs, images
    )
    blocks = [(*b, p) for b, p in zip(blocks + [last], projs)]
    embeds = mine + swap(send, "fsdp", 1)
    ge, loss = hsic(place.reshape(1), gather_slabs(embeds, slabs), slabs, images, groups)

    (far,) = backward(features, f_sib, ge, blocks[-1:], images, True)
    msgs = [swap(far, "fsdp", 2 * (peers - 1))]
    near = backward(features, f_sib, ge, blocks[1:-1], images, True)
    msgs = [swap(m, "fsdp", 2 * j) for j, m in enumerate(near, 1)] + msgs
    (own,) = backward(features, f_sib, ge, blocks[:1], images, False)

    half = slabs * images
    pooled = jnp.concatenate([blocks[0][2]] + [m[count + half :, :count] for m in msgs], axis=0)
    total = own
    for m in msgs:
        total = total + m[:count].astype(F32)
    bit = 1
    while bit < slabs:
        total = total.astype(BF)
        total = total.astype(F32) + swap(total, "dp", bit).astype(F32)
        bit *= 2
    grad_proj = proj_grad(ge, msgs, gather_slabs(pooled, slabs), slabs, images, count)
    return total, grad_proj, loss.reshape(1)


def solution(mesh):
    return jax.shard_map(
        local,
        mesh=mesh,
        in_specs=(
            P(("dp", "fsdp"), None),
            P(("dp", "fsdp"), None),
            P("fsdp", None),
            P("fsdp", None),
            P(("dp", "fsdp")),
        ),
        out_specs=(P("fsdp", None), P("fsdp", None), P("fsdp")),
        check_vma=False,
    )
```

```python
import functools

import jax
import jax.numpy as jnp
from jax import lax
from jax.experimental import pallas as pl
from jax.experimental.pallas import tpu as pltpu
from jax.sharding import PartitionSpec as P

POS = 49
GAMMA = 3.0
EPSILON = 1e-06
BF = jnp.bfloat16
F32 = jnp.float32
NT = (((1,), (1,)), ((), ()))
TN = (((0,), (0,)), ((), ()))
VMEM_LIMIT = 8 * 1024 * 1024
SPLIT = 4


def dot(a, b, dims=(((1,), (0,)), ((), ()))):
    return lax.dot_general(a, b, dims, preferred_element_type=F32)


def vspec():
    return pl.BlockSpec(memory_space=pltpu.VMEM)


def params(more=0):
    return pltpu.CompilerParams(vmem_limit_bytes=VMEM_LIMIT + more)


def image_of_row(shape, row_dim, image_dim):
    row = lax.broadcasted_iota(jnp.int32, shape, row_dim)
    first = lax.broadcasted_iota(jnp.int32, shape, image_dim) * POS
    return jnp.where((row >= first) & (row < first + POS), 1.0, 0.0).astype(BF)


def forward_block(feat, short, conv, pick):
    hidden = jnp.maximum(dot(feat, conv, NT) + short.astype(F32), 0.0)
    mask = jnp.where(hidden > 0, 1.0, 0.0).astype(BF)
    pooled = dot(pick, hidden.astype(BF)) / POS
    return mask, pooled


def forward_blocks(picks, feats, shorts, convs, projs, embed, outs, ready=None):
    images = outs[2].shape[0] // 2
    pick_rows = image_of_row((images, feats[0].shape[0]), 1, 0)
    for j in range(picks):
        pooled = []
        for side in (0, 1):
            if ready is not None:
                ready(j, side)
            mask, mean = forward_block(feats[side][...], shorts[2 * j + side][...], convs[j][...], pick_rows)
            outs[3 * j + side][...] = mask
            pooled.append(mean)
        pooled = jnp.concatenate(pooled, axis=0).astype(BF)
        outs[3 * j + 2][...] = pooled
        embed = embed + dot(pooled, projs[j][...])
    return embed


def first_kernel(peers, images, index_ref, partner, f_sib, f_own, s_own, s_sib, conv, proj, *refs):
    blocks, embed_ref, feat, proj_out, member_ref = refs[:3], refs[3], refs[4], refs[5], refs[6]
    ahead, (short, conv_buf, sems) = refs[7 : 5 + 2 * peers], refs[5 + 2 * peers :]
    index = index_ref[0]
    count = conv_buf.shape[0]
    copies = []

    def fetch(source, target):
        copies.append(pltpu.make_async_copy(source, target, sems.at[len(copies)]))
        copies[-1].start()

    fetch(f_own, feat)
    fetch(conv, conv_buf)
    shorts = [short.at[0], short.at[1], *ahead]
    for k, target in enumerate(shorts):
        at = pl.ds(pl.multiple_of((index ^ (k // 2 * 2)) * count, count), count)
        fetch((s_own, s_sib)[k % 2].at[:, at], target)
        if k == 1:
            fetch(proj, proj_out)
    member = lax.broadcasted_iota(jnp.int32, member_ref.shape, 0)
    whole = jnp.zeros(member_ref.shape, F32)
    for i in range(images):
        whole = jnp.where(member == i, partner[i].astype(F32), whole)
    member_ref[...] = whole
    for copy in copies[:5]:
        copy.wait()
    embed = jnp.zeros(embed_ref.shape, F32)
    embed_ref[...] = forward_blocks(1, (feat, f_sib), shorts, [conv_buf], [proj_out], embed, blocks)
    for copy in copies[5:]:
        copy.wait()


def middle_kernel(blocks, f_own, f_sib, before, *refs):
    shorts, convs, projs = refs[: 2 * blocks], refs[2 * blocks : 3 * blocks], refs[3 * blocks : 4 * blocks]
    outs = refs[4 * blocks :]
    outs[-1][...] = forward_blocks(blocks, (f_own, f_sib), shorts, convs, projs, before[...], outs)


def last_kernel(images, f_own, f_sib, before, member, s_own, s_sib, conv, proj, *outs):
    embed = forward_blocks(1, (f_own, f_sib), (s_own, s_sib), [conv], [proj], before[...], outs)
    mine_ref, send_ref = outs[-2:]
    half = embed.shape[1] // 2
    whole = jnp.concatenate([member[...]] * (half // member.shape[1]), axis=1)
    none = jnp.zeros((images, half), F32)
    mine_ref[0 : 2 * images] = embed
    mine_ref[2 * images :] = jnp.concatenate([whole, none], axis=1)
    send_ref[0:images] = embed[images:]
    send_ref[images : 2 * images] = embed[:images]
    send_ref[2 * images :] = jnp.concatenate([none, whole], axis=1)


def forward_call(kernel, in_specs, shapes, scratch, busy, name, *arrays):
    rows, width, count = busy
    return pl.pallas_call(
        kernel,
        in_specs=in_specs,
        out_specs=[vspec()] * len(shapes),
        out_shape=[jax.ShapeDtypeStruct(shape, kind) for shape, kind in shapes],
        scratch_shapes=scratch,
        compiler_params=params(),
        cost_estimate=pl.CostEstimate(
            flops=16 * rows * width * count, bytes_accessed=8 * rows * count, transcendentals=0
        ),
        name=name,
    )(*arrays)


def block_shapes(rows, count, images):
    return [((rows, count), BF), ((rows, count), BF), ((2 * images, count), BF)]


def forward_first(index, partner, feats, shorts, conv, proj, peers, images):
    rows, width = feats[0].shape
    count, embed = proj.shape
    hbm = [pltpu.with_memory_space_constraint(a, pltpu.HBM) for a in (feats[0], shorts[0], conv, proj)]
    hbm.insert(2, shorts[1])
    shapes = block_shapes(rows, count, images)
    shapes += [((2 * images, embed), F32), ((rows, width), BF), ((count, embed), BF), ((images, 128), F32)]
    shapes += [((rows, count), BF)] * (2 * peers - 2)
    outs = forward_call(
        functools.partial(first_kernel, peers, images),
        [pl.BlockSpec(memory_space=pltpu.SMEM)] * 2 + [vspec()] + [pl.BlockSpec(memory_space=pl.ANY)] * 5,
        shapes,
        [
            pltpu.VMEM((2, rows, count), BF),
            pltpu.VMEM((count, width), BF),
            pltpu.SemaphoreType.DMA((3 + 2 * peers,)),
        ],
        (rows, width, count),
        "forward_first",
        *(index, pltpu.with_memory_space_constraint(partner, pltpu.HBM), feats[1], *hbm),
    )
    return outs[:3], outs[3], outs[4], outs[5], outs[6], outs[7:]


def forward_middle(feats, shorts, convs, projs, images, before):
    rows, width = feats[0].shape
    count, blocks = convs[0].shape[0], len(convs)
    arrays = (*feats, before, *shorts, *convs, *projs)
    outs = forward_call(
        functools.partial(middle_kernel, blocks),
        [vspec()] * len(arrays),
        block_shapes(rows, count, images) * blocks + [(before.shape, F32)],
        [],
        (rows, width, blocks * count),
        "forward_middle",
        *arrays,
    )
    return [outs[3 * j : 3 * j + 3] for j in range(blocks)], outs[-1]


def forward_last(feats, shorts, conv, proj, images, before, member):
    rows, width = feats[0].shape
    count, embed = proj.shape
    arrays = (*feats, before, member, *shorts, conv, proj)
    outs = forward_call(
        functools.partial(last_kernel, images),
        [vspec()] * len(arrays),
        block_shapes(rows, count, images) + [((3 * images, embed), F32)] * 2,
        [],
        (rows, width, count),
        "forward_last",
        *arrays,
    )
    return outs[:3], outs[3], outs[4]


def group_terms(z, partner, groups):
    count = z.shape[0]
    z = z - jnp.mean(z, axis=0, keepdims=True)
    squares = jnp.sum(z * z, axis=1, keepdims=True)
    spread = 2.0 * jnp.mean(squares)
    inner = lax.dot_general(z, z, NT, precision=lax.Precision.HIGHEST, preferred_element_type=F32)
    row = lax.broadcasted_iota(jnp.int32, (count, count), 0)
    col = lax.broadcasted_iota(jnp.int32, (count, count), 1)
    across = jnp.sum(jnp.where(row == col, squares, 0.0), axis=0, keepdims=True)
    kernel = jnp.exp(-(squares + across - 2.0 * inner) / (2.0 * spread))
    r_col = jnp.mean(kernel, axis=1, keepdims=True)
    r_row = jnp.mean(kernel, axis=0, keepdims=True)
    t = jnp.mean(r_col)
    centered = kernel - r_col - r_row + t
    scale_sq = float(count - 1) ** 2
    root = jnp.sqrt(jnp.sum(centered * centered, keepdims=True) / scale_sq + EPSILON)
    onehot = jnp.where(partner == col.astype(F32), 1.0, 0.0)
    positive = jnp.sum(kernel * onehot, keepdims=True) / count
    loss = -(positive - t) + GAMMA * root
    coeff = (-onehot / count + 1.0 / (count * count) + GAMMA * centered / (scale_sq * root)) / groups
    weighted = coeff * kernel
    moved = lax.dot_general(
        weighted, z, (((1,), (0,)), ((), ())), precision=lax.Precision.HIGHEST, preferred_element_type=F32
    )
    return loss, -(2.0 / spread) * (jnp.sum(weighted, axis=1, keepdims=True) * z - moved)


def hsic_kernel(slabs, images, groups, place_ref, *refs):
    chunks = refs[:-5]
    ge_ref, loss_ref, z_ref, p_ref, g_ref = refs[-5:]
    place = place_ref[0]
    half = z_ref.shape[2] // 2
    for j in range(slabs):
        block = chunks[0].at[j] if len(chunks) == 1 else chunks[j]
        at = pl.ds(pl.multiple_of((place ^ j) * images, images), images)
        for g in (0, 1):
            z_ref[g, at] = block[g * images : (g + 1) * images]
            p_ref[g, at] = block[2 * images :, g * half : g * half + 128]
    for g in (0, 1):
        partner = jnp.max(p_ref[g], axis=1, keepdims=True)
        loss, grad = group_terms(z_ref[g], partner, groups)
        if g == 0:
            loss_ref[...] = loss
        g_ref[g] = grad
    for j in range(slabs):
        at = pl.ds(pl.multiple_of((place ^ j) * images, images), images)
        for g in (0, 1):
            ge_ref[j, g * images : (g + 1) * images] = g_ref[g, at]


def hsic(place, chunks, slabs, images, groups):
    embed = chunks[0].shape[-1]
    return pl.pallas_call(
        functools.partial(hsic_kernel, slabs, images, groups),
        in_specs=[pl.BlockSpec(memory_space=pltpu.SMEM)] + [vspec()] * len(chunks),
        out_specs=[vspec()] * 2,
        out_shape=[
            jax.ShapeDtypeStruct((slabs, 2 * images, embed), F32),
            jax.ShapeDtypeStruct((1, 1), F32),
        ],
        scratch_shapes=[pltpu.VMEM((2, slabs * images, width), F32) for width in (embed, 128, embed)],
        compiler_params=params(80 * (slabs * images) ** 2),
        cost_estimate=pl.CostEstimate(flops=10**9, bytes_accessed=0, transcendentals=0),
        name="hsic_groups",
    )(place, *chunks)


def backward_kernel(blocks, images, part, extra, after, f_own, f_sib, ge_ref, *refs):
    ins, outs = refs[: 4 * blocks], refs[4 * blocks + after :]
    spread = image_of_row((f_own.shape[0], images), 0, 1)
    mine = ge_ref[0].astype(BF)
    start, rows = part
    width = f_own.shape[1]
    for j in range(blocks):
        m_own, m_sib, pooled, proj = ins[4 * j : 4 * j + 4]
        out = outs[j]
        grad_pool = dot(mine, proj[start : start + rows], NT) / POS
        total = jnp.zeros((rows, width), F32)
        for mask, feat, piece in (
            (m_own, f_own, grad_pool[:images]),
            (m_sib, f_sib, grad_pool[images:]),
        ):
            grad_hidden = dot(spread, piece.astype(BF)).astype(BF) * mask[:, start : start + rows]
            total = total + dot(grad_hidden, feat[...], TN)
        out[0:rows] = total.astype(out.dtype)
        if extra == "pooled":
            rest = jnp.zeros((2 * images, width - pooled.shape[1]), BF)
            out[rows:] = jnp.concatenate([pooled[...], rest], axis=1)
        if extra == "embed":
            slabs = ge_ref.shape[0]
            flat = ge_ref[...].reshape(slabs * 2 * images, ge_ref.shape[2]).astype(BF)
            half = slabs * images
            out[rows:] = jnp.concatenate([flat[:half], flat[half:]], axis=1)


def backward(feats, ge, blocks, images, part, extra=None, after=()):
    length, width = feats[0].shape
    rows = part[1]
    high = rows + {None: 0, "pooled": 2 * images, "embed": ge.shape[0] * images}[extra]
    return pl.pallas_call(
        functools.partial(backward_kernel, len(blocks), images, part, extra, len(after)),
        in_specs=[vspec()] * (3 + 4 * len(blocks)) + [pl.BlockSpec(memory_space=pl.ANY)] * len(after),
        out_specs=[vspec()] * len(blocks),
        out_shape=[jax.ShapeDtypeStruct((high, width), BF if extra else F32)] * len(blocks),
        compiler_params=params(),
        cost_estimate=pl.CostEstimate(
            flops=16 * len(blocks) * length * width * rows,
            bytes_accessed=4 * len(blocks) * length * rows,
            transcendentals=0,
        ),
        name="backward_blocks",
    )(*feats, ge, *[a for block in blocks for a in block], *after)


def small_call(kernel, shapes, name, *arrays, tokens=()):
    return pl.pallas_call(
        kernel,
        in_specs=[vspec()] * len(arrays) + [pl.BlockSpec(memory_space=pl.ANY)] * len(tokens),
        out_specs=[vspec()] * len(shapes),
        out_shape=[jax.ShapeDtypeStruct(shape, kind) for shape, kind in shapes],
        compiler_params=params(),
        cost_estimate=pl.CostEstimate(flops=0, bytes_accessed=0, transcendentals=0),
        name=name,
    )(*arrays, *tokens)


def sum_kernel(*refs):
    total = refs[0][...].astype(F32)
    for ref in refs[1:-1]:
        total = total + ref[...].astype(F32)
    refs[-1][...] = total.astype(refs[-1].dtype)


def sum_of(kind, *arrays):
    return small_call(sum_kernel, [(arrays[0].shape, kind)], "sum_arrays", *arrays)[0]


def collect_kernel(start, rows, count_msgs, own, pooled, *refs):
    msgs, out = refs[:count_msgs], refs[-1]
    total = own[start : start + rows]
    for msg in msgs:
        total = total + msg[0:rows].astype(F32)
    out[0:rows] = total.astype(BF)
    if out.shape[0] == rows:
        return
    high, count = pooled.shape
    slab = [pooled[...]] + [msg[rows : rows + high, 0:count] for msg in msgs]
    tall = (out.shape[0] - rows) // high
    for k, piece in enumerate(slab):
        at = rows + k % tall * high
        out[at : at + high, k // tall * count : (k // tall + 1) * count] = piece


def collect(own, pooled, msgs, part, with_pooled, token):
    start, rows = part
    width = own.shape[1]
    more = (len(msgs) + 1) * pooled.size // width if with_pooled else 0
    kernel = functools.partial(collect_kernel, start, rows, len(msgs))
    return small_call(kernel, [((rows + more, width), BF)], "collect_terms", own, pooled, *msgs, tokens=token)[0]


def merge_kernel(rows, mine, other, *refs):
    out = refs[-1]
    out[0:rows] = (mine[0:rows].astype(F32) + other[0:rows].astype(F32)).astype(BF)
    more = mine.shape[0] - rows
    if more:
        out[rows : rows + more] = mine[rows:]
        out[rows + more :] = other[rows:]


def merge(rows, mine, other, *token):
    high, width = mine.shape
    shape = (2 * high - rows, width)
    return small_call(functools.partial(merge_kernel, rows), [(shape, BF)], "merge_slabs", mine, other, tokens=token)[0]


def final_kernel(*refs):
    pieces, out = refs[:-1], refs[-1]
    tail = pieces[2].shape[0]
    head = out.shape[0] - tail
    out[0:head] = pieces[0][0:head].astype(F32) + pieces[1][0:head].astype(F32)
    out[head:] = pieces[2][...].astype(F32) + pieces[3][...].astype(F32)


def proj_kernel(slabs, images, rows, msg_rows, own_ge, mine, other, *refs):
    msgs, (out, token) = refs[:-2], refs[-2:]
    token[...] = jnp.zeros(token.shape, F32)
    count, embed = out.shape
    groups = mine.shape[1] // count
    half = slabs * images
    per = (mine.shape[0] - rows) // (slabs // 2)
    together = per // (2 * images)
    parts = []
    for j in range(slabs):
        pieces = [own_ge[j].astype(BF)]
        start, left = j * 2 * images, 0
        if start >= half:
            start, left = start - half, embed
        for msg in msgs:
            pieces.append(msg[msg_rows + start : msg_rows + start + 2 * images, left : left + embed])
        ref, at = (mine, j) if j < slabs // 2 else (other, j - slabs // 2)
        total = jnp.zeros((count, embed), F32)
        for g in range(groups):
            pooled = ref[rows + at * per : rows + (at + 1) * per, g * count : (g + 1) * count]
            grads = jnp.concatenate(pieces[g * together : (g + 1) * together], axis=0)
            total = total + dot(pooled, grads, TN)
        parts.append(total)
    while len(parts) > 1:
        parts = [parts[k] + parts[k + 1] for k in range(0, len(parts), 2)]
    out[...] = parts[0]


def gate_kernel(x, token, out):
    out[...] = x[...]


def after(x, token):
    return small_call(gate_kernel, [(x.shape, x.dtype)], "gate", x, tokens=(token,))[0]


def pack_kernel(start, conv, proj, token, out):
    half = conv.shape[0] // 2
    fold = conv.shape[1] // proj.shape[1]
    out[0:half] = conv[start : start + half]
    rows = half // fold
    for k in range(fold):
        piece = proj[start + k * rows : start + (k + 1) * rows]
        out[half:, k * proj.shape[1] : (k + 1) * proj.shape[1]] = piece


def pack_half(start, conv, proj, token):
    half, fold = conv.shape[0] // 2, conv.shape[1] // proj.shape[1]
    shape = (half + half // fold, conv.shape[1])
    return small_call(functools.partial(pack_kernel, start), [(shape, BF)], "pack_half", conv, proj, tokens=(token,))[0]


def unpack_kernel(*refs):
    conv, proj = refs[-2:]
    half = conv.shape[0] // 2
    fold = conv.shape[1] // proj.shape[1]
    rows = half // fold
    for k, ref in enumerate(refs[:-2]):
        conv[k * half : (k + 1) * half] = ref[0:half]
        for j in range(fold):
            at = k * half + j * rows
            proj[at : at + rows] = ref[half:, j * proj.shape[1] : (j + 1) * proj.shape[1]]


def swap(x, axis, bit):
    size = lax.axis_size(axis)
    return lax.ppermute(x, axis, [(i, i ^ bit) for i in range(size)])


def gather_slabs(x, slabs):
    if slabs <= 4:
        return [x] + [swap(x, "dp", j) for j in range(1, slabs)]
    whole = lax.all_gather(x, "dp", axis=0, tiled=False)
    return [jnp.take(whole, lax.axis_index("dp") ^ jnp.arange(slabs), axis=0)]


def local(features, shortcut, conv_weight, proj_weight, partner):
    slabs, groups = lax.axis_size("dp"), lax.axis_size("fsdp")
    peers = groups // 2
    images = features.shape[0] // POS
    count, width = conv_weight.shape
    place = lax.axis_index("dp").astype(jnp.int32).reshape(1)
    index = lax.axis_index("fsdp").astype(jnp.int32).reshape(1)

    f_sib = swap(features, "fsdp", 1)
    s_sib = swap(shortcut, "fsdp", 1)
    first, embed, f_own, proj_own, member, ahead = forward_first(
        index, partner, (features, f_sib), (shortcut, s_sib), conv_weight, proj_weight, peers, images
    )
    feats = (f_own, f_sib)
    if peers == 4:
        conv_y = swap(conv_weight, "fsdp", 4)
        proj_x = swap(proj_weight, "fsdp", 2)
        conv_x = swap(conv_weight, "fsdp", 2)
        proj_y = swap(proj_weight, "fsdp", 4)
        halves = [
            swap(pack_half(0, conv_y, proj_y, embed), "fsdp", 2),
            swap(pack_half(count // 2, conv_x, proj_x, embed), "fsdp", 4),
        ]
        conv_far, proj_far = small_call(
            unpack_kernel, [(conv_weight.shape, BF), (proj_weight.shape, BF)], "unpack_halves", *halves
        )
        convs, projs = [conv_x, conv_y, conv_far], [proj_x, proj_y, proj_far]
    else:
        convs = [swap(conv_weight, "fsdp", 2 * j) for j in range(1, peers)]
        projs = [swap(proj_weight, "fsdp", 2 * j) for j in range(1, peers)]
    middle, embed = forward_middle(feats, ahead[:-2], convs[:-1], projs[:-1], images, embed)
    last, mine, send = forward_last(feats, ahead[-2:], convs[-1], projs[-1], images, embed, member)
    blocks, projs = [first, *middle, last], [proj_own, *projs]
    blocks = [(*b, p) for b, p in zip(blocks, projs)]
    embeds = sum_of(F32, mine, swap(send, "fsdp", 1))
    ge, loss = hsic(place, gather_slabs(embeds, slabs), slabs, images, groups)

    first_rows = count * SPLIT // 8
    parts = [(0, first_rows), (first_rows, count - first_rows)]
    terms, done = [], ()
    for part, extra in zip(parts, ("pooled", "embed")):
        far = backward(feats, ge, blocks[-1:], images, part, extra, done)
        near = backward(feats, ge, blocks[1:-1], images, part, extra, tuple(far))
        done = tuple(near)
        terms.append([*near, *far])
    (own,) = backward(feats, ge, blocks[:1], images, (0, count), None, done)

    pieces, token = [], ()
    for k, part in enumerate(parts):
        if k:
            terms[k] = [after(m, total) for m in terms[k]]
        msgs = [swap(m, "fsdp", 2 * j) for j, m in enumerate(terms[k], 1)]
        total = collect(own, blocks[0][2], msgs, part, k == 0, pieces[:1])
        if k:
            grad_proj, token = small_call(
                functools.partial(proj_kernel, slabs, images, parts[0][1], part[1]),
                [(proj_weight.shape, F32), ((8, 128), F32)],
                "proj_grad",
                *(ge, *pieces, *msgs),
            )
            token = (token,)
        piece, bit = total, 1
        while 2 * bit < slabs:
            piece = merge(part[1], piece, swap(piece, "dp", bit), *token)
            bit *= 2
        pieces += [piece, swap(piece, "dp", bit)]
    (grad_conv,) = small_call(
        final_kernel, [((count, width), F32)], "sum_slabs", *pieces
    )
    return grad_conv, grad_proj, loss.reshape(1)


def solution(mesh):
    return jax.shard_map(
        local,
        mesh=mesh,
        in_specs=(
            P(("dp", "fsdp"), None),
            P(("dp", "fsdp"), None),
            P("fsdp", None),
            P("fsdp", None),
            P(("dp", "fsdp")),
        ),
        out_specs=(P("fsdp", None), P("fsdp", None), P("fsdp")),
        check_vma=False,
    )
```

```python
import functools

import jax
import jax.numpy as jnp
from jax import lax
from jax.experimental import pallas as pl
from jax.experimental.pallas import tpu as pltpu
from jax.sharding import PartitionSpec as P

POS = 49
GAMMA = 3.0
EPSILON = 1e-06
BF = jnp.bfloat16
F32 = jnp.float32
NT = (((1,), (1,)), ((), ()))
TN = (((0,), (0,)), ((), ()))
VMEM_LIMIT = 8 * 1024 * 1024
SPLIT = 4
ORDER = (0, 3, 1, 2)


def dot(a, b, dims=(((1,), (0,)), ((), ()))):
    return lax.dot_general(a, b, dims, preferred_element_type=F32)


def vspec():
    return pl.BlockSpec(memory_space=pltpu.VMEM)


def params(more=0):
    return pltpu.CompilerParams(vmem_limit_bytes=VMEM_LIMIT + more)


def image_of_row(shape, row_dim, image_dim):
    row = lax.broadcasted_iota(jnp.int32, shape, row_dim)
    first = lax.broadcasted_iota(jnp.int32, shape, image_dim) * POS
    return jnp.where((row >= first) & (row < first + POS), 1.0, 0.0).astype(BF)


def forward_block(feat, short, convs, pick):
    preact = [dot(feat, conv[...], NT) for conv in convs]
    preact = preact[0] if len(preact) == 1 else jnp.concatenate(preact, axis=1)
    hidden = jnp.maximum(preact + short.astype(F32), 0.0)
    mask = jnp.where(hidden > 0, 1.0, 0.0).astype(BF)
    pooled = dot(pick, hidden.astype(BF)) / POS
    return mask, pooled


def forward_blocks(picks, feats, shorts, convs, projs, embed, outs, ready=None):
    images = outs[2].shape[0] // 2
    pick_rows = image_of_row((images, feats[0].shape[0]), 1, 0)
    for j in range(picks):
        pooled = [None, None]
        for side in (1, 0):
            if ready is not None:
                ready(j, side)
            mask, pooled[side] = forward_block(feats[side][...], shorts[2 * j + side][...], convs[j], pick_rows)
            outs[3 * j + side][...] = mask
        pooled = jnp.concatenate(pooled, axis=0).astype(BF)
        outs[3 * j + 2][...] = pooled
        embed = embed + dot(pooled, projs[j][...])
    return embed


def fetcher(sems):
    copies = []

    def fetch(source, target):
        copies.append(pltpu.make_async_copy(source, target, sems.at[len(copies)]))
        copies[-1].start()
        return copies[-1]

    return fetch


def columns(index_ref, pick, count):
    return pl.ds(pl.multiple_of((index_ref[0] ^ (2 * pick)) * count, count), count)


def first_kernel(images, index_ref, f_sib, partner_ref, f_own, s_own, s_sib, conv, proj, *refs):
    blocks, embed_ref, feat, proj_out, member_ref = refs[:3], refs[3], refs[4], refs[5], refs[6]
    short, conv_buf, partner, sems = refs[7:]
    fetch = fetcher(sems)
    at = columns(index_ref, 0, conv_buf.shape[0])
    shorts = [short.at[0], short.at[1]]
    waits = [
        [fetch(conv, conv_buf), fetch(s_sib.at[:, at], shorts[1])],
        [fetch(f_own, feat), fetch(s_own.at[:, at], shorts[0]), fetch(proj, proj_out)],
    ]
    partner_copy = fetch(partner_ref, partner)

    def ready(j, side):
        for copy in waits[1 - side]:
            copy.wait()

    embed = jnp.zeros(embed_ref.shape, F32)
    embed_ref[...] = forward_blocks(1, (feat, f_sib), shorts, [[conv_buf]], [proj_out], embed, blocks, ready)
    partner_copy.wait()
    member = lax.broadcasted_iota(jnp.int32, member_ref.shape, 0)
    whole = jnp.zeros(member_ref.shape, F32)
    for i in range(images):
        whole = jnp.where(member == i, partner[i].astype(F32), whole)
    member_ref[...] = whole


def middle_kernel(blocks, index_ref, f_own, f_sib, before, s_own, s_sib, *refs):
    convs, projs, refs = refs[:blocks], refs[blocks : 2 * blocks], refs[2 * blocks :]
    *outs, embed_ref, ahead_own, ahead_sib, short, sems = refs
    fetch = fetcher(sems)
    targets = [short.at[k] for k in range(2 * blocks)] + [ahead_own, ahead_sib]
    copies = [None] * len(targets)
    for j in range(blocks + 1):
        at = columns(index_ref, j + 1, short.shape[2])
        for side in (1, 0):
            copies[2 * j + side] = fetch((s_own, s_sib)[side].at[:, at], targets[2 * j + side])

    def ready(j, side):
        copies[2 * j + side].wait()

    feats, weights = (f_own, f_sib), [[c] for c in convs]
    embed_ref[...] = forward_blocks(blocks, feats, targets, weights, projs, before[...], outs, ready)
    ready(blocks, 1)
    ready(blocks, 0)


def last_kernel(images, f_own, f_sib, before, member, s_own, s_sib, proj, *refs):
    convs, outs = refs[:-5], refs[-5:]
    embed = forward_blocks(1, (f_own, f_sib), (s_own, s_sib), [convs], [proj], before[...], outs)
    mine_ref, send_ref = outs[-2:]
    half = embed.shape[1] // 2
    whole = jnp.concatenate([member[...]] * (half // member.shape[1]), axis=1)
    none = jnp.zeros((images, half), F32)
    mine_ref[0 : 2 * images] = embed
    mine_ref[2 * images :] = jnp.concatenate([whole, none], axis=1)
    send_ref[0:images] = embed[images:]
    send_ref[images : 2 * images] = embed[:images]
    send_ref[2 * images :] = jnp.concatenate([none, whole], axis=1)


def forward_call(kernel, in_specs, shapes, scratch, busy, name, *arrays):
    rows, width, count = busy
    return pl.pallas_call(
        kernel,
        in_specs=in_specs,
        out_specs=[vspec()] * len(shapes),
        out_shape=[jax.ShapeDtypeStruct(shape, kind) for shape, kind in shapes],
        scratch_shapes=scratch,
        compiler_params=params(),
        cost_estimate=pl.CostEstimate(
            flops=16 * rows * width * count, bytes_accessed=8 * rows * count, transcendentals=0
        ),
        name=name,
    )(*arrays)


def block_shapes(rows, count, images):
    return [((rows, count), BF), ((rows, count), BF), ((2 * images, count), BF)]


def from_hbm(x):
    return pltpu.with_memory_space_constraint(x, pltpu.HBM)


def forward_first(index, partner, feats, shorts, conv, proj, images):
    rows, width = feats[0].shape
    count, embed = proj.shape
    shapes = block_shapes(rows, count, images)
    shapes += [((2 * images, embed), F32), ((rows, width), BF), ((count, embed), BF), ((images, 128), F32)]
    outs = forward_call(
        functools.partial(first_kernel, images),
        [pl.BlockSpec(memory_space=pltpu.SMEM)] + [vspec()] + [pl.BlockSpec(memory_space=pl.ANY)] * 6,
        shapes,
        [
            pltpu.VMEM((2, rows, count), BF),
            pltpu.VMEM((count, width), BF),
            pltpu.SMEM((images,), jnp.int32),
            pltpu.SemaphoreType.DMA((6,)),
        ],
        (rows, width, count),
        "forward_first",
        *(index, feats[1], from_hbm(partner), from_hbm(feats[0]), from_hbm(shorts[0]), from_hbm(shorts[1])),
        *(from_hbm(conv), from_hbm(proj)),
    )
    return outs[:3], outs[3], outs[4], outs[5], outs[6]


def forward_middle(index, feats, shorts, convs, projs, images, before):
    rows, width = feats[0].shape
    count, blocks = convs[0].shape[0], len(convs)
    outs = forward_call(
        functools.partial(middle_kernel, blocks),
        [pl.BlockSpec(memory_space=pltpu.SMEM)]
        + [vspec()] * 3
        + [pl.BlockSpec(memory_space=pl.ANY)] * 2
        + [vspec()] * (2 * blocks),
        block_shapes(rows, count, images) * blocks + [(before.shape, F32)] + [((rows, count), BF)] * 2,
        [pltpu.VMEM((2 * blocks, rows, count), BF), pltpu.SemaphoreType.DMA((2 * blocks + 2,))],
        (rows, width, blocks * count),
        "forward_middle",
        *(index, *feats, before, from_hbm(shorts[0]), from_hbm(shorts[1]), *convs, *projs),
    )
    return [outs[3 * j : 3 * j + 3] for j in range(blocks)], outs[-3], outs[-2:]


def forward_last(feats, shorts, convs, proj, images, before, member):
    rows, width = feats[0].shape
    count, embed = proj.shape
    arrays = (*feats, before, member, *shorts, proj, *convs)
    outs = forward_call(
        functools.partial(last_kernel, images),
        [vspec()] * len(arrays),
        block_shapes(rows, count, images) + [((3 * images, embed), F32)] * 2,
        [],
        (rows, width, count),
        "forward_last",
        *arrays,
    )
    return outs[:3], outs[3], outs[4]


def group_terms(z, partner, groups):
    count = z.shape[0]
    z = z - jnp.mean(z, axis=0, keepdims=True)
    squares = jnp.sum(z * z, axis=1, keepdims=True)
    spread = 2.0 * jnp.mean(squares)
    inner = lax.dot_general(z, z, NT, precision=lax.Precision.HIGHEST, preferred_element_type=F32)
    row = lax.broadcasted_iota(jnp.int32, (count, count), 0)
    col = lax.broadcasted_iota(jnp.int32, (count, count), 1)
    across = jnp.sum(jnp.where(row == col, squares, 0.0), axis=0, keepdims=True)
    kernel = jnp.exp(-(squares + across - 2.0 * inner) / (2.0 * spread))
    r_col = jnp.mean(kernel, axis=1, keepdims=True)
    r_row = jnp.mean(kernel, axis=0, keepdims=True)
    t = jnp.mean(r_col)
    centered = kernel - r_col - r_row + t
    scale_sq = float(count - 1) ** 2
    root = jnp.sqrt(jnp.sum(centered * centered, keepdims=True) / scale_sq + EPSILON)
    onehot = jnp.where(partner == col.astype(F32), 1.0, 0.0)
    positive = jnp.sum(kernel * onehot, keepdims=True) / count
    loss = -(positive - t) + GAMMA * root
    coeff = (-onehot / count + 1.0 / (count * count) + GAMMA * centered / (scale_sq * root)) / groups
    weighted = coeff * kernel
    moved = lax.dot_general(
        weighted, z, (((1,), (0,)), ((), ())), precision=lax.Precision.HIGHEST, preferred_element_type=F32
    )
    return loss, -(2.0 / spread) * (jnp.sum(weighted, axis=1, keepdims=True) * z - moved)


def hsic_kernel(slabs, images, groups, place_ref, *refs):
    chunks = refs[:-5]
    ge_ref, loss_ref, z_ref, p_ref, g_ref = refs[-5:]
    place = place_ref[0]
    half = z_ref.shape[2] // 2
    for j in range(slabs):
        block = chunks[0].at[j] if len(chunks) == 1 else chunks[ORDER.index(j)]
        at = pl.ds(pl.multiple_of((place ^ j) * images, images), images)
        for g in (0, 1):
            z_ref[g, at] = block[g * images : (g + 1) * images]
            p_ref[g, at] = block[2 * images :, g * half : g * half + 128]
    for g in (0, 1):
        partner = jnp.max(p_ref[g], axis=1, keepdims=True)
        loss, grad = group_terms(z_ref[g], partner, groups)
        if g == 0:
            loss_ref[...] = loss
        g_ref[g] = grad
    for j in range(slabs):
        at = pl.ds(pl.multiple_of((place ^ j) * images, images), images)
        for g in (0, 1):
            ge_ref[j, g * images : (g + 1) * images] = g_ref[g, at]


def hsic(place, chunks, slabs, images, groups):
    embed = chunks[0].shape[-1]
    return pl.pallas_call(
        functools.partial(hsic_kernel, slabs, images, groups),
        in_specs=[pl.BlockSpec(memory_space=pltpu.SMEM)] + [vspec()] * len(chunks),
        out_specs=[vspec()] * 2,
        out_shape=[
            jax.ShapeDtypeStruct((slabs, 2 * images, embed), F32),
            jax.ShapeDtypeStruct((1, 1), F32),
        ],
        scratch_shapes=[pltpu.VMEM((2, slabs * images, width), F32) for width in (embed, 128, embed)],
        compiler_params=params(80 * (slabs * images) ** 2),
        cost_estimate=pl.CostEstimate(flops=10**9, bytes_accessed=0, transcendentals=0),
        name="hsic_groups",
    )(place, *([chunks[j] for j in ORDER] if len(chunks) > 1 else chunks))


def backward_kernel(blocks, images, part, extra, after, f_own, f_sib, ge_ref, *refs):
    ins, outs = refs[: 4 * blocks], refs[4 * blocks + after :]
    spread = image_of_row((f_own.shape[0], images), 0, 1)
    mine = ge_ref[0].astype(BF)
    start, rows = part
    width = f_own.shape[1]
    for j in range(blocks):
        m_own, m_sib, pooled, proj = ins[4 * j : 4 * j + 4]
        out = outs[j]
        grad_pool = dot(mine, proj[start : start + rows], NT) / POS
        total = jnp.zeros((rows, width), F32)
        for mask, feat, piece in (
            (m_own, f_own, grad_pool[:images]),
            (m_sib, f_sib, grad_pool[images:]),
        ):
            grad_hidden = dot(spread, piece.astype(BF)).astype(BF) * mask[:, start : start + rows]
            total = total + dot(grad_hidden, feat[...], TN)
        out[0:rows] = total.astype(out.dtype)
        if extra == "pooled":
            rest = jnp.zeros((2 * images, width - pooled.shape[1]), BF)
            out[rows:] = jnp.concatenate([pooled[...], rest], axis=1)
        if extra == "embed":
            slabs = ge_ref.shape[0]
            flat = ge_ref[...].reshape(slabs * 2 * images, ge_ref.shape[2]).astype(BF)
            half = slabs * images
            out[rows:] = jnp.concatenate([flat[:half], flat[half:]], axis=1)


def backward(feats, ge, blocks, images, part, extra=None, after=()):
    length, width = feats[0].shape
    rows = part[1]
    high = rows + {None: 0, "pooled": 2 * images, "embed": ge.shape[0] * images}[extra]
    return pl.pallas_call(
        functools.partial(backward_kernel, len(blocks), images, part, extra, len(after)),
        in_specs=[vspec()] * (3 + 4 * len(blocks)) + [pl.BlockSpec(memory_space=pl.ANY)] * len(after),
        out_specs=[vspec()] * len(blocks),
        out_shape=[jax.ShapeDtypeStruct((high, width), BF if extra else F32)] * len(blocks),
        compiler_params=params(),
        cost_estimate=pl.CostEstimate(
            flops=16 * len(blocks) * length * width * rows,
            bytes_accessed=4 * len(blocks) * length * rows,
            transcendentals=0,
        ),
        name="backward_blocks",
    )(*feats, ge, *[a for block in blocks for a in block], *after)


def small_call(kernel, shapes, name, *arrays, tokens=()):
    return pl.pallas_call(
        kernel,
        in_specs=[vspec()] * len(arrays) + [pl.BlockSpec(memory_space=pl.ANY)] * len(tokens),
        out_specs=[vspec()] * len(shapes),
        out_shape=[jax.ShapeDtypeStruct(shape, kind) for shape, kind in shapes],
        compiler_params=params(),
        cost_estimate=pl.CostEstimate(flops=0, bytes_accessed=0, transcendentals=0),
        name=name,
    )(*arrays, *tokens)


def sum_kernel(*refs):
    total = refs[0][...].astype(F32)
    for ref in refs[1:-1]:
        total = total + ref[...].astype(F32)
    refs[-1][...] = total.astype(refs[-1].dtype)


def sum_of(kind, *arrays):
    return small_call(sum_kernel, [(arrays[0].shape, kind)], "sum_arrays", *arrays)[0]


def collect_kernel(start, rows, count_msgs, own, pooled, *refs):
    msgs, out = refs[:count_msgs], refs[-1]
    total = own[start : start + rows]
    for msg in msgs:
        total = total + msg[0:rows].astype(F32)
    out[0:rows] = total.astype(BF)
    if out.shape[0] == rows:
        return
    high, count = pooled.shape
    slab = [pooled[...]] + [msg[rows : rows + high, 0:count] for msg in msgs]
    tall = (out.shape[0] - rows) // high
    for k, piece in enumerate(slab):
        at = rows + k % tall * high
        out[at : at + high, k // tall * count : (k // tall + 1) * count] = piece


def collect(own, pooled, msgs, part, with_pooled, token):
    start, rows = part
    width = own.shape[1]
    more = (len(msgs) + 1) * pooled.size // width if with_pooled else 0
    kernel = functools.partial(collect_kernel, start, rows, len(msgs))
    return small_call(kernel, [((rows + more, width), BF)], "collect_terms", own, pooled, *msgs, tokens=token)[0]


def merge_kernel(rows, mine, other, *refs):
    out = refs[-1]
    out[0:rows] = (mine[0:rows].astype(F32) + other[0:rows].astype(F32)).astype(BF)
    more = mine.shape[0] - rows
    if more:
        out[rows : rows + more] = mine[rows:]
        out[rows + more :] = other[rows:]


def merge(rows, mine, other, *token):
    high, width = mine.shape
    shape = (2 * high - rows, width)
    return small_call(functools.partial(merge_kernel, rows), [(shape, BF)], "merge_slabs", mine, other, tokens=token)[0]


def final_kernel(*refs):
    pieces, out = refs[:-1], refs[-1]
    tail = pieces[2].shape[0]
    head = out.shape[0] - tail
    out[0:head] = pieces[0][0:head].astype(F32) + pieces[1][0:head].astype(F32)
    out[head:] = pieces[2][...].astype(F32) + pieces[3][...].astype(F32)


def proj_kernel(slabs, images, rows, msg_rows, own_ge, mine, other, *refs):
    msgs, (out, token) = refs[:-2], refs[-2:]
    token[...] = jnp.zeros(token.shape, F32)
    count, embed = out.shape
    groups = mine.shape[1] // count
    half = slabs * images
    per = (mine.shape[0] - rows) // (slabs // 2)
    together = per // (2 * images)
    parts = []
    for j in range(slabs):
        pieces = [own_ge[j].astype(BF)]
        start, left = j * 2 * images, 0
        if start >= half:
            start, left = start - half, embed
        for msg in msgs:
            pieces.append(msg[msg_rows + start : msg_rows + start + 2 * images, left : left + embed])
        ref, at = (mine, j) if j < slabs // 2 else (other, j - slabs // 2)
        total = jnp.zeros((count, embed), F32)
        for g in range(groups):
            pooled = ref[rows + at * per : rows + (at + 1) * per, g * count : (g + 1) * count]
            grads = jnp.concatenate(pieces[g * together : (g + 1) * together], axis=0)
            total = total + dot(pooled, grads, TN)
        parts.append(total)
    while len(parts) > 1:
        parts = [parts[k] + parts[k + 1] for k in range(0, len(parts), 2)]
    out[...] = parts[0]


def gate_kernel(x, token, out):
    out[...] = x[...]


def after(x, token):
    return small_call(gate_kernel, [(x.shape, x.dtype)], "gate", x, tokens=(token,))[0]


def part_kernel(start, x, token, out):
    out[...] = x[start : start + out.shape[0]]


def half_of(start, x, token):
    shape = (x.shape[0] // 2, x.shape[1])
    return small_call(functools.partial(part_kernel, start), [(shape, x.dtype)], "half_of", x, tokens=(token,))[0]


def swap(x, axis, bit):
    size = lax.axis_size(axis)
    return lax.ppermute(x, axis, [(i, i ^ bit) for i in range(size)])


def gather_slabs(x, slabs):
    if slabs <= 4:
        return [x] + [swap(x, "dp", j) for j in range(1, slabs)]
    whole = lax.all_gather(x, "dp", axis=0, tiled=False)
    return [jnp.take(whole, lax.axis_index("dp") ^ jnp.arange(slabs), axis=0)]


def local(features, shortcut, conv_weight, proj_weight, partner):
    slabs, groups = lax.axis_size("dp"), lax.axis_size("fsdp")
    peers = groups // 2
    images = features.shape[0] // POS
    count, width = conv_weight.shape
    place = lax.axis_index("dp").astype(jnp.int32).reshape(1)
    index = lax.axis_index("fsdp").astype(jnp.int32).reshape(1)

    f_sib = swap(features, "fsdp", 1)
    s_sib = swap(shortcut, "fsdp", 1)
    shorts = (shortcut, s_sib)
    first, embed, f_own, proj_own, member = forward_first(
        index, partner, (features, f_sib), shorts, conv_weight, proj_weight, images
    )
    feats = (f_own, f_sib)
    projs = [swap(proj_weight, "fsdp", 2 * j) for j in range(1, peers)]
    if peers == 4:
        conv_y = swap(conv_weight, "fsdp", 4)
        conv_x = swap(conv_weight, "fsdp", 2)
        halves = [
            swap(half_of(0, conv_y, embed), "fsdp", 2),
            swap(half_of(count // 2, conv_x, embed), "fsdp", 4),
        ]
        convs = [conv_x, conv_y, halves]
    else:
        convs = [swap(conv_weight, "fsdp", 2 * j) for j in range(1, peers)]
        convs[-1] = [convs[-1]]
    middle, embed, ahead = forward_middle(index, feats, shorts, convs[:-1], projs[:-1], images, embed)
    last, mine, send = forward_last(feats, ahead, convs[-1], projs[-1], images, embed, member)
    blocks, projs = [first, *middle, last], [proj_own, *projs]
    blocks = [(*b, p) for b, p in zip(blocks, projs)]
    embeds = sum_of(F32, mine, swap(send, "fsdp", 1))
    ge, loss = hsic(place, gather_slabs(embeds, slabs), slabs, images, groups)

    first_rows = count * SPLIT // 8
    parts = [(0, first_rows), (first_rows, count - first_rows)]
    terms, done = [], ()
    for part, extra in zip(parts, ("pooled", "embed")):
        far = backward(feats, ge, blocks[-1:], images, part, extra, done)
        near = backward(feats, ge, blocks[1:-1], images, part, extra, tuple(far))
        done = tuple(near)
        terms.append([*near, *far])
    (own,) = backward(feats, ge, blocks[:1], images, (0, count), None, done)

    pieces, token = [], ()
    for k, part in enumerate(parts):
        if k:
            terms[k] = [after(m, total) for m in terms[k]]
        msgs = [swap(m, "fsdp", 2 * j) for j, m in enumerate(terms[k], 1)]
        total = collect(own, blocks[0][2], msgs, part, k == 0, pieces[:1])
        if k:
            grad_proj, token = small_call(
                functools.partial(proj_kernel, slabs, images, parts[0][1], part[1]),
                [(proj_weight.shape, F32), ((8, 128), F32)],
                "proj_grad",
                *(ge, *pieces, *msgs),
            )
            token = (token,)
        piece, bit = total, 1
        while 2 * bit < slabs:
            piece = merge(part[1], piece, swap(piece, "dp", bit), *token)
            bit *= 2
        pieces += [piece, swap(piece, "dp", bit)]
    (grad_conv,) = small_call(
        final_kernel, [((count, width), F32)], "sum_slabs", *pieces
    )
    return grad_conv, grad_proj, loss.reshape(1)


def solution(mesh):
    return jax.shard_map(
        local,
        mesh=mesh,
        in_specs=(
            P(("dp", "fsdp"), None),
            P(("dp", "fsdp"), None),
            P("fsdp", None),
            P("fsdp", None),
            P(("dp", "fsdp")),
        ),
        out_specs=(P("fsdp", None), P("fsdp", None), P("fsdp")),
        check_vma=False,
    )
```

```python
import functools

import jax
import jax.numpy as jnp
from jax import lax
from jax.experimental import pallas as pl
from jax.experimental.pallas import tpu as pltpu
from jax.sharding import PartitionSpec as P

POS = 49
GAMMA = 3.0
EPSILON = 1e-06
BF = jnp.bfloat16
F32 = jnp.float32
NT = (((1,), (1,)), ((), ()))
TN = (((0,), (0,)), ((), ()))
VMEM_LIMIT = 8 * 1024 * 1024
SPLIT = 4
ORDER = (0, 2, 3, 1)


def dot(a, b, dims=(((1,), (0,)), ((), ()))):
    return lax.dot_general(a, b, dims, preferred_element_type=F32)


def vspec():
    return pl.BlockSpec(memory_space=pltpu.VMEM)


def params(more=0):
    return pltpu.CompilerParams(vmem_limit_bytes=VMEM_LIMIT + more)


def tile_iota(width):
    return lax.broadcasted_iota(jnp.int32, (8, width), 0)


def pool_rows(hidden, images):
    width = hidden.shape[1]
    row = tile_iota(width)
    pooled = jnp.zeros((images, width), F32)
    for i in range(images):
        first, last = i * POS, i * POS + POS - 1
        total = jnp.zeros((8, width), F32)
        for t in range(first // 8, last // 8 + 1):
            tile = hidden[8 * t : 8 * t + 8]
            if 8 * t < first:
                tile = jnp.where(row >= first - 8 * t, tile, 0.0)
            if 8 * t + 7 > last:
                tile = jnp.where(row <= last - 8 * t, tile, 0.0)
            total = total + tile
        pooled = jnp.where(row == i, jnp.sum(total, axis=0, keepdims=True) / POS, pooled)
    return pooled


def spread_rows(values, images):
    width = values.shape[1]
    row = tile_iota(width)
    whole = [jnp.broadcast_to(values[i : i + 1], (8, width)) for i in range(images)]
    tiles = []
    for t in range(images * POS // 8):
        low, high = 8 * t // POS, (8 * t + 7) // POS
        tiles.append(whole[low] if low == high else jnp.where(row < high * POS - 8 * t, whole[low], whole[high]))
    return jnp.concatenate(tiles, axis=0)


def forward_block(feat, short, convs, images):
    preact = [dot(feat, conv[...], NT) for conv in convs]
    preact = preact[0] if len(preact) == 1 else jnp.concatenate(preact, axis=1)
    hidden = jnp.maximum(preact + short.astype(F32), 0.0)
    mask = jnp.where(hidden > 0, 1.0, 0.0).astype(BF)
    return mask, pool_rows(hidden, images)


def forward_blocks(picks, feats, shorts, convs, projs, embed, outs, ready=None):
    images = outs[2].shape[0] // 2
    for j in range(picks):
        pooled = [None, None]
        for side in (1, 0):
            if ready is not None:
                ready(j, side)
            mask, pooled[side] = forward_block(feats[side][...], shorts[2 * j + side][...], convs[j], images)
            outs[3 * j + side][...] = mask
        pooled = jnp.concatenate(pooled, axis=0).astype(BF)
        outs[3 * j + 2][...] = pooled
        embed = embed + dot(pooled, projs[j][...])
    return embed


def fetcher(sems):
    copies = []

    def fetch(source, target):
        copies.append(pltpu.make_async_copy(source, target, sems.at[len(copies)]))
        copies[-1].start()
        return copies[-1]

    return fetch


def columns(index_ref, pick, count):
    return pl.ds(pl.multiple_of((index_ref[0] ^ (2 * pick)) * count, count), count)


def first_kernel(images, index_ref, f_sib, partner_ref, f_own, s_own, s_sib, conv, proj, *refs):
    blocks, embed_ref, feat, proj_out, member_ref = refs[:3], refs[3], refs[4], refs[5], refs[6]
    short, conv_buf, partner, sems = refs[7:]
    fetch = fetcher(sems)
    at = columns(index_ref, 0, conv_buf.shape[0])
    shorts = [short.at[0], short.at[1]]
    waits = [
        [fetch(conv, conv_buf), fetch(s_sib.at[:, at], shorts[1])],
        [fetch(f_own, feat), fetch(s_own.at[:, at], shorts[0]), fetch(proj, proj_out)],
    ]
    partner_copy = fetch(partner_ref, partner)

    def ready(j, side):
        for copy in waits[1 - side]:
            copy.wait()

    embed = jnp.zeros(embed_ref.shape, F32)
    embed_ref[...] = forward_blocks(1, (feat, f_sib), shorts, [[conv_buf]], [proj_out], embed, blocks, ready)
    partner_copy.wait()
    member = lax.broadcasted_iota(jnp.int32, member_ref.shape, 0)
    whole = jnp.zeros(member_ref.shape, F32)
    for i in range(images):
        whole = jnp.where(member == i, partner[i].astype(F32), whole)
    member_ref[...] = whole


def middle_kernel(blocks, index_ref, f_own, f_sib, before, s_own, s_sib, *refs):
    convs, projs, refs = refs[:blocks], refs[blocks : 2 * blocks], refs[2 * blocks :]
    *outs, embed_ref, ahead_own, ahead_sib, short, sems = refs
    fetch = fetcher(sems)
    targets = [short.at[k] for k in range(2 * blocks)] + [ahead_own, ahead_sib]
    copies = [None] * len(targets)
    for j in range(blocks + 1):
        at = columns(index_ref, j + 1, short.shape[2])
        for side in (1, 0):
            copies[2 * j + side] = fetch((s_own, s_sib)[side].at[:, at], targets[2 * j + side])

    def ready(j, side):
        copies[2 * j + side].wait()

    feats, weights = (f_own, f_sib), [[c] for c in convs]
    embed_ref[...] = forward_blocks(blocks, feats, targets, weights, projs, before[...], outs, ready)
    ready(blocks, 1)
    ready(blocks, 0)


def last_kernel(images, f_own, f_sib, before, member, s_own, s_sib, proj, *refs):
    convs, outs = refs[:-5], refs[-5:]
    embed = forward_blocks(1, (f_own, f_sib), (s_own, s_sib), [convs], [proj], before[...], outs)
    mine_ref, send_ref = outs[-2:]
    half = embed.shape[1] // 2
    whole = jnp.concatenate([member[...]] * (half // member.shape[1]), axis=1)
    none = jnp.zeros((images, half), F32)
    mine_ref[0 : 2 * images] = embed
    mine_ref[2 * images :] = jnp.concatenate([whole, none], axis=1)
    send_ref[0:images] = embed[images:]
    send_ref[images : 2 * images] = embed[:images]
    send_ref[2 * images :] = jnp.concatenate([none, whole], axis=1)


def forward_call(kernel, in_specs, shapes, scratch, busy, name, *arrays):
    rows, width, count = busy
    return pl.pallas_call(
        kernel,
        in_specs=in_specs,
        out_specs=[vspec()] * len(shapes),
        out_shape=[jax.ShapeDtypeStruct(shape, kind) for shape, kind in shapes],
        scratch_shapes=scratch,
        compiler_params=params(),
        cost_estimate=pl.CostEstimate(
            flops=16 * rows * width * count, bytes_accessed=8 * rows * count, transcendentals=0
        ),
        name=name,
    )(*arrays)


def block_shapes(rows, count, images):
    return [((rows, count), BF), ((rows, count), BF), ((2 * images, count), BF)]


def from_hbm(x):
    return pltpu.with_memory_space_constraint(x, pltpu.HBM)


def forward_first(index, partner, feats, shorts, conv, proj, images):
    rows, width = feats[0].shape
    count, embed = proj.shape
    shapes = block_shapes(rows, count, images)
    shapes += [((2 * images, embed), F32), ((rows, width), BF), ((count, embed), BF), ((images, 128), F32)]
    outs = forward_call(
        functools.partial(first_kernel, images),
        [pl.BlockSpec(memory_space=pltpu.SMEM)] + [vspec()] + [pl.BlockSpec(memory_space=pl.ANY)] * 6,
        shapes,
        [
            pltpu.VMEM((2, rows, count), BF),
            pltpu.VMEM((count, width), BF),
            pltpu.SMEM((images,), jnp.int32),
            pltpu.SemaphoreType.DMA((6,)),
        ],
        (rows, width, count),
        "forward_first",
        *(index, feats[1], from_hbm(partner), from_hbm(feats[0]), from_hbm(shorts[0]), from_hbm(shorts[1])),
        *(from_hbm(conv), from_hbm(proj)),
    )
    return outs[:3], outs[3], outs[4], outs[5], outs[6]


def forward_middle(index, feats, shorts, convs, projs, images, before):
    rows, width = feats[0].shape
    count, blocks = convs[0].shape[0], len(convs)
    outs = forward_call(
        functools.partial(middle_kernel, blocks),
        [pl.BlockSpec(memory_space=pltpu.SMEM)]
        + [vspec()] * 3
        + [pl.BlockSpec(memory_space=pl.ANY)] * 2
        + [vspec()] * (2 * blocks),
        block_shapes(rows, count, images) * blocks + [(before.shape, F32)] + [((rows, count), BF)] * 2,
        [pltpu.VMEM((2 * blocks, rows, count), BF), pltpu.SemaphoreType.DMA((2 * blocks + 2,))],
        (rows, width, blocks * count),
        "forward_middle",
        *(index, *feats, before, from_hbm(shorts[0]), from_hbm(shorts[1]), *convs, *projs),
    )
    return [outs[3 * j : 3 * j + 3] for j in range(blocks)], outs[-3], outs[-2:]


def forward_last(feats, shorts, convs, proj, images, before, member):
    rows, width = feats[0].shape
    count, embed = proj.shape
    arrays = (*feats, before, member, *shorts, proj, *convs)
    outs = forward_call(
        functools.partial(last_kernel, images),
        [vspec()] * len(arrays),
        block_shapes(rows, count, images) + [((3 * images, embed), F32)] * 2,
        [],
        (rows, width, count),
        "forward_last",
        *arrays,
    )
    return outs[:3], outs[3], outs[4]


def group_terms(z, partner, groups):
    count = z.shape[0]
    z = z - jnp.mean(z, axis=0, keepdims=True)
    squares = jnp.sum(z * z, axis=1, keepdims=True)
    spread = 2.0 * jnp.mean(squares)
    inner = lax.dot_general(z, z, NT, precision=lax.Precision.HIGHEST, preferred_element_type=F32)
    row = lax.broadcasted_iota(jnp.int32, (count, count), 0)
    col = lax.broadcasted_iota(jnp.int32, (count, count), 1)
    across = jnp.sum(jnp.where(row == col, squares, 0.0), axis=0, keepdims=True)
    kernel = jnp.exp(-(squares + across - 2.0 * inner) / (2.0 * spread))
    r_col = jnp.mean(kernel, axis=1, keepdims=True)
    r_row = jnp.mean(kernel, axis=0, keepdims=True)
    t = jnp.mean(r_col)
    centered = kernel - r_col - r_row + t
    scale_sq = float(count - 1) ** 2
    root = jnp.sqrt(jnp.sum(centered * centered, keepdims=True) / scale_sq + EPSILON)
    onehot = jnp.where(partner == col.astype(F32), 1.0, 0.0)
    positive = jnp.sum(kernel * onehot, keepdims=True) / count
    loss = -(positive - t) + GAMMA * root
    coeff = (-onehot / count + 1.0 / (count * count) + GAMMA * centered / (scale_sq * root)) / groups
    weighted = coeff * kernel
    moved = lax.dot_general(
        weighted, z, (((1,), (0,)), ((), ())), precision=lax.Precision.HIGHEST, preferred_element_type=F32
    )
    return loss, -(2.0 / spread) * (jnp.sum(weighted, axis=1, keepdims=True) * z - moved)


def hsic_kernel(slabs, images, groups, place_ref, *refs):
    chunks = refs[:-5]
    ge_ref, loss_ref, z_ref, p_ref, g_ref = refs[-5:]
    place = place_ref[0]
    half = z_ref.shape[2] // 2
    for j in range(slabs):
        block = chunks[0].at[j] if len(chunks) == 1 else chunks[ORDER.index(j)]
        at = pl.ds(pl.multiple_of((place ^ j) * images, images), images)
        for g in (0, 1):
            z_ref[g, at] = block[g * images : (g + 1) * images]
            p_ref[g, at] = block[2 * images :, g * half : g * half + 128]
    for g in (0, 1):
        partner = jnp.max(p_ref[g], axis=1, keepdims=True)
        loss, grad = group_terms(z_ref[g], partner, groups)
        if g == 0:
            loss_ref[...] = loss
        g_ref[g] = grad
    for j in range(slabs):
        at = pl.ds(pl.multiple_of((place ^ j) * images, images), images)
        for g in (0, 1):
            ge_ref[j, g * images : (g + 1) * images] = g_ref[g, at]


def hsic(place, chunks, slabs, images, groups):
    embed = chunks[0].shape[-1]
    return pl.pallas_call(
        functools.partial(hsic_kernel, slabs, images, groups),
        in_specs=[pl.BlockSpec(memory_space=pltpu.SMEM)] + [vspec()] * len(chunks),
        out_specs=[vspec()] * 2,
        out_shape=[
            jax.ShapeDtypeStruct((slabs, 2 * images, embed), F32),
            jax.ShapeDtypeStruct((1, 1), F32),
        ],
        scratch_shapes=[pltpu.VMEM((2, slabs * images, width), F32) for width in (embed, 128, embed)],
        compiler_params=params(80 * (slabs * images) ** 2),
        cost_estimate=pl.CostEstimate(flops=10**9, bytes_accessed=0, transcendentals=0),
        name="hsic_groups",
    )(place, *([chunks[j] for j in ORDER] if len(chunks) > 1 else chunks))


def backward_kernel(blocks, images, part, extra, after, f_own, f_sib, ge_ref, *refs):
    ins, outs = refs[: 4 * blocks], refs[4 * blocks + after :]
    mine = ge_ref[0].astype(BF)
    start, rows = part
    width = f_own.shape[1]
    grad_pool = [dot(mine, ins[4 * j + 3][start : start + rows], NT) / POS for j in range(blocks)]
    total = jnp.zeros((blocks * rows, width), F32)
    for side, feat in enumerate((f_own, f_sib)):
        grad_hidden = []
        for j in range(blocks):
            spread = spread_rows(grad_pool[j][side * images : (side + 1) * images], images)
            grad_hidden.append(spread.astype(BF) * ins[4 * j + side][:, start : start + rows])
        total = total + dot(jnp.concatenate(grad_hidden, axis=1), feat[...], TN)
    for j in range(blocks):
        out, pooled = outs[j], ins[4 * j + 2]
        out[0:rows] = total[j * rows : (j + 1) * rows].astype(out.dtype)
        if extra == "pooled":
            rest = jnp.zeros((2 * images, width - pooled.shape[1]), BF)
            out[rows:] = jnp.concatenate([pooled[...], rest], axis=1)
        if extra == "embed":
            slabs = ge_ref.shape[0]
            flat = ge_ref[...].reshape(slabs * 2 * images, ge_ref.shape[2]).astype(BF)
            half = slabs * images
            out[rows:] = jnp.concatenate([flat[:half], flat[half:]], axis=1)


def backward(feats, ge, blocks, images, part, extra=None, after=()):
    length, width = feats[0].shape
    rows = part[1]
    high = rows + {None: 0, "pooled": 2 * images, "embed": ge.shape[0] * images}[extra]
    return pl.pallas_call(
        functools.partial(backward_kernel, len(blocks), images, part, extra, len(after)),
        in_specs=[vspec()] * (3 + 4 * len(blocks)) + [pl.BlockSpec(memory_space=pl.ANY)] * len(after),
        out_specs=[vspec()] * len(blocks),
        out_shape=[jax.ShapeDtypeStruct((high, width), BF if extra else F32)] * len(blocks),
        compiler_params=params(),
        cost_estimate=pl.CostEstimate(
            flops=16 * len(blocks) * length * width * rows,
            bytes_accessed=4 * len(blocks) * length * rows,
            transcendentals=0,
        ),
        name="backward_blocks",
    )(*feats, ge, *[a for block in blocks for a in block], *after)


def small_call(kernel, shapes, name, *arrays, tokens=()):
    return pl.pallas_call(
        kernel,
        in_specs=[vspec()] * len(arrays) + [pl.BlockSpec(memory_space=pl.ANY)] * len(tokens),
        out_specs=[vspec()] * len(shapes),
        out_shape=[jax.ShapeDtypeStruct(shape, kind) for shape, kind in shapes],
        compiler_params=params(),
        cost_estimate=pl.CostEstimate(flops=0, bytes_accessed=0, transcendentals=0),
        name=name,
    )(*arrays, *tokens)


def sum_kernel(*refs):
    total = refs[0][...].astype(F32)
    for ref in refs[1:-1]:
        total = total + ref[...].astype(F32)
    refs[-1][...] = total.astype(refs[-1].dtype)


def sum_of(kind, *arrays):
    return small_call(sum_kernel, [(arrays[0].shape, kind)], "sum_arrays", *arrays)[0]


def collect_kernel(start, rows, count_msgs, own, pooled, *refs):
    msgs, out = refs[:count_msgs], refs[-1]
    total = own[start : start + rows]
    for msg in msgs:
        total = total + msg[0:rows].astype(F32)
    out[0:rows] = total.astype(BF)
    if out.shape[0] == rows:
        return
    high, count = pooled.shape
    slab = [pooled[...]] + [msg[rows : rows + high, 0:count] for msg in msgs]
    tall = (out.shape[0] - rows) // high
    for k, piece in enumerate(slab):
        at = rows + k % tall * high
        out[at : at + high, k // tall * count : (k // tall + 1) * count] = piece


def collect(own, pooled, msgs, part, with_pooled, token):
    start, rows = part
    width = own.shape[1]
    more = (len(msgs) + 1) * pooled.size // width if with_pooled else 0
    kernel = functools.partial(collect_kernel, start, rows, len(msgs))
    return small_call(kernel, [((rows + more, width), BF)], "collect_terms", own, pooled, *msgs, tokens=token)[0]


def merge_kernel(rows, mine, other, *refs):
    out = refs[-1]
    out[0:rows] = (mine[0:rows].astype(F32) + other[0:rows].astype(F32)).astype(BF)
    more = mine.shape[0] - rows
    if more:
        out[rows : rows + more] = mine[rows:]
        out[rows + more :] = other[rows:]


def merge(rows, mine, other, *token):
    high, width = mine.shape
    shape = (2 * high - rows, width)
    return small_call(functools.partial(merge_kernel, rows), [(shape, BF)], "merge_slabs", mine, other, tokens=token)[0]


def final_kernel(*refs):
    pieces, out = refs[:-1], refs[-1]
    tail = pieces[2].shape[0]
    head = out.shape[0] - tail
    out[0:head] = pieces[0][0:head].astype(F32) + pieces[1][0:head].astype(F32)
    out[head:] = pieces[2][...].astype(F32) + pieces[3][...].astype(F32)


def proj_kernel(slabs, images, rows, msg_rows, own_ge, mine, other, *refs):
    msgs, (out, token) = refs[:-2], refs[-2:]
    token[...] = jnp.zeros(token.shape, F32)
    count, embed = out.shape
    groups = mine.shape[1] // count
    half = slabs * images
    per = (mine.shape[0] - rows) // (slabs // 2)
    together = per // (2 * images)
    parts = []
    for j in range(slabs):
        pieces = [own_ge[j].astype(BF)]
        start, left = j * 2 * images, 0
        if start >= half:
            start, left = start - half, embed
        for msg in msgs:
            pieces.append(msg[msg_rows + start : msg_rows + start + 2 * images, left : left + embed])
        ref, at = (mine, j) if j < slabs // 2 else (other, j - slabs // 2)
        total = jnp.zeros((count, embed), F32)
        for g in range(groups):
            pooled = ref[rows + at * per : rows + (at + 1) * per, g * count : (g + 1) * count]
            grads = jnp.concatenate(pieces[g * together : (g + 1) * together], axis=0)
            total = total + dot(pooled, grads, TN)
        parts.append(total)
    while len(parts) > 1:
        parts = [parts[k] + parts[k + 1] for k in range(0, len(parts), 2)]
    out[...] = parts[0]


def gate_kernel(x, token, out):
    out[...] = x[...]


def after(x, token):
    return small_call(gate_kernel, [(x.shape, x.dtype)], "gate", x, tokens=(token,))[0]


def part_kernel(start, x, token, out):
    out[...] = x[start : start + out.shape[0]]


def half_of(start, x, token):
    shape = (x.shape[0] // 2, x.shape[1])
    return small_call(functools.partial(part_kernel, start), [(shape, x.dtype)], "half_of", x, tokens=(token,))[0]


def swap(x, axis, bit):
    size = lax.axis_size(axis)
    return lax.ppermute(x, axis, [(i, i ^ bit) for i in range(size)])


def gather_slabs(x, slabs):
    if slabs <= 4:
        return [x] + [swap(x, "dp", j) for j in range(1, slabs)]
    whole = lax.all_gather(x, "dp", axis=0, tiled=False)
    return [jnp.take(whole, lax.axis_index("dp") ^ jnp.arange(slabs), axis=0)]


def local(features, shortcut, conv_weight, proj_weight, partner):
    slabs, groups = lax.axis_size("dp"), lax.axis_size("fsdp")
    peers = groups // 2
    images = features.shape[0] // POS
    count, width = conv_weight.shape
    place = lax.axis_index("dp").astype(jnp.int32).reshape(1)
    index = lax.axis_index("fsdp").astype(jnp.int32).reshape(1)

    f_sib = swap(features, "fsdp", 1)
    s_sib = swap(shortcut, "fsdp", 1)
    shorts = (shortcut, s_sib)
    first, embed, f_own, proj_own, member = forward_first(
        index, partner, (features, f_sib), shorts, conv_weight, proj_weight, images
    )
    feats = (f_own, f_sib)
    projs = [swap(proj_weight, "fsdp", 2 * j) for j in range(1, peers)]
    if peers == 4:
        conv_y = swap(conv_weight, "fsdp", 4)
        conv_x = swap(conv_weight, "fsdp", 2)
        halves = [
            swap(half_of(0, conv_y, embed), "fsdp", 2),
            swap(half_of(count // 2, conv_x, embed), "fsdp", 4),
        ]
        convs = [conv_x, conv_y, halves]
    else:
        convs = [swap(conv_weight, "fsdp", 2 * j) for j in range(1, peers)]
        convs[-1] = [convs[-1]]
    middle, embed, ahead = forward_middle(index, feats, shorts, convs[:-1], projs[:-1], images, embed)
    last, mine, send = forward_last(feats, ahead, convs[-1], projs[-1], images, embed, member)
    blocks, projs = [first, *middle, last], [proj_own, *projs]
    blocks = [(*b, p) for b, p in zip(blocks, projs)]
    embeds = sum_of(F32, mine, swap(send, "fsdp", 1))
    ge, loss = hsic(place, gather_slabs(embeds, slabs), slabs, images, groups)

    first_rows = count * SPLIT // 8
    parts = [(0, first_rows), (first_rows, count - first_rows)]
    terms, done = [], ()
    for part, extra in zip(parts, ("pooled", "embed")):
        done = tuple(backward(feats, ge, blocks[1:], images, part, extra, done))
        terms.append(done)
    (own,) = backward(feats, ge, blocks[:1], images, (0, count), None, done)

    pieces, token = [], ()
    for k, part in enumerate(parts):
        if k:
            terms[k] = [after(m, total) for m in terms[k]]
        msgs = [swap(m, "fsdp", 2 * j) for j, m in enumerate(terms[k], 1)]
        total = collect(own, blocks[0][2], msgs, part, k == 0, pieces[:1])
        if k:
            grad_proj, token = small_call(
                functools.partial(proj_kernel, slabs, images, parts[0][1], part[1]),
                [(proj_weight.shape, F32), ((8, 128), F32)],
                "proj_grad",
                *(ge, *pieces, *msgs),
            )
            token = (pieces[1],)
        piece, bit = total, 1
        while 2 * bit < slabs:
            piece = merge(part[1], piece, swap(piece, "dp", bit), *token)
            bit *= 2
        pieces += [piece, swap(piece, "dp", bit)]
    (grad_conv,) = small_call(
        final_kernel, [((count, width), F32)], "sum_slabs", *pieces
    )
    return grad_conv, grad_proj, loss.reshape(1)


def solution(mesh):
    return jax.shard_map(
        local,
        mesh=mesh,
        in_specs=(
            P(("dp", "fsdp"), None),
            P(("dp", "fsdp"), None),
            P("fsdp", None),
            P("fsdp", None),
            P(("dp", "fsdp")),
        ),
        out_specs=(P("fsdp", None), P("fsdp", None), P("fsdp")),
        check_vma=False,
    )
```

```python
import functools

import jax
import jax.numpy as jnp
from jax import lax
from jax.experimental import pallas as pl
from jax.experimental.pallas import tpu as pltpu
from jax.sharding import PartitionSpec as P

POS = 49
GAMMA = 3.0
EPSILON = 1e-06
BF = jnp.bfloat16
F32 = jnp.float32
NT = (((1,), (1,)), ((), ()))
TN = (((0,), (0,)), ((), ()))
VMEM_LIMIT = 8 * 1024 * 1024
SPLIT = 4
ORDER = (0, 2, 3, 1)


def dot(a, b, dims=(((1,), (0,)), ((), ()))):
    return lax.dot_general(a, b, dims, preferred_element_type=F32)


def vspec():
    return pl.BlockSpec(memory_space=pltpu.VMEM)


def params(more=0):
    return pltpu.CompilerParams(vmem_limit_bytes=VMEM_LIMIT + more)


def tile_iota(width):
    return lax.broadcasted_iota(jnp.int32, (8, width), 0)


def pool_rows(hidden, images):
    width = hidden.shape[1]
    row = tile_iota(width)
    pooled = jnp.zeros((images, width), F32)
    for i in range(images):
        first, last = i * POS, i * POS + POS - 1
        total = jnp.zeros((8, width), F32)
        for t in range(first // 8, last // 8 + 1):
            tile = hidden[8 * t : 8 * t + 8]
            if 8 * t < first:
                tile = jnp.where(row >= first - 8 * t, tile, 0.0)
            if 8 * t + 7 > last:
                tile = jnp.where(row <= last - 8 * t, tile, 0.0)
            total = total + tile
        pooled = jnp.where(row == i, jnp.sum(total, axis=0, keepdims=True) / POS, pooled)
    return pooled


def spread_rows(values, images):
    width = values.shape[1]
    row = tile_iota(width)
    whole = [jnp.broadcast_to(values[i : i + 1], (8, width)) for i in range(images)]
    tiles = []
    for t in range(images * POS // 8):
        low, high = 8 * t // POS, (8 * t + 7) // POS
        tiles.append(whole[low] if low == high else jnp.where(row < high * POS - 8 * t, whole[low], whole[high]))
    return jnp.concatenate(tiles, axis=0)


def forward_block(feat, short, convs, images):
    preact = [dot(feat, conv[...], NT) for conv in convs]
    preact = preact[0] if len(preact) == 1 else jnp.concatenate(preact, axis=1)
    hidden = jnp.maximum(preact + short.astype(F32), 0.0)
    mask = jnp.where(hidden > 0, 1.0, 0.0).astype(BF)
    return mask, pool_rows(hidden, images)


def forward_blocks(picks, feats, shorts, convs, projs, embed, outs, ready=None):
    images = outs[2].shape[0] // 2
    for j in range(picks):
        pooled = [None, None]
        for side in (1, 0):
            if ready is not None:
                ready(j, side)
            mask, pooled[side] = forward_block(feats[side][...], shorts[2 * j + side][...], convs[j], images)
            outs[3 * j + side][...] = mask
        pooled = jnp.concatenate(pooled, axis=0).astype(BF)
        outs[3 * j + 2][...] = pooled
        embed = embed + dot(pooled, projs[j][...])
    return embed


def fetcher(sems):
    copies = []

    def fetch(source, target):
        copies.append(pltpu.make_async_copy(source, target, sems.at[len(copies)]))
        copies[-1].start()
        return copies[-1]

    return fetch


def columns(index_ref, pick, count):
    return pl.ds(pl.multiple_of((index_ref[0] ^ (2 * pick)) * count, count), count)


def first_kernel(images, index_ref, f_sib, partner_ref, f_own, s_own, s_sib, conv, proj, *refs):
    blocks, embed_ref, feat, proj_out, member_ref = refs[:3], refs[3], refs[4], refs[5], refs[6]
    short, conv_buf, partner, sems = refs[7:]
    fetch = fetcher(sems)
    at = columns(index_ref, 0, conv_buf.shape[0])
    shorts = [short.at[0], short.at[1]]
    waits = [
        [fetch(conv, conv_buf), fetch(s_sib.at[:, at], shorts[1])],
        [fetch(f_own, feat), fetch(s_own.at[:, at], shorts[0]), fetch(proj, proj_out)],
    ]
    partner_copy = fetch(partner_ref, partner)

    def ready(j, side):
        for copy in waits[1 - side]:
            copy.wait()

    embed = jnp.zeros(embed_ref.shape, F32)
    embed_ref[...] = forward_blocks(1, (feat, f_sib), shorts, [[conv_buf]], [proj_out], embed, blocks, ready)
    partner_copy.wait()
    member = lax.broadcasted_iota(jnp.int32, member_ref.shape, 0)
    whole = jnp.zeros(member_ref.shape, F32)
    for i in range(images):
        whole = jnp.where(member == i, partner[i].astype(F32), whole)
    member_ref[...] = whole


def middle_kernel(blocks, index_ref, f_own, f_sib, before, s_own, s_sib, *refs):
    convs, projs, refs = refs[:blocks], refs[blocks : 2 * blocks], refs[2 * blocks :]
    *outs, embed_ref, ahead_own, ahead_sib, short, sems = refs
    fetch = fetcher(sems)
    targets = [short.at[k] for k in range(2 * blocks)] + [ahead_own, ahead_sib]
    copies = [None] * len(targets)
    for j in range(blocks + 1):
        at = columns(index_ref, j + 1, short.shape[2])
        for side in (1, 0):
            copies[2 * j + side] = fetch((s_own, s_sib)[side].at[:, at], targets[2 * j + side])

    def ready(j, side):
        copies[2 * j + side].wait()

    feats, weights = (f_own, f_sib), [[c] for c in convs]
    embed_ref[...] = forward_blocks(blocks, feats, targets, weights, projs, before[...], outs, ready)
    ready(blocks, 1)
    ready(blocks, 0)


def last_kernel(images, f_own, f_sib, before, member, s_own, s_sib, proj, *refs):
    convs, outs = refs[:-5], refs[-5:]
    embed = forward_blocks(1, (f_own, f_sib), (s_own, s_sib), [convs], [proj], before[...], outs)
    mine_ref, send_ref = outs[-2:]
    half = embed.shape[1] // 2
    whole = jnp.concatenate([member[...]] * (half // member.shape[1]), axis=1)
    none = jnp.zeros((images, half), F32)
    mine_ref[0 : 2 * images] = embed
    mine_ref[2 * images :] = jnp.concatenate([whole, none], axis=1)
    send_ref[0:images] = embed[images:]
    send_ref[images : 2 * images] = embed[:images]
    send_ref[2 * images :] = jnp.concatenate([none, whole], axis=1)


def forward_call(kernel, in_specs, shapes, scratch, busy, name, *arrays):
    rows, width, count = busy
    return pl.pallas_call(
        kernel,
        in_specs=in_specs,
        out_specs=[vspec()] * len(shapes),
        out_shape=[jax.ShapeDtypeStruct(shape, kind) for shape, kind in shapes],
        scratch_shapes=scratch,
        compiler_params=params(),
        cost_estimate=pl.CostEstimate(
            flops=16 * rows * width * count, bytes_accessed=8 * rows * count, transcendentals=0
        ),
        name=name,
    )(*arrays)


def block_shapes(rows, count, images):
    return [((rows, count), BF), ((rows, count), BF), ((2 * images, count), BF)]


def from_hbm(x):
    return pltpu.with_memory_space_constraint(x, pltpu.HBM)


def forward_first(index, partner, feats, shorts, conv, proj, images):
    rows, width = feats[0].shape
    count, embed = proj.shape
    shapes = block_shapes(rows, count, images)
    shapes += [((2 * images, embed), F32), ((rows, width), BF), ((count, embed), BF), ((images, 128), F32)]
    outs = forward_call(
        functools.partial(first_kernel, images),
        [pl.BlockSpec(memory_space=pltpu.SMEM)] + [vspec()] + [pl.BlockSpec(memory_space=pl.ANY)] * 6,
        shapes,
        [
            pltpu.VMEM((2, rows, count), BF),
            pltpu.VMEM((count, width), BF),
            pltpu.SMEM((images,), jnp.int32),
            pltpu.SemaphoreType.DMA((6,)),
        ],
        (rows, width, count),
        "forward_first",
        *(index, feats[1], from_hbm(partner), from_hbm(feats[0]), from_hbm(shorts[0]), from_hbm(shorts[1])),
        *(from_hbm(conv), from_hbm(proj)),
    )
    return outs[:3], outs[3], outs[4], outs[5], outs[6]


def forward_middle(index, feats, shorts, convs, projs, images, before):
    rows, width = feats[0].shape
    count, blocks = convs[0].shape[0], len(convs)
    outs = forward_call(
        functools.partial(middle_kernel, blocks),
        [pl.BlockSpec(memory_space=pltpu.SMEM)]
        + [vspec()] * 3
        + [pl.BlockSpec(memory_space=pl.ANY)] * 2
        + [vspec()] * (2 * blocks),
        block_shapes(rows, count, images) * blocks + [(before.shape, F32)] + [((rows, count), BF)] * 2,
        [pltpu.VMEM((2 * blocks, rows, count), BF), pltpu.SemaphoreType.DMA((2 * blocks + 2,))],
        (rows, width, blocks * count),
        "forward_middle",
        *(index, *feats, before, from_hbm(shorts[0]), from_hbm(shorts[1]), *convs, *projs),
    )
    return [outs[3 * j : 3 * j + 3] for j in range(blocks)], outs[-3], outs[-2:]


def forward_last(feats, shorts, convs, proj, images, before, member):
    rows, width = feats[0].shape
    count, embed = proj.shape
    arrays = (*feats, before, member, *shorts, proj, *convs)
    outs = forward_call(
        functools.partial(last_kernel, images),
        [vspec()] * len(arrays),
        block_shapes(rows, count, images) + [((3 * images, embed), F32)] * 2,
        [],
        (rows, width, count),
        "forward_last",
        *arrays,
    )
    return outs[:3], outs[3], outs[4]


def group_terms(z, partner, groups):
    count = z.shape[0]
    z = z - jnp.mean(z, axis=0, keepdims=True)
    squares = jnp.sum(z * z, axis=1, keepdims=True)
    spread = 2.0 * jnp.mean(squares)
    inner = lax.dot_general(z, z, NT, precision=lax.Precision.HIGHEST, preferred_element_type=F32)
    row = lax.broadcasted_iota(jnp.int32, (count, count), 0)
    col = lax.broadcasted_iota(jnp.int32, (count, count), 1)
    across = jnp.sum(jnp.where(row == col, squares, 0.0), axis=0, keepdims=True)
    kernel = jnp.exp(-(squares + across - 2.0 * inner) / (2.0 * spread))
    r_col = jnp.mean(kernel, axis=1, keepdims=True)
    r_row = jnp.mean(kernel, axis=0, keepdims=True)
    t = jnp.mean(r_col)
    centered = kernel - r_col - r_row + t
    scale_sq = float(count - 1) ** 2
    root = jnp.sqrt(jnp.sum(centered * centered, keepdims=True) / scale_sq + EPSILON)
    onehot = jnp.where(partner == col.astype(F32), 1.0, 0.0)
    positive = jnp.sum(kernel * onehot, keepdims=True) / count
    loss = -(positive - t) + GAMMA * root
    coeff = (-onehot / count + 1.0 / (count * count) + GAMMA * centered / (scale_sq * root)) / groups
    weighted = coeff * kernel
    moved = lax.dot_general(
        weighted, z, (((1,), (0,)), ((), ())), precision=lax.Precision.HIGHEST, preferred_element_type=F32
    )
    return loss, -(2.0 / spread) * (jnp.sum(weighted, axis=1, keepdims=True) * z - moved)


def hsic_kernel(slabs, images, groups, place_ref, *refs):
    chunks = refs[:-6]
    ge_ref, loss_ref, odd_ref, z_ref, p_ref, g_ref = refs[-6:]
    place = place_ref[0]
    odd_ref[...] = jnp.full(odd_ref.shape, (place & 1).astype(F32))
    half = z_ref.shape[2] // 2
    for j in range(slabs):
        block = chunks[0].at[j] if len(chunks) == 1 else chunks[ORDER.index(j)]
        at = pl.ds(pl.multiple_of((place ^ j) * images, images), images)
        for g in (0, 1):
            z_ref[g, at] = block[g * images : (g + 1) * images]
            p_ref[g, at] = block[2 * images :, g * half : g * half + 128]
    for g in (0, 1):
        partner = jnp.max(p_ref[g], axis=1, keepdims=True)
        loss, grad = group_terms(z_ref[g], partner, groups)
        if g == 0:
            loss_ref[...] = loss
        g_ref[g] = grad
    for j in range(slabs):
        at = pl.ds(pl.multiple_of((place ^ j) * images, images), images)
        for g in (0, 1):
            ge_ref[j, g * images : (g + 1) * images] = g_ref[g, at]


def hsic(place, chunks, slabs, images, groups):
    embed = chunks[0].shape[-1]
    return pl.pallas_call(
        functools.partial(hsic_kernel, slabs, images, groups),
        in_specs=[pl.BlockSpec(memory_space=pltpu.SMEM)] + [vspec()] * len(chunks),
        out_specs=[vspec()] * 3,
        out_shape=[
            jax.ShapeDtypeStruct((slabs, 2 * images, embed), F32),
            jax.ShapeDtypeStruct((1, 1), F32),
            jax.ShapeDtypeStruct((8, 128), F32),
        ],
        scratch_shapes=[pltpu.VMEM((2, slabs * images, width), F32) for width in (embed, 128, embed)],
        compiler_params=params(80 * (slabs * images) ** 2),
        cost_estimate=pl.CostEstimate(flops=10**9, bytes_accessed=0, transcendentals=0),
        name="hsic_groups",
    )(place, *([chunks[j] for j in ORDER] if len(chunks) > 1 else chunks))


def backward_kernel(blocks, images, part, extra, after, f_own, f_sib, ge_ref, *refs):
    ins, outs = refs[: 4 * blocks], refs[4 * blocks + after :]
    mine = ge_ref[0].astype(BF)
    start, rows = part
    width = f_own.shape[1]
    grad_pool = [dot(mine, ins[4 * j + 3][start : start + rows], NT) / POS for j in range(blocks)]
    total = jnp.zeros((blocks * rows, width), F32)
    for side, feat in enumerate((f_own, f_sib)):
        grad_hidden = []
        for j in range(blocks):
            spread = spread_rows(grad_pool[j][side * images : (side + 1) * images], images)
            grad_hidden.append(spread.astype(BF) * ins[4 * j + side][:, start : start + rows])
        total = total + dot(jnp.concatenate(grad_hidden, axis=1), feat[...], TN)
    for j in range(blocks):
        out, pooled = outs[j], ins[4 * j + 2]
        out[0:rows] = total[j * rows : (j + 1) * rows].astype(out.dtype)
        if extra == "pooled":
            rest = jnp.zeros((2 * images, width - pooled.shape[1]), BF)
            out[rows:] = jnp.concatenate([pooled[...], rest], axis=1)
        if extra == "embed":
            slabs = ge_ref.shape[0]
            flat = ge_ref[...].reshape(slabs * 2 * images, ge_ref.shape[2]).astype(BF)
            half = slabs * images
            out[rows:] = jnp.concatenate([flat[:half], flat[half:]], axis=1)


def backward(feats, ge, blocks, images, part, extra=None, after=()):
    length, width = feats[0].shape
    rows = part[1]
    high = rows + {None: 0, "pooled": 2 * images, "embed": ge.shape[0] * images}[extra]
    return pl.pallas_call(
        functools.partial(backward_kernel, len(blocks), images, part, extra, len(after)),
        in_specs=[vspec()] * (3 + 4 * len(blocks)) + [pl.BlockSpec(memory_space=pl.ANY)] * len(after),
        out_specs=[vspec()] * len(blocks),
        out_shape=[jax.ShapeDtypeStruct((high, width), BF if extra else F32)] * len(blocks),
        compiler_params=params(),
        cost_estimate=pl.CostEstimate(
            flops=16 * len(blocks) * length * width * rows,
            bytes_accessed=4 * len(blocks) * length * rows,
            transcendentals=0,
        ),
        name="backward_blocks",
    )(*feats, ge, *[a for block in blocks for a in block], *after)


def small_call(kernel, shapes, name, *arrays, tokens=()):
    return pl.pallas_call(
        kernel,
        in_specs=[vspec()] * len(arrays) + [pl.BlockSpec(memory_space=pl.ANY)] * len(tokens),
        out_specs=[vspec()] * len(shapes),
        out_shape=[jax.ShapeDtypeStruct(shape, kind) for shape, kind in shapes],
        compiler_params=params(),
        cost_estimate=pl.CostEstimate(flops=0, bytes_accessed=0, transcendentals=0),
        name=name,
    )(*arrays, *tokens)


def sum_kernel(*refs):
    total = refs[0][...].astype(F32)
    for ref in refs[1:-1]:
        total = total + ref[...].astype(F32)
    refs[-1][...] = total.astype(refs[-1].dtype)


def sum_of(kind, *arrays):
    return small_call(sum_kernel, [(arrays[0].shape, kind)], "sum_arrays", *arrays)[0]


def collect_kernel(start, rows, count_msgs, own, pooled, *refs):
    msgs, out = refs[:count_msgs], refs[-1]
    total = own[start : start + rows]
    for msg in msgs:
        total = total + msg[0:rows].astype(F32)
    out[0:rows] = total.astype(BF)
    if out.shape[0] == rows:
        return
    high, count = pooled.shape
    slab = [pooled[...]] + [msg[rows : rows + high, 0:count] for msg in msgs]
    tall = (out.shape[0] - rows) // high
    for k, piece in enumerate(slab):
        at = rows + k % tall * high
        out[at : at + high, k // tall * count : (k // tall + 1) * count] = piece


def collect(own, pooled, msgs, part, with_pooled, token):
    start, rows = part
    width = own.shape[1]
    more = (len(msgs) + 1) * pooled.size // width if with_pooled else 0
    kernel = functools.partial(collect_kernel, start, rows, len(msgs))
    return small_call(kernel, [((rows + more, width), BF)], "collect_terms", own, pooled, *msgs, tokens=token)[0]


def merge_kernel(rows, mine, other, *refs):
    out = refs[-1]
    out[0:rows] = (mine[0:rows].astype(F32) + other[0:rows].astype(F32)).astype(BF)
    more = mine.shape[0] - rows
    if more:
        out[rows : rows + more] = mine[rows:]
        out[rows + more :] = other[rows:]


def merge(rows, mine, other, *token):
    high, width = mine.shape
    shape = (2 * high - rows, width)
    return small_call(functools.partial(merge_kernel, rows), [(shape, BF)], "merge_slabs", mine, other, tokens=token)[0]


def choose(odd, width):
    return jnp.broadcast_to(odd[0:1, 0:1], (1, width)) > 0.5


def collect_halves_kernel(start, rows, own, pooled, odd, *refs):
    msgs, (keep, send, slab_ref) = refs[:-3], refs[-3:]
    width, half = own.shape[1], rows // 2
    total = own[start : start + rows]
    for msg in msgs:
        total = total + msg[0:rows].astype(F32)
    total = total.astype(BF).astype(F32)
    pick = choose(odd, width)
    keep[...] = jnp.where(pick, total[half:], total[:half]).astype(BF)
    send[...] = jnp.where(pick, total[:half], total[half:]).astype(BF)
    high, count = pooled.shape
    slab = [pooled[...]] + [msg[rows : rows + high, 0:count] for msg in msgs]
    tall = slab_ref.shape[0] // high
    for k, piece in enumerate(slab):
        at = k % tall * high
        slab_ref[at : at + high, k // tall * count : (k // tall + 1) * count] = piece


def add_and_append_kernel(rows, count, mine, other, *refs):
    more, out = refs[:count], refs[-1]
    out[0:rows] = (mine[0:rows].astype(F32) + other[0:rows].astype(F32)).astype(BF)
    at = rows
    for ref in more:
        tail = ref[...] if ref.shape[0] < rows else ref[rows:]
        out[at : at + tail.shape[0]] = tail
        at += tail.shape[0]


def sum_by_halves(own, pooled, odd, msgs, part, token, late):
    start, rows = part
    width, half = own.shape[1], rows // 2
    slab_rows = (len(msgs) + 1) * pooled.size // width
    keep, send, slab = small_call(
        functools.partial(collect_halves_kernel, start, rows),
        [((half, width), BF), ((half, width), BF), ((slab_rows, width), BF)],
        "collect_terms",
        *(own, pooled, odd, *msgs),
    )
    first = small_call(
        functools.partial(add_and_append_kernel, half, 1),
        [((half + slab_rows, width), BF)],
        "merge_slabs",
        *(keep, swap(send, "dp", 1), slab),
        tokens=token,
    )[0]
    far = swap(first, "dp", 2)
    mine = small_call(
        functools.partial(add_and_append_kernel, half, 2),
        [((half + 2 * slab_rows, width), BF)],
        "merge_slabs",
        *(first, far, first, far),
        tokens=late,
    )[0]
    return mine, swap(mine, "dp", 1)


def final_halves(odd, mine, other, pieces, out):
    tail = pieces[0].shape[0]
    head = out.shape[0] - tail
    half = head // 2
    pick = choose(odd, out.shape[1])
    left, right = mine[0:half].astype(F32), other[0:half].astype(F32)
    out[0:half] = jnp.where(pick, right, left)
    out[half:head] = jnp.where(pick, left, right)
    out[head:] = pieces[0][...].astype(F32) + pieces[1][...].astype(F32)


def final_whole(pieces, out):
    tail = pieces[2].shape[0]
    head = out.shape[0] - tail
    out[0:head] = pieces[0][0:head].astype(F32) + pieces[1][0:head].astype(F32)
    out[head:] = pieces[2][...].astype(F32) + pieces[3][...].astype(F32)


def proj_sum(slabs, images, order, rows, msg_rows, own_ge, mine, other, msgs, out):
    count, embed = out.shape
    groups = mine.shape[1] // count
    half = slabs * images
    per = (mine.shape[0] - rows) // (slabs // 2)
    together = per // (2 * images)
    parts = []
    for j in range(slabs):
        pieces = [own_ge[j].astype(BF)]
        start, left = j * 2 * images, 0
        if start >= half:
            start, left = start - half, embed
        for msg in msgs:
            pieces.append(msg[msg_rows + start : msg_rows + start + 2 * images, left : left + embed])
        at = order.index(j)
        ref, at = (mine, at) if at < slabs // 2 else (other, at - slabs // 2)
        total = jnp.zeros((count, embed), F32)
        for g in range(groups):
            pooled = ref[rows + at * per : rows + (at + 1) * per, g * count : (g + 1) * count]
            grads = jnp.concatenate(pieces[g * together : (g + 1) * together], axis=0)
            total = total + dot(pooled, grads, TN)
        parts.append(total)
    while len(parts) > 1:
        parts = [parts[k] + parts[k + 1] for k in range(0, len(parts), 2)]
    out[...] = parts[0]


def gate_kernel(x, token, out):
    out[...] = x[...]


def after(x, token):
    return small_call(gate_kernel, [(x.shape, x.dtype)], "gate", x, tokens=(token,))[0]


def part_kernel(start, x, token, out):
    out[...] = x[start : start + out.shape[0]]


def half_of(start, x, token):
    shape = (x.shape[0] // 2, x.shape[1])
    return small_call(functools.partial(part_kernel, start), [(shape, x.dtype)], "half_of", x, tokens=(token,))[0]


def last_sums_kernel(slabs, images, order, rows, msg_rows, own_ge, odd, last_mine, last_other, mine, other, *refs):
    msgs, (conv_out, proj_out) = refs[:-2], refs[-2:]
    proj_sum(slabs, images, order, rows, msg_rows, own_ge, mine, other, msgs, proj_out)
    if slabs == 4:
        final_halves(odd, mine, other, (last_mine, last_other), conv_out)
    else:
        final_whole((mine, other, last_mine, last_other), conv_out)


def swap(x, axis, bit):
    size = lax.axis_size(axis)
    return lax.ppermute(x, axis, [(i, i ^ bit) for i in range(size)])


def gather_slabs(x, slabs):
    if slabs <= 4:
        return [x] + [swap(x, "dp", j) for j in range(1, slabs)]
    whole = lax.all_gather(x, "dp", axis=0, tiled=False)
    return [jnp.take(whole, lax.axis_index("dp") ^ jnp.arange(slabs), axis=0)]


def local(features, shortcut, conv_weight, proj_weight, partner):
    slabs, groups = lax.axis_size("dp"), lax.axis_size("fsdp")
    peers = groups // 2
    images = features.shape[0] // POS
    count, width = conv_weight.shape
    place = lax.axis_index("dp").astype(jnp.int32).reshape(1)
    index = lax.axis_index("fsdp").astype(jnp.int32).reshape(1)

    f_sib = swap(features, "fsdp", 1)
    s_sib = swap(shortcut, "fsdp", 1)
    shorts = (shortcut, s_sib)
    first, embed, f_own, proj_own, member = forward_first(
        index, partner, (features, f_sib), shorts, conv_weight, proj_weight, images
    )
    feats = (f_own, f_sib)
    projs = [swap(proj_weight, "fsdp", 2 * j) for j in range(1, peers)]
    if peers == 4:
        conv_y = swap(conv_weight, "fsdp", 4)
        conv_x = swap(conv_weight, "fsdp", 2)
        halves = [
            swap(half_of(0, conv_y, embed), "fsdp", 2),
            swap(half_of(count // 2, conv_x, embed), "fsdp", 4),
        ]
        convs = [conv_x, conv_y, halves]
    else:
        convs = [swap(conv_weight, "fsdp", 2 * j) for j in range(1, peers)]
        convs[-1] = [convs[-1]]
    middle, embed, ahead = forward_middle(index, feats, shorts, convs[:-1], projs[:-1], images, embed)
    last, mine, send = forward_last(feats, ahead, convs[-1], projs[-1], images, embed, member)
    blocks, projs = [first, *middle, last], [proj_own, *projs]
    blocks = [(*b, p) for b, p in zip(blocks, projs)]
    embeds = sum_of(F32, mine, swap(send, "fsdp", 1))
    ge, loss, odd = hsic(place, gather_slabs(embeds, slabs), slabs, images, groups)

    first_rows = count * SPLIT // 8
    parts = [(0, first_rows), (first_rows, count - first_rows)]
    terms, done = [], ()
    for part, extra in zip(parts, ("pooled", "embed")):
        done = tuple(backward(feats, ge, blocks[1:], images, part, extra, done))
        terms.append(done)
    (own,) = backward(feats, ge, blocks[:1], images, (0, count), None, done)

    received = [[swap(m, "fsdp", 2 * j) for j, m in enumerate(term, 1)] for term in terms]
    total = collect(own, blocks[0][2], received[1], parts[1], False, ())
    if slabs == 4:
        merged = merge(parts[1][1], total, swap(total, "dp", 1))
        mine, other = sum_by_halves(own, blocks[0][2], odd, received[0], parts[0], (), (merged,))
        pieces = [mine, other, merged, swap(merged, "dp", 2)]
        order, above = [0, 2, 1, 3], parts[0][1] // 2
    else:
        pieces, order, above = [], list(range(slabs)), parts[0][1]
        for piece, part in zip((collect(own, blocks[0][2], received[0], parts[0], True, ()), total), parts):
            bit = 1
            while 2 * bit < slabs:
                piece = merge(part[1], piece, swap(piece, "dp", bit))
                bit *= 2
            pieces += [piece, swap(piece, "dp", bit)]
    grad_conv, grad_proj = small_call(
        functools.partial(last_sums_kernel, slabs, images, order, above, parts[1][1]),
        [((count, width), F32), (proj_weight.shape, F32)],
        "last_sums",
        *(ge, odd, pieces[2], pieces[3], pieces[0], pieces[1], *received[1]),
    )
    return grad_conv, grad_proj, loss.reshape(1)


def solution(mesh):
    return jax.shard_map(
        local,
        mesh=mesh,
        in_specs=(
            P(("dp", "fsdp"), None),
            P(("dp", "fsdp"), None),
            P("fsdp", None),
            P("fsdp", None),
            P(("dp", "fsdp")),
        ),
        out_specs=(P("fsdp", None), P("fsdp", None), P("fsdp")),
        check_vma=False,
    )
```

```python
import functools

import jax
import jax.numpy as jnp
from jax import lax
from jax.experimental import pallas as pl
from jax.experimental.pallas import tpu as pltpu
from jax.sharding import PartitionSpec as P

POS = 49
GAMMA = 3.0
EPSILON = 1e-06
BF = jnp.bfloat16
F32 = jnp.float32
NT = (((1,), (1,)), ((), ()))
TN = (((0,), (0,)), ((), ()))
VMEM_LIMIT = 8 * 1024 * 1024
SPLIT = 4
ORDER = (0, 2, 3, 1)


def dot(a, b, dims=(((1,), (0,)), ((), ()))):
    return lax.dot_general(a, b, dims, preferred_element_type=F32)


def vspec():
    return pl.BlockSpec(memory_space=pltpu.VMEM)


def params(more=0):
    return pltpu.CompilerParams(vmem_limit_bytes=VMEM_LIMIT + more)


def tile_iota(width):
    return lax.broadcasted_iota(jnp.int32, (8, width), 0)


def pool_rows(hidden, images):
    width = hidden.shape[1]
    row = tile_iota(width)
    pooled = jnp.zeros((images, width), F32)
    for i in range(images):
        first, last = i * POS, i * POS + POS - 1
        total = jnp.zeros((8, width), F32)
        for t in range(first // 8, last // 8 + 1):
            tile = hidden[8 * t : 8 * t + 8]
            if 8 * t < first:
                tile = jnp.where(row >= first - 8 * t, tile, 0.0)
            if 8 * t + 7 > last:
                tile = jnp.where(row <= last - 8 * t, tile, 0.0)
            total = total + tile
        pooled = jnp.where(row == i, jnp.sum(total, axis=0, keepdims=True) / POS, pooled)
    return pooled


def spread_rows(values, images):
    width = values.shape[1]
    row = tile_iota(width)
    whole = [jnp.broadcast_to(values[i : i + 1], (8, width)) for i in range(images)]
    tiles = []
    for t in range(images * POS // 8):
        low, high = 8 * t // POS, (8 * t + 7) // POS
        tiles.append(whole[low] if low == high else jnp.where(row < high * POS - 8 * t, whole[low], whole[high]))
    return jnp.concatenate(tiles, axis=0)


def forward_block(feat, short, convs, images):
    preact = [dot(feat, conv[...], NT) for conv in convs]
    preact = preact[0] if len(preact) == 1 else jnp.concatenate(preact, axis=1)
    hidden = jnp.maximum(preact + short.astype(F32), 0.0)
    mask = jnp.where(hidden > 0, 1.0, 0.0).astype(BF)
    return mask, pool_rows(hidden, images)


def forward_blocks(picks, feats, shorts, convs, projs, embed, outs, ready=None):
    images = outs[2].shape[0] // 2
    for j in range(picks):
        pooled = [None, None]
        for side in (1, 0):
            if ready is not None:
                ready(j, side)
            mask, pooled[side] = forward_block(feats[side][...], shorts[2 * j + side][...], convs[j], images)
            outs[3 * j + side][...] = mask
        pooled = jnp.concatenate(pooled, axis=0).astype(BF)
        outs[3 * j + 2][...] = pooled
        embed = embed + dot(pooled, projs[j][...])
    return embed


def fetcher(sems):
    copies = []

    def fetch(source, target):
        copies.append(pltpu.make_async_copy(source, target, sems.at[len(copies)]))
        copies[-1].start()
        return copies[-1]

    return fetch


def columns(index_ref, pick, count):
    return pl.ds(pl.multiple_of((index_ref[0] ^ (2 * pick)) * count, count), count)


def first_kernel(images, index_ref, f_sib, partner_ref, f_own, s_own, s_sib, conv, proj, *refs):
    blocks, embed_ref, feat, proj_out, member_ref = refs[:3], refs[3], refs[4], refs[5], refs[6]
    short, conv_buf, partner, sems = refs[7:]
    fetch = fetcher(sems)
    at = columns(index_ref, 0, conv_buf.shape[0])
    shorts = [short.at[0], short.at[1]]
    waits = [
        [fetch(conv, conv_buf), fetch(s_sib.at[:, at], shorts[1])],
        [fetch(f_own, feat), fetch(s_own.at[:, at], shorts[0]), fetch(proj, proj_out)],
    ]
    partner_copy = fetch(partner_ref, partner)

    def ready(j, side):
        for copy in waits[1 - side]:
            copy.wait()

    embed = jnp.zeros(embed_ref.shape, F32)
    embed_ref[...] = forward_blocks(1, (feat, f_sib), shorts, [[conv_buf]], [proj_out], embed, blocks, ready)
    partner_copy.wait()
    member = lax.broadcasted_iota(jnp.int32, member_ref.shape, 0)
    whole = jnp.zeros(member_ref.shape, F32)
    for i in range(images):
        whole = jnp.where(member == i, partner[i].astype(F32), whole)
    member_ref[...] = whole


def middle_kernel(blocks, index_ref, f_own, f_sib, before, s_own, s_sib, *refs):
    convs, projs, refs = refs[:blocks], refs[blocks : 2 * blocks], refs[2 * blocks :]
    *outs, embed_ref, ahead_own, ahead_sib, short, sems = refs
    fetch = fetcher(sems)
    targets = [short.at[k] for k in range(2 * blocks)] + [ahead_own, ahead_sib]
    copies = [None] * len(targets)
    for j in range(blocks + 1):
        at = columns(index_ref, j + 1, short.shape[2])
        for side in (1, 0):
            copies[2 * j + side] = fetch((s_own, s_sib)[side].at[:, at], targets[2 * j + side])

    def ready(j, side):
        copies[2 * j + side].wait()

    feats, weights = (f_own, f_sib), [[c] for c in convs]
    embed_ref[...] = forward_blocks(blocks, feats, targets, weights, projs, before[...], outs, ready)
    ready(blocks, 1)
    ready(blocks, 0)


def last_kernel(images, f_own, f_sib, before, member, s_own, s_sib, proj, *refs):
    convs, outs = refs[:-5], refs[-5:]
    embed = forward_blocks(1, (f_own, f_sib), (s_own, s_sib), [convs], [proj], before[...], outs)
    mine_ref, send_ref = outs[-2:]
    lanes = member.shape[1]
    tiles = embed.shape[1] // lanes
    for g in (0, 1):
        for t in range(tiles):
            piece = embed[g * images : (g + 1) * images, t * lanes : (t + 1) * lanes]
            at = (g * tiles + t) * images
            mine_ref[at : at + images] = piece
            at = ((1 - g) * tiles + t) * images
            send_ref[at : at + images] = piece
    low = lax.broadcasted_iota(jnp.int32, (images, lanes), 1) < lanes // 2
    mine_ref[2 * tiles * images :] = jnp.where(low, member[...], 0.0)
    send_ref[2 * tiles * images :] = jnp.where(low, 0.0, member[...])


def forward_call(kernel, in_specs, shapes, scratch, busy, name, *arrays):
    rows, width, count = busy
    return pl.pallas_call(
        kernel,
        in_specs=in_specs,
        out_specs=[vspec()] * len(shapes),
        out_shape=[jax.ShapeDtypeStruct(shape, kind) for shape, kind in shapes],
        scratch_shapes=scratch,
        compiler_params=params(),
        cost_estimate=pl.CostEstimate(
            flops=16 * rows * width * count, bytes_accessed=8 * rows * count, transcendentals=0
        ),
        name=name,
    )(*arrays)


def block_shapes(rows, count, images):
    return [((rows, count), BF), ((rows, count), BF), ((2 * images, count), BF)]


def from_hbm(x):
    return pltpu.with_memory_space_constraint(x, pltpu.HBM)


def forward_first(index, partner, feats, shorts, conv, proj, images):
    rows, width = feats[0].shape
    count, embed = proj.shape
    shapes = block_shapes(rows, count, images)
    shapes += [((2 * images, embed), F32), ((rows, width), BF), ((count, embed), BF), ((images, 128), F32)]
    outs = forward_call(
        functools.partial(first_kernel, images),
        [pl.BlockSpec(memory_space=pltpu.SMEM)] + [vspec()] + [pl.BlockSpec(memory_space=pl.ANY)] * 6,
        shapes,
        [
            pltpu.VMEM((2, rows, count), BF),
            pltpu.VMEM((count, width), BF),
            pltpu.SMEM((images,), jnp.int32),
            pltpu.SemaphoreType.DMA((6,)),
        ],
        (rows, width, count),
        "forward_first",
        *(index, feats[1], from_hbm(partner), from_hbm(feats[0]), from_hbm(shorts[0]), from_hbm(shorts[1])),
        *(from_hbm(conv), from_hbm(proj)),
    )
    return outs[:3], outs[3], outs[4], outs[5], outs[6]


def forward_middle(index, feats, shorts, convs, projs, images, before):
    rows, width = feats[0].shape
    count, blocks = convs[0].shape[0], len(convs)
    outs = forward_call(
        functools.partial(middle_kernel, blocks),
        [pl.BlockSpec(memory_space=pltpu.SMEM)]
        + [vspec()] * 3
        + [pl.BlockSpec(memory_space=pl.ANY)] * 2
        + [vspec()] * (2 * blocks),
        block_shapes(rows, count, images) * blocks + [(before.shape, F32)] + [((rows, count), BF)] * 2,
        [pltpu.VMEM((2 * blocks, rows, count), BF), pltpu.SemaphoreType.DMA((2 * blocks + 2,))],
        (rows, width, blocks * count),
        "forward_middle",
        *(index, *feats, before, from_hbm(shorts[0]), from_hbm(shorts[1]), *convs, *projs),
    )
    return [outs[3 * j : 3 * j + 3] for j in range(blocks)], outs[-3], outs[-2:]


def forward_last(feats, shorts, convs, proj, images, before, member):
    rows, width = feats[0].shape
    count, embed = proj.shape
    arrays = (*feats, before, member, *shorts, proj, *convs)
    outs = forward_call(
        functools.partial(last_kernel, images),
        [vspec()] * len(arrays),
        block_shapes(rows, count, images) + [(((2 * embed // 128 + 1) * images, 128), F32)] * 2,
        [],
        (rows, width, count),
        "forward_last",
        *arrays,
    )
    return outs[:3], outs[3], outs[4]


def group_terms(z, partner, groups):
    count = z.shape[0]
    z = z - jnp.mean(z, axis=0, keepdims=True)
    squares = jnp.sum(z * z, axis=1, keepdims=True)
    spread = 2.0 * jnp.mean(squares)
    inner = lax.dot_general(z, z, NT, precision=lax.Precision.HIGHEST, preferred_element_type=F32)
    row = lax.broadcasted_iota(jnp.int32, (count, count), 0)
    col = lax.broadcasted_iota(jnp.int32, (count, count), 1)
    across = jnp.sum(jnp.where(row == col, squares, 0.0), axis=0, keepdims=True)
    kernel = jnp.exp(-(squares + across - 2.0 * inner) / (2.0 * spread))
    r_col = jnp.mean(kernel, axis=1, keepdims=True)
    r_row = jnp.mean(kernel, axis=0, keepdims=True)
    t = jnp.mean(r_col)
    centered = kernel - r_col - r_row + t
    scale_sq = float(count - 1) ** 2
    root = jnp.sqrt(jnp.sum(centered * centered, keepdims=True) / scale_sq + EPSILON)
    onehot = jnp.where(partner == col.astype(F32), 1.0, 0.0)
    positive = jnp.sum(kernel * onehot, keepdims=True) / count
    loss = -(positive - t) + GAMMA * root
    coeff = (-onehot / count + 1.0 / (count * count) + GAMMA * centered / (scale_sq * root)) / groups
    weighted = coeff * kernel
    moved = lax.dot_general(
        weighted, z, (((1,), (0,)), ((), ())), precision=lax.Precision.HIGHEST, preferred_element_type=F32
    )
    return loss, -(2.0 / spread) * (jnp.sum(weighted, axis=1, keepdims=True) * z - moved)


def hsic_kernel(slabs, images, groups, place_ref, *refs):
    chunks = refs[:-6]
    ge_ref, loss_ref, odd_ref, z_ref, p_ref, g_ref = refs[-6:]
    place = place_ref[0]
    odd_ref[...] = jnp.full(odd_ref.shape, (place & 1).astype(F32))
    tiles = z_ref.shape[2] // 128
    for j in range(slabs):
        block = chunks[0].at[j] if len(chunks) == 1 else chunks[ORDER.index(j)]
        at = pl.ds(pl.multiple_of((place ^ j) * images, images), images)
        for g in (0, 1):
            for t in range(tiles):
                row = (g * tiles + t) * images
                z_ref[g, at, t * 128 : (t + 1) * 128] = block[row : row + images]
        p_ref[at] = block[2 * tiles * images :]
    high_lane = lax.broadcasted_iota(jnp.int32, p_ref.shape, 1) >= 64
    for g in (0, 1):
        partner = jnp.max(jnp.where(high_lane == (g == 1), p_ref[...], -1.0), axis=1, keepdims=True)
        loss, grad = group_terms(z_ref[g], partner, groups)
        if g == 0:
            loss_ref[...] = loss
        g_ref[g] = grad
    for j in range(slabs):
        at = pl.ds(pl.multiple_of((place ^ j) * images, images), images)
        for g in (0, 1):
            ge_ref[j, g * images : (g + 1) * images] = g_ref[g, at]


def hsic(place, chunks, embed, slabs, images, groups):
    return pl.pallas_call(
        functools.partial(hsic_kernel, slabs, images, groups),
        in_specs=[pl.BlockSpec(memory_space=pltpu.SMEM)] + [vspec()] * len(chunks),
        out_specs=[vspec()] * 3,
        out_shape=[
            jax.ShapeDtypeStruct((slabs, 2 * images, embed), F32),
            jax.ShapeDtypeStruct((1, 1), F32),
            jax.ShapeDtypeStruct((8, 128), F32),
        ],
        scratch_shapes=[
            pltpu.VMEM((2, slabs * images, embed), F32),
            pltpu.VMEM((slabs * images, 128), F32),
            pltpu.VMEM((2, slabs * images, embed), F32),
        ],
        compiler_params=params(80 * (slabs * images) ** 2),
        cost_estimate=pl.CostEstimate(flops=10**9, bytes_accessed=0, transcendentals=0),
        name="hsic_groups",
    )(place, *([chunks[j] for j in ORDER] if len(chunks) > 1 else chunks))


def backward_kernel(blocks, images, part, extra, after, f_own, f_sib, ge_ref, *refs):
    ins, outs = refs[: 4 * blocks], refs[4 * blocks + after :]
    mine = ge_ref[0].astype(BF)
    start, rows = part
    width = f_own.shape[1]
    grad_pool = [dot(mine, ins[4 * j + 3][start : start + rows], NT) / POS for j in range(blocks)]
    total = jnp.zeros((blocks * rows, width), F32)
    for side, feat in enumerate((f_own, f_sib)):
        grad_hidden = []
        for j in range(blocks):
            spread = spread_rows(grad_pool[j][side * images : (side + 1) * images], images)
            grad_hidden.append(spread.astype(BF) * ins[4 * j + side][:, start : start + rows])
        total = total + dot(jnp.concatenate(grad_hidden, axis=1), feat[...], TN)
    for j in range(blocks):
        out, pooled = outs[j], ins[4 * j + 2]
        out[0:rows] = total[j * rows : (j + 1) * rows].astype(out.dtype)
        if extra == "pooled":
            rest = jnp.zeros((2 * images, width - pooled.shape[1]), BF)
            out[rows:] = jnp.concatenate([pooled[...], rest], axis=1)
        if extra == "embed":
            half = ge_ref.shape[0] * images // 2
            flat = ge_ref[:, :images].reshape(2 * half, ge_ref.shape[2]).astype(BF)
            out[rows:] = jnp.concatenate([flat[:half], flat[half:]], axis=1)


def backward(feats, ge, blocks, images, part, extra=None, after=()):
    length, width = feats[0].shape
    rows = part[1]
    high = rows + {None: 0, "pooled": 2 * images, "embed": ge.shape[0] * images // 2}[extra]
    return pl.pallas_call(
        functools.partial(backward_kernel, len(blocks), images, part, extra, len(after)),
        in_specs=[vspec()] * (3 + 4 * len(blocks)) + [pl.BlockSpec(memory_space=pl.ANY)] * len(after),
        out_specs=[vspec()] * len(blocks),
        out_shape=[jax.ShapeDtypeStruct((high, width), BF if extra else F32)] * len(blocks),
        compiler_params=params(),
        cost_estimate=pl.CostEstimate(
            flops=16 * len(blocks) * length * width * rows,
            bytes_accessed=4 * len(blocks) * length * rows,
            transcendentals=0,
        ),
        name="backward_blocks",
    )(*feats, ge, *[a for block in blocks for a in block], *after)


def small_call(kernel, shapes, name, *arrays, tokens=()):
    return pl.pallas_call(
        kernel,
        in_specs=[vspec()] * len(arrays) + [pl.BlockSpec(memory_space=pl.ANY)] * len(tokens),
        out_specs=[vspec()] * len(shapes),
        out_shape=[jax.ShapeDtypeStruct(shape, kind) for shape, kind in shapes],
        compiler_params=params(),
        cost_estimate=pl.CostEstimate(flops=0, bytes_accessed=0, transcendentals=0),
        name=name,
    )(*arrays, *tokens)


def sum_kernel(*refs):
    total = refs[0][...].astype(F32)
    for ref in refs[1:-1]:
        total = total + ref[...].astype(F32)
    refs[-1][...] = total.astype(refs[-1].dtype)


def sum_of(kind, *arrays):
    return small_call(sum_kernel, [(arrays[0].shape, kind)], "sum_arrays", *arrays)[0]


def collect_kernel(start, rows, count_msgs, own, pooled, *refs):
    msgs, out = refs[:count_msgs], refs[-1]
    total = own[start : start + rows]
    for msg in msgs:
        total = total + msg[0:rows].astype(F32)
    out[0:rows] = total.astype(BF)
    if out.shape[0] == rows:
        return
    high, count = pooled.shape
    slab = [pooled[...]] + [msg[rows : rows + high, 0:count] for msg in msgs]
    tall = (out.shape[0] - rows) // high
    for k, piece in enumerate(slab):
        at = rows + k % tall * high
        out[at : at + high, k // tall * count : (k // tall + 1) * count] = piece


def collect(own, pooled, msgs, part, with_pooled, token):
    start, rows = part
    width = own.shape[1]
    more = (len(msgs) + 1) * pooled.size // width if with_pooled else 0
    kernel = functools.partial(collect_kernel, start, rows, len(msgs))
    return small_call(kernel, [((rows + more, width), BF)], "collect_terms", own, pooled, *msgs, tokens=token)[0]


def collect_grads_kernel(start, rows, own, *refs):
    msgs, (out, tails) = refs[:-2], refs[-2:]
    total = own[start : start + rows]
    for msg in msgs:
        total = total + msg[0:rows].astype(F32)
    out[...] = total.astype(BF)
    high = msgs[0].shape[0] - rows
    for k, msg in enumerate(msgs):
        tails[k * high : (k + 1) * high] = msg[rows:]


def collect_grads(own, msgs, part):
    start, rows = part
    width = own.shape[1]
    shapes = [((rows, width), BF), ((len(msgs) * (msgs[0].shape[0] - rows), width), BF)]
    return small_call(functools.partial(collect_grads_kernel, start, rows), shapes, "collect_terms", own, *msgs)


def merge_kernel(rows, mine, other, *refs):
    out = refs[-1]
    out[0:rows] = (mine[0:rows].astype(F32) + other[0:rows].astype(F32)).astype(BF)
    more = mine.shape[0] - rows
    if more:
        out[rows : rows + more] = mine[rows:]
        out[rows + more :] = other[rows:]


def merge(rows, mine, other, *token):
    high, width = mine.shape
    shape = (2 * high - rows, width)
    return small_call(functools.partial(merge_kernel, rows), [(shape, BF)], "merge_slabs", mine, other, tokens=token)[0]


def choose(odd, width):
    return jnp.broadcast_to(odd[0:1, 0:1], (1, width)) > 0.5


def collect_halves_kernel(start, rows, own, pooled, odd, *refs):
    msgs, (keep, send, slab_ref) = refs[:-3], refs[-3:]
    width, half = own.shape[1], rows // 2
    total = own[start : start + rows]
    for msg in msgs:
        total = total + msg[0:rows].astype(F32)
    total = total.astype(BF).astype(F32)
    pick = choose(odd, width)
    keep[...] = jnp.where(pick, total[half:], total[:half]).astype(BF)
    send[...] = jnp.where(pick, total[:half], total[half:]).astype(BF)
    high, count = pooled.shape
    slab = [pooled[...]] + [msg[rows : rows + high, 0:count] for msg in msgs]
    tall = slab_ref.shape[0] // high
    for k, piece in enumerate(slab):
        at = k % tall * high
        slab_ref[at : at + high, k // tall * count : (k // tall + 1) * count] = piece


def add_and_append_kernel(rows, count, mine, other, *refs):
    more, out = refs[:count], refs[-1]
    out[0:rows] = (mine[0:rows].astype(F32) + other[0:rows].astype(F32)).astype(BF)
    at = rows
    for ref in more:
        tail = ref[...] if ref.shape[0] < rows else ref[rows:]
        out[at : at + tail.shape[0]] = tail
        at += tail.shape[0]


def sum_by_halves(own, pooled, odd, msgs, part, token, late):
    start, rows = part
    width, half = own.shape[1], rows // 2
    slab_rows = (len(msgs) + 1) * pooled.size // width
    keep, send, slab = small_call(
        functools.partial(collect_halves_kernel, start, rows),
        [((half, width), BF), ((half, width), BF), ((slab_rows, width), BF)],
        "collect_terms",
        *(own, pooled, odd, *msgs),
    )
    first = small_call(
        functools.partial(add_and_append_kernel, half, 1),
        [((half + slab_rows, width), BF)],
        "merge_slabs",
        *(keep, swap(send, "dp", 1), slab),
        tokens=token,
    )[0]
    far = swap(first, "dp", 2)
    mine = small_call(
        functools.partial(add_and_append_kernel, half, 2),
        [((half + 2 * slab_rows, width), BF)],
        "merge_slabs",
        *(first, far, first, far),
        tokens=late,
    )[0]
    return mine, swap(mine, "dp", 1)


def final_halves(odd, mine, other, pieces, out):
    tail = pieces[0].shape[0]
    head = out.shape[0] - tail
    half = head // 2
    pick = choose(odd, out.shape[1])
    left, right = mine[0:half].astype(F32), other[0:half].astype(F32)
    out[0:half] = jnp.where(pick, right, left)
    out[half:head] = jnp.where(pick, left, right)
    out[head:] = pieces[0][...].astype(F32) + pieces[1][...].astype(F32)


def final_whole(pieces, out):
    tail = pieces[2].shape[0]
    head = out.shape[0] - tail
    out[0:head] = pieces[0][0:head].astype(F32) + pieces[1][0:head].astype(F32)
    out[head:] = pieces[2][...].astype(F32) + pieces[3][...].astype(F32)


def proj_sum(slabs, images, order, rows, own_ge, mine, other, tails, out):
    count, embed = out.shape
    groups = mine.shape[1] // count
    half = slabs * images // 2
    per = (mine.shape[0] - rows) // (slabs // 2)
    together = per // (2 * images)
    parts = []
    for j in range(slabs):
        pieces = [own_ge[j].astype(BF)]
        start, left = j * images % half, j * images // half * embed
        base = start // 16 * 16
        for k in range(0, tails[0].shape[0], half):
            pair = [t[k + base : k + base + 16, left : left + embed].astype(F32) for t in tails]
            pieces.append(jnp.concatenate([p[start - base : start - base + images] for p in pair], axis=0).astype(BF))
        at = order.index(j)
        ref, at = (mine, at) if at < slabs // 2 else (other, at - slabs // 2)
        total = jnp.zeros((count, embed), F32)
        for g in range(groups):
            pooled = ref[rows + at * per : rows + (at + 1) * per, g * count : (g + 1) * count]
            grads = jnp.concatenate(pieces[g * together : (g + 1) * together], axis=0)
            total = total + dot(pooled, grads, TN)
        parts.append(total)
    while len(parts) > 1:
        parts = [parts[k] + parts[k + 1] for k in range(0, len(parts), 2)]
    out[...] = parts[0]


def gate_kernel(x, token, out):
    out[...] = x[...]


def after(x, token):
    return small_call(gate_kernel, [(x.shape, x.dtype)], "gate", x, tokens=(token,))[0]


def part_kernel(start, x, token, out):
    out[...] = x[start : start + out.shape[0]]


def half_of(start, x, token):
    shape = (x.shape[0] // 2, x.shape[1])
    return small_call(functools.partial(part_kernel, start), [(shape, x.dtype)], "half_of", x, tokens=(token,))[0]


def last_sums_kernel(slabs, images, order, rows, own_ge, odd, last_mine, last_other, mine, other, *refs):
    tails, (conv_out, proj_out) = refs[:-2], refs[-2:]
    proj_sum(slabs, images, order, rows, own_ge, mine, other, tails, proj_out)
    if slabs == 4:
        final_halves(odd, mine, other, (last_mine, last_other), conv_out)
    else:
        final_whole((mine, other, last_mine, last_other), conv_out)


def swap(x, axis, bit):
    size = lax.axis_size(axis)
    return lax.ppermute(x, axis, [(i, i ^ bit) for i in range(size)])


def gather_slabs(x, slabs):
    if slabs <= 4:
        return [x] + [swap(x, "dp", j) for j in range(1, slabs)]
    whole = lax.all_gather(x, "dp", axis=0, tiled=False)
    return [jnp.take(whole, lax.axis_index("dp") ^ jnp.arange(slabs), axis=0)]


def local(features, shortcut, conv_weight, proj_weight, partner):
    slabs, groups = lax.axis_size("dp"), lax.axis_size("fsdp")
    peers = groups // 2
    images = features.shape[0] // POS
    count, width = conv_weight.shape
    place = lax.axis_index("dp").astype(jnp.int32).reshape(1)
    index = lax.axis_index("fsdp").astype(jnp.int32).reshape(1)

    f_sib = swap(features, "fsdp", 1)
    s_sib = swap(shortcut, "fsdp", 1)
    shorts = (shortcut, s_sib)
    first, embed, f_own, proj_own, member = forward_first(
        index, partner, (features, f_sib), shorts, conv_weight, proj_weight, images
    )
    feats = (f_own, f_sib)
    projs = [swap(proj_weight, "fsdp", 2 * j) for j in range(1, peers)]
    if peers == 4:
        conv_y = swap(conv_weight, "fsdp", 4)
        conv_x = swap(conv_weight, "fsdp", 2)
        halves = [
            swap(half_of(0, conv_y, embed), "fsdp", 2),
            swap(half_of(count // 2, conv_x, embed), "fsdp", 4),
        ]
        convs = [conv_x, conv_y, halves]
    else:
        convs = [swap(conv_weight, "fsdp", 2 * j) for j in range(1, peers)]
        convs[-1] = [convs[-1]]
    middle, embed, ahead = forward_middle(index, feats, shorts, convs[:-1], projs[:-1], images, embed)
    last, mine, send = forward_last(feats, ahead, convs[-1], projs[-1], images, embed, member)
    blocks, projs = [first, *middle, last], [proj_own, *projs]
    blocks = [(*b, p) for b, p in zip(blocks, projs)]
    embeds = sum_of(F32, mine, swap(send, "fsdp", 1))
    ge, loss, odd = hsic(place, gather_slabs(embeds, slabs), proj_weight.shape[1], slabs, images, groups)

    first_rows = count * SPLIT // 8
    parts = [(0, first_rows), (first_rows, count - first_rows)]
    terms, done = [], ()
    for part, extra in zip(parts, ("pooled", "embed")):
        done = tuple(backward(feats, ge, blocks[1:], images, part, extra, done))
        terms.append(done)
    (own,) = backward(feats, ge, blocks[:1], images, (0, count), None, done)

    received = [[swap(m, "fsdp", 2 * j) for j, m in enumerate(term, 1)] for term in terms]
    total, tails = collect_grads(own, received[1], parts[1])
    if slabs == 4:
        merged = merge(parts[1][1], total, swap(total, "dp", 1))
        mine, other = sum_by_halves(own, blocks[0][2], odd, received[0], parts[0], (), (merged,))
        pieces = [mine, other, merged, swap(merged, "dp", 2)]
        order, above = [0, 2, 1, 3], parts[0][1] // 2
    else:
        pieces, order, above = [], list(range(slabs)), parts[0][1]
        for piece, part in zip((collect(own, blocks[0][2], received[0], parts[0], True, ()), total), parts):
            bit = 1
            while 2 * bit < slabs:
                piece = merge(part[1], piece, swap(piece, "dp", bit))
                bit *= 2
            pieces += [piece, swap(piece, "dp", bit)]
    grad_conv, grad_proj = small_call(
        functools.partial(last_sums_kernel, slabs, images, order, above),
        [((count, width), F32), (proj_weight.shape, F32)],
        "last_sums",
        *(ge, odd, pieces[2], pieces[3], pieces[0], pieces[1], tails, swap(tails, "fsdp", 1)),
    )
    return grad_conv, grad_proj, loss.reshape(1)


def solution(mesh):
    return jax.shard_map(
        local,
        mesh=mesh,
        in_specs=(
            P(("dp", "fsdp"), None),
            P(("dp", "fsdp"), None),
            P("fsdp", None),
            P("fsdp", None),
            P(("dp", "fsdp")),
        ),
        out_specs=(P("fsdp", None), P("fsdp", None), P("fsdp")),
        check_vma=False,
    )
```

```python
import functools

import jax
import jax.numpy as jnp
from jax import lax
from jax.experimental import pallas as pl
from jax.experimental.pallas import tpu as pltpu
from jax.sharding import PartitionSpec as P

POS = 49
GAMMA = 3.0
EPSILON = 1e-06
BF = jnp.bfloat16
F32 = jnp.float32
NT = (((1,), (1,)), ((), ()))
TN = (((0,), (0,)), ((), ()))
VMEM_LIMIT = 8 * 1024 * 1024
SPLIT = 4
ORDER = (0, 2, 3, 1)


def dot(a, b, dims=(((1,), (0,)), ((), ()))):
    return lax.dot_general(a, b, dims, preferred_element_type=F32)


def vspec():
    return pl.BlockSpec(memory_space=pltpu.VMEM)


def params(more=0):
    return pltpu.CompilerParams(vmem_limit_bytes=VMEM_LIMIT + more)


def tile_iota(width):
    return lax.broadcasted_iota(jnp.int32, (8, width), 0)


def pool_rows(hidden, images):
    width = hidden.shape[1]
    row = tile_iota(width)
    pooled = jnp.zeros((images, width), F32)
    for i in range(images):
        first, last = i * POS, i * POS + POS - 1
        total = jnp.zeros((8, width), F32)
        for t in range(first // 8, last // 8 + 1):
            tile = hidden[8 * t : 8 * t + 8]
            if 8 * t < first:
                tile = jnp.where(row >= first - 8 * t, tile, 0.0)
            if 8 * t + 7 > last:
                tile = jnp.where(row <= last - 8 * t, tile, 0.0)
            total = total + tile
        pooled = jnp.where(row == i, jnp.sum(total, axis=0, keepdims=True) / POS, pooled)
    return pooled


def spread_rows(values, images):
    width = values.shape[1]
    row = tile_iota(width)
    whole = [jnp.broadcast_to(values[i : i + 1], (8, width)) for i in range(images)]
    tiles = []
    for t in range(images * POS // 8):
        low, high = 8 * t // POS, (8 * t + 7) // POS
        tiles.append(whole[low] if low == high else jnp.where(row < high * POS - 8 * t, whole[low], whole[high]))
    return jnp.concatenate(tiles, axis=0)


def forward_block(feat, short, convs, images):
    preact = [dot(feat, conv[...], NT) for conv in convs]
    preact = preact[0] if len(preact) == 1 else jnp.concatenate(preact, axis=1)
    hidden = jnp.maximum(preact + short.astype(F32), 0.0)
    mask = jnp.where(hidden > 0, 1.0, 0.0).astype(BF)
    return mask, pool_rows(hidden, images)


def forward_blocks(picks, feats, shorts, convs, projs, embed, outs, ready=None):
    images = outs[2].shape[0] // 2
    for j in range(picks):
        pooled = [None, None]
        for side in (1, 0):
            if ready is not None:
                ready(j, side)
            mask, pooled[side] = forward_block(feats[side][...], shorts[2 * j + side][...], convs[j], images)
            outs[3 * j + side][...] = mask
        pooled = jnp.concatenate(pooled, axis=0).astype(BF)
        outs[3 * j + 2][...] = pooled
        embed = embed + dot(pooled, projs[j][...])
    return embed


def fetcher(sems):
    copies = []

    def fetch(source, target):
        copies.append(pltpu.make_async_copy(source, target, sems.at[len(copies)]))
        copies[-1].start()
        return copies[-1]

    return fetch


def columns(index_ref, pick, count):
    return pl.ds(pl.multiple_of((index_ref[0] ^ (2 * pick)) * count, count), count)


def first_kernel(images, index_ref, f_sib, partner_ref, f_own, s_own, s_sib, conv, proj, *refs):
    blocks, embed_ref, feat, proj_out, member_ref = refs[:3], refs[3], refs[4], refs[5], refs[6]
    short, conv_buf, partner, sems = refs[7:]
    fetch = fetcher(sems)
    at = columns(index_ref, 0, conv_buf.shape[0])
    shorts = [short.at[0], short.at[1]]
    waits = [
        [fetch(conv, conv_buf), fetch(s_sib.at[:, at], shorts[1])],
        [fetch(f_own, feat), fetch(s_own.at[:, at], shorts[0]), fetch(proj, proj_out)],
    ]
    partner_copy = fetch(partner_ref, partner)

    def ready(j, side):
        for copy in waits[1 - side]:
            copy.wait()

    embed = jnp.zeros(embed_ref.shape, F32)
    embed_ref[...] = forward_blocks(1, (feat, f_sib), shorts, [[conv_buf]], [proj_out], embed, blocks, ready)
    partner_copy.wait()
    member = lax.broadcasted_iota(jnp.int32, member_ref.shape, 0)
    whole = jnp.zeros(member_ref.shape, F32)
    for i in range(images):
        whole = jnp.where(member == i, partner[i].astype(F32), whole)
    member_ref[...] = whole


def middle_kernel(blocks, index_ref, f_own, f_sib, before, s_own, s_sib, *refs):
    convs, projs, refs = refs[:blocks], refs[blocks : 2 * blocks], refs[2 * blocks :]
    *outs, embed_ref, ahead_own, ahead_sib, short, sems = refs
    fetch = fetcher(sems)
    targets = [short.at[k] for k in range(2 * blocks)] + [ahead_own, ahead_sib]
    copies = [None] * len(targets)
    for j in range(blocks + 1):
        at = columns(index_ref, j + 1, short.shape[2])
        for side in (1, 0):
            copies[2 * j + side] = fetch((s_own, s_sib)[side].at[:, at], targets[2 * j + side])

    def ready(j, side):
        copies[2 * j + side].wait()

    feats, weights = (f_own, f_sib), [[c] for c in convs]
    embed_ref[...] = forward_blocks(blocks, feats, targets, weights, projs, before[...], outs, ready)
    ready(blocks, 1)
    ready(blocks, 0)


def last_kernel(images, f_own, f_sib, before, member, s_own, s_sib, proj, *refs):
    convs, outs = refs[:-5], refs[-5:]
    embed = forward_blocks(1, (f_own, f_sib), (s_own, s_sib), [convs], [proj], before[...], outs)
    mine_ref, send_ref = outs[-2:]
    lanes = member.shape[1]
    tiles = embed.shape[1] // lanes
    for g in (0, 1):
        for t in range(tiles):
            piece = embed[g * images : (g + 1) * images, t * lanes : (t + 1) * lanes]
            at = (g * tiles + t) * images
            mine_ref[at : at + images] = piece
            at = ((1 - g) * tiles + t) * images
            send_ref[at : at + images] = piece
    low = lax.broadcasted_iota(jnp.int32, (images, lanes), 1) < lanes // 2
    mine_ref[2 * tiles * images :] = jnp.where(low, member[...], 0.0)
    send_ref[2 * tiles * images :] = jnp.where(low, 0.0, member[...])


def forward_call(kernel, in_specs, shapes, scratch, busy, name, *arrays):
    rows, width, count = busy
    return pl.pallas_call(
        kernel,
        in_specs=in_specs,
        out_specs=[vspec()] * len(shapes),
        out_shape=[jax.ShapeDtypeStruct(shape, kind) for shape, kind in shapes],
        scratch_shapes=scratch,
        compiler_params=params(),
        cost_estimate=pl.CostEstimate(
            flops=16 * rows * width * count, bytes_accessed=8 * rows * count, transcendentals=0
        ),
        name=name,
    )(*arrays)


def block_shapes(rows, count, images):
    return [((rows, count), BF), ((rows, count), BF), ((2 * images, count), BF)]


def from_hbm(x):
    return pltpu.with_memory_space_constraint(x, pltpu.HBM)


def forward_first(index, partner, feats, shorts, conv, proj, images):
    rows, width = feats[0].shape
    count, embed = proj.shape
    shapes = block_shapes(rows, count, images)
    shapes += [((2 * images, embed), F32), ((rows, width), BF), ((count, embed), BF), ((images, 128), F32)]
    outs = forward_call(
        functools.partial(first_kernel, images),
        [pl.BlockSpec(memory_space=pltpu.SMEM)] + [vspec()] + [pl.BlockSpec(memory_space=pl.ANY)] * 6,
        shapes,
        [
            pltpu.VMEM((2, rows, count), BF),
            pltpu.VMEM((count, width), BF),
            pltpu.SMEM((images,), jnp.int32),
            pltpu.SemaphoreType.DMA((6,)),
        ],
        (rows, width, count),
        "forward_first",
        *(index, feats[1], from_hbm(partner), from_hbm(feats[0]), from_hbm(shorts[0]), from_hbm(shorts[1])),
        *(from_hbm(conv), from_hbm(proj)),
    )
    return outs[:3], outs[3], outs[4], outs[5], outs[6]


def forward_middle(index, feats, shorts, convs, projs, images, before):
    rows, width = feats[0].shape
    count, blocks = convs[0].shape[0], len(convs)
    outs = forward_call(
        functools.partial(middle_kernel, blocks),
        [pl.BlockSpec(memory_space=pltpu.SMEM)]
        + [vspec()] * 3
        + [pl.BlockSpec(memory_space=pl.ANY)] * 2
        + [vspec()] * (2 * blocks),
        block_shapes(rows, count, images) * blocks + [(before.shape, F32)] + [((rows, count), BF)] * 2,
        [pltpu.VMEM((2 * blocks, rows, count), BF), pltpu.SemaphoreType.DMA((2 * blocks + 2,))],
        (rows, width, blocks * count),
        "forward_middle",
        *(index, *feats, before, from_hbm(shorts[0]), from_hbm(shorts[1]), *convs, *projs),
    )
    return [outs[3 * j : 3 * j + 3] for j in range(blocks)], outs[-3], outs[-2:]


def forward_last(feats, shorts, convs, proj, images, before, member):
    rows, width = feats[0].shape
    count, embed = proj.shape
    arrays = (*feats, before, member, *shorts, proj, *convs)
    outs = forward_call(
        functools.partial(last_kernel, images),
        [vspec()] * len(arrays),
        block_shapes(rows, count, images) + [(((2 * embed // 128 + 1) * images, 128), F32)] * 2,
        [],
        (rows, width, count),
        "forward_last",
        *arrays,
    )
    return outs[:3], outs[3], outs[4]


def group_terms(z, partner, groups):
    count = z.shape[0]
    z = z - jnp.mean(z, axis=0, keepdims=True)
    squares = jnp.sum(z * z, axis=1, keepdims=True)
    spread = 2.0 * jnp.mean(squares)
    inner = lax.dot_general(z, z, NT, precision=lax.Precision.HIGHEST, preferred_element_type=F32)
    row = lax.broadcasted_iota(jnp.int32, (count, count), 0)
    col = lax.broadcasted_iota(jnp.int32, (count, count), 1)
    across = jnp.sum(jnp.where(row == col, squares, 0.0), axis=0, keepdims=True)
    kernel = jnp.exp(-(squares + across - 2.0 * inner) / (2.0 * spread))
    r_col = jnp.mean(kernel, axis=1, keepdims=True)
    r_row = jnp.mean(kernel, axis=0, keepdims=True)
    t = jnp.mean(r_col)
    centered = kernel - r_col - r_row + t
    scale_sq = float(count - 1) ** 2
    root = jnp.sqrt(jnp.sum(centered * centered, keepdims=True) / scale_sq + EPSILON)
    onehot = jnp.where(partner == col.astype(F32), 1.0, 0.0)
    positive = jnp.sum(kernel * onehot, keepdims=True) / count
    loss = -(positive - t) + GAMMA * root
    coeff = (-onehot / count + 1.0 / (count * count) + GAMMA * centered / (scale_sq * root)) / groups
    weighted = coeff * kernel
    moved = lax.dot_general(
        weighted, z, (((1,), (0,)), ((), ())), precision=lax.Precision.HIGHEST, preferred_element_type=F32
    )
    return loss, -(2.0 / spread) * (jnp.sum(weighted, axis=1, keepdims=True) * z - moved)


def hsic_kernel(slabs, images, groups, place_ref, *refs):
    chunks = refs[:-6]
    ge_ref, loss_ref, odd_ref, z_ref, p_ref, g_ref = refs[-6:]
    place = place_ref[0]
    odd_ref[...] = jnp.full(odd_ref.shape, (place & 1).astype(F32))
    tiles = z_ref.shape[2] // 128
    for j in range(slabs):
        block = chunks[0].at[j] if len(chunks) == 1 else chunks[ORDER.index(j)]
        at = pl.ds(pl.multiple_of((place ^ j) * images, images), images)
        for g in (0, 1):
            for t in range(tiles):
                row = (g * tiles + t) * images
                z_ref[g, at, t * 128 : (t + 1) * 128] = block[row : row + images]
        p_ref[at] = block[2 * tiles * images :]
    high_lane = lax.broadcasted_iota(jnp.int32, p_ref.shape, 1) >= 64
    for g in (0, 1):
        partner = jnp.max(jnp.where(high_lane == (g == 1), p_ref[...], -1.0), axis=1, keepdims=True)
        loss, grad = group_terms(z_ref[g], partner, groups)
        if g == 0:
            loss_ref[...] = loss
        g_ref[g] = grad
    for j in range(slabs):
        at = pl.ds(pl.multiple_of((place ^ j) * images, images), images)
        for g in (0, 1):
            ge_ref[j, g * images : (g + 1) * images] = g_ref[g, at]


def hsic(place, chunks, embed, slabs, images, groups):
    return pl.pallas_call(
        functools.partial(hsic_kernel, slabs, images, groups),
        in_specs=[pl.BlockSpec(memory_space=pltpu.SMEM)] + [vspec()] * len(chunks),
        out_specs=[vspec()] * 3,
        out_shape=[
            jax.ShapeDtypeStruct((slabs, 2 * images, embed), F32),
            jax.ShapeDtypeStruct((1, 1), F32),
            jax.ShapeDtypeStruct((8, 128), F32),
        ],
        scratch_shapes=[
            pltpu.VMEM((2, slabs * images, embed), F32),
            pltpu.VMEM((slabs * images, 128), F32),
            pltpu.VMEM((2, slabs * images, embed), F32),
        ],
        compiler_params=params(80 * (slabs * images) ** 2),
        cost_estimate=pl.CostEstimate(flops=10**9, bytes_accessed=0, transcendentals=0),
        name="hsic_groups",
    )(place, *([chunks[j] for j in ORDER] if len(chunks) > 1 else chunks))


def backward_kernel(blocks, images, part, extra, after, f_own, f_sib, ge_ref, *refs):
    ins, outs = refs[: 4 * blocks], refs[4 * blocks + after :]
    mine = ge_ref[0].astype(BF)
    start, rows = part
    width = f_own.shape[1]
    grad_pool = [dot(mine, ins[4 * j + 3][start : start + rows], NT) / POS for j in range(blocks)]
    total = jnp.zeros((blocks * rows, width), F32)
    for side, feat in enumerate((f_own, f_sib)):
        grad_hidden = []
        for j in range(blocks):
            spread = spread_rows(grad_pool[j][side * images : (side + 1) * images], images)
            grad_hidden.append(spread.astype(BF) * ins[4 * j + side][:, start : start + rows])
        total = total + dot(jnp.concatenate(grad_hidden, axis=1), feat[...], TN)
    for j in range(blocks):
        out, pooled = outs[j], ins[4 * j + 2]
        out[0:rows] = total[j * rows : (j + 1) * rows].astype(out.dtype)
        if extra == "pooled":
            rest = jnp.zeros((2 * images, width - pooled.shape[1]), BF)
            out[rows:] = jnp.concatenate([pooled[...], rest], axis=1)
        if extra == "embed":
            half = ge_ref.shape[0] * images // 2
            flat = ge_ref[:, :images].reshape(2 * half, ge_ref.shape[2]).astype(BF)
            out[rows:] = jnp.concatenate([flat[:half], flat[half:]], axis=1)


def backward(feats, ge, blocks, images, part, extra=None, after=()):
    length, width = feats[0].shape
    rows = part[1]
    high = rows + {None: 0, "pooled": 2 * images, "embed": ge.shape[0] * images // 2}[extra]
    return pl.pallas_call(
        functools.partial(backward_kernel, len(blocks), images, part, extra, len(after)),
        in_specs=[vspec()] * (3 + 4 * len(blocks)) + [pl.BlockSpec(memory_space=pl.ANY)] * len(after),
        out_specs=[vspec()] * len(blocks),
        out_shape=[jax.ShapeDtypeStruct((high, width), BF if extra else F32)] * len(blocks),
        compiler_params=params(),
        cost_estimate=pl.CostEstimate(
            flops=16 * len(blocks) * length * width * rows,
            bytes_accessed=4 * len(blocks) * length * rows,
            transcendentals=0,
        ),
        name="backward_blocks",
    )(*feats, ge, *[a for block in blocks for a in block], *after)


def small_call(kernel, shapes, name, *arrays, tokens=()):
    return pl.pallas_call(
        kernel,
        in_specs=[vspec()] * len(arrays) + [pl.BlockSpec(memory_space=pl.ANY)] * len(tokens),
        out_specs=[vspec()] * len(shapes),
        out_shape=[jax.ShapeDtypeStruct(shape, kind) for shape, kind in shapes],
        compiler_params=params(),
        cost_estimate=pl.CostEstimate(flops=0, bytes_accessed=0, transcendentals=0),
        name=name,
    )(*arrays, *tokens)


def sum_kernel(*refs):
    total = refs[0][...].astype(F32)
    for ref in refs[1:-1]:
        total = total + ref[...].astype(F32)
    refs[-1][...] = total.astype(refs[-1].dtype)


def sum_of(kind, *arrays):
    return small_call(sum_kernel, [(arrays[0].shape, kind)], "sum_arrays", *arrays)[0]


def collect_kernel(start, rows, count_msgs, own, pooled, *refs):
    msgs, out = refs[:count_msgs], refs[-1]
    total = own[start : start + rows]
    for msg in msgs:
        total = total + msg[0:rows].astype(F32)
    out[0:rows] = total.astype(BF)
    if out.shape[0] == rows:
        return
    high, count = pooled.shape
    slab = [pooled[...]] + [msg[rows : rows + high, 0:count] for msg in msgs]
    tall = (out.shape[0] - rows) // high
    for k, piece in enumerate(slab):
        at = rows + k % tall * high
        out[at : at + high, k // tall * count : (k // tall + 1) * count] = piece


def collect(own, pooled, msgs, part, with_pooled, token):
    start, rows = part
    width = own.shape[1]
    more = (len(msgs) + 1) * pooled.size // width if with_pooled else 0
    kernel = functools.partial(collect_kernel, start, rows, len(msgs))
    return small_call(kernel, [((rows + more, width), BF)], "collect_terms", own, pooled, *msgs, tokens=token)[0]


def collect_grads_kernel(start, rows, own, *refs):
    msgs, (out, tails) = refs[:-2], refs[-2:]
    total = own[start : start + rows]
    for msg in msgs:
        total = total + msg[0:rows].astype(F32)
    out[...] = total.astype(BF)
    high = msgs[0].shape[0] - rows
    for k, msg in enumerate(msgs):
        tails[k * high : (k + 1) * high] = msg[rows:]


def collect_grads(own, msgs, part):
    start, rows = part
    width = own.shape[1]
    shapes = [((rows, width), BF), ((len(msgs) * (msgs[0].shape[0] - rows), width), BF)]
    return small_call(functools.partial(collect_grads_kernel, start, rows), shapes, "collect_terms", own, *msgs)


def merge_kernel(rows, mine, other, *refs):
    out = refs[-1]
    out[0:rows] = (mine[0:rows].astype(F32) + other[0:rows].astype(F32)).astype(BF)
    more = mine.shape[0] - rows
    if more:
        out[rows : rows + more] = mine[rows:]
        out[rows + more :] = other[rows:]


def merge(rows, mine, other, *token):
    high, width = mine.shape
    shape = (2 * high - rows, width)
    return small_call(functools.partial(merge_kernel, rows), [(shape, BF)], "merge_slabs", mine, other, tokens=token)[0]


def choose(odd, width):
    return jnp.broadcast_to(odd[0:1, 0:1], (1, width)) > 0.5


def collect_halves_kernel(start, rows, own, pooled, odd, *refs):
    msgs, (keep, send, slab_ref) = [refs[(2, 0, 1).index(i)] for i in range(len(refs) - 3)], refs[-3:]
    width, half = own.shape[1], rows // 2
    total = own[start : start + rows]
    for msg in msgs:
        total = total + msg[0:rows].astype(F32)
    total = total.astype(BF).astype(F32)
    pick = choose(odd, width)
    keep[...] = jnp.where(pick, total[half:], total[:half]).astype(BF)
    send[...] = jnp.where(pick, total[:half], total[half:]).astype(BF)
    high, count = pooled.shape
    slab = [pooled[...]] + [msg[rows : rows + high, 0:count] for msg in msgs]
    tall = slab_ref.shape[0] // high
    for k, piece in enumerate(slab):
        at = k % tall * high
        slab_ref[at : at + high, k // tall * count : (k // tall + 1) * count] = piece


def add_and_append_kernel(rows, count, mine, other, *refs):
    more, out = refs[:count], refs[-1]
    out[0:rows] = (mine[0:rows].astype(F32) + other[0:rows].astype(F32)).astype(BF)
    at = rows
    for ref in more:
        tail = ref[...] if ref.shape[0] < rows else ref[rows:]
        out[at : at + tail.shape[0]] = tail
        at += tail.shape[0]


def sum_by_halves(own, pooled, odd, msgs, part, token, late):
    start, rows = part
    width, half = own.shape[1], rows // 2
    slab_rows = (len(msgs) + 1) * pooled.size // width
    keep, send, slab = small_call(
        functools.partial(collect_halves_kernel, start, rows),
        [((half, width), BF), ((half, width), BF), ((slab_rows, width), BF)],
        "collect_terms",
        *(own, pooled, odd, *[msgs[i] for i in (2, 0, 1)]),
    )
    first = small_call(
        functools.partial(add_and_append_kernel, half, 1),
        [((half + slab_rows, width), BF)],
        "merge_slabs",
        *(keep, swap(send, "dp", 1), slab),
        tokens=token,
    )[0]
    far = swap(first, "dp", 2)
    mine = small_call(
        functools.partial(add_and_append_kernel, half, 2),
        [((half + 2 * slab_rows, width), BF)],
        "merge_slabs",
        *(first, far, first, far),
        tokens=late,
    )[0]
    return mine, swap(mine, "dp", 1)


def final_halves(odd, mine, other, pieces, out):
    tail = pieces[0].shape[0]
    head = out.shape[0] - tail
    half = head // 2
    pick = choose(odd, out.shape[1])
    left, right = mine[0:half].astype(F32), other[0:half].astype(F32)
    out[0:half] = jnp.where(pick, right, left)
    out[half:head] = jnp.where(pick, left, right)
    out[head:] = pieces[0][...].astype(F32) + pieces[1][...].astype(F32)


def final_whole(pieces, out):
    tail = pieces[2].shape[0]
    head = out.shape[0] - tail
    out[0:head] = pieces[0][0:head].astype(F32) + pieces[1][0:head].astype(F32)
    out[head:] = pieces[2][...].astype(F32) + pieces[3][...].astype(F32)


def proj_sum(slabs, images, order, rows, own_ge, mine, other, tails, out):
    count, embed = out.shape
    groups = mine.shape[1] // count
    half = slabs * images // 2
    per = (mine.shape[0] - rows) // (slabs // 2)
    together = per // (2 * images)
    parts = []
    for j in range(slabs):
        pieces = [own_ge[j].astype(BF)]
        start, left = j * images % half, j * images // half * embed
        base = start // 16 * 16
        for k in range(0, tails[0].shape[0], half):
            pair = [t[k + base : k + base + 16, left : left + embed].astype(F32) for t in tails]
            pieces.append(jnp.concatenate([p[start - base : start - base + images] for p in pair], axis=0).astype(BF))
        at = order.index(j)
        ref, at = (mine, at) if at < slabs // 2 else (other, at - slabs // 2)
        total = jnp.zeros((count, embed), F32)
        for g in range(groups):
            pooled = ref[rows + at * per : rows + (at + 1) * per, g * count : (g + 1) * count]
            grads = jnp.concatenate(pieces[g * together : (g + 1) * together], axis=0)
            total = total + dot(pooled, grads, TN)
        parts.append(total)
    while len(parts) > 1:
        parts = [parts[k] + parts[k + 1] for k in range(0, len(parts), 2)]
    out[...] = parts[0]


def gate_kernel(x, token, out):
    out[...] = x[...]


def after(x, token):
    return small_call(gate_kernel, [(x.shape, x.dtype)], "gate", x, tokens=(token,))[0]


def part_kernel(start, x, token, out):
    out[...] = x[start : start + out.shape[0]]


def half_of(start, x, token):
    shape = (x.shape[0] // 2, x.shape[1])
    return small_call(functools.partial(part_kernel, start), [(shape, x.dtype)], "half_of", x, tokens=(token,))[0]


def last_sums_kernel(slabs, images, order, rows, own_ge, odd, last_mine, last_other, mine, other, *refs):
    tails, (conv_out, proj_out) = refs[:-2], refs[-2:]
    proj_sum(slabs, images, order, rows, own_ge, mine, other, tails, proj_out)
    if slabs == 4:
        final_halves(odd, mine, other, (last_mine, last_other), conv_out)
    else:
        final_whole((mine, other, last_mine, last_other), conv_out)


def swap(x, axis, bit):
    size = lax.axis_size(axis)
    return lax.ppermute(x, axis, [(i, i ^ bit) for i in range(size)])


def gather_slabs(x, slabs):
    if slabs <= 4:
        return [x] + [swap(x, "dp", j) for j in range(1, slabs)]
    whole = lax.all_gather(x, "dp", axis=0, tiled=False)
    return [jnp.take(whole, lax.axis_index("dp") ^ jnp.arange(slabs), axis=0)]


def local(features, shortcut, conv_weight, proj_weight, partner):
    slabs, groups = lax.axis_size("dp"), lax.axis_size("fsdp")
    peers = groups // 2
    images = features.shape[0] // POS
    count, width = conv_weight.shape
    place = lax.axis_index("dp").astype(jnp.int32).reshape(1)
    index = lax.axis_index("fsdp").astype(jnp.int32).reshape(1)

    f_sib = swap(features, "fsdp", 1)
    s_sib = swap(shortcut, "fsdp", 1)
    shorts = (shortcut, s_sib)
    first, embed, f_own, proj_own, member = forward_first(
        index, partner, (features, f_sib), shorts, conv_weight, proj_weight, images
    )
    feats = (f_own, f_sib)
    projs = [swap(proj_weight, "fsdp", 2 * j) for j in range(1, peers)]
    if peers == 4:
        conv_y = swap(conv_weight, "fsdp", 4)
        conv_x = swap(conv_weight, "fsdp", 2)
        halves = [
            swap(half_of(0, conv_y, embed), "fsdp", 2),
            swap(half_of(count // 2, conv_x, embed), "fsdp", 4),
        ]
        convs = [conv_x, conv_y, halves]
    else:
        convs = [swap(conv_weight, "fsdp", 2 * j) for j in range(1, peers)]
        convs[-1] = [convs[-1]]
    middle, embed, ahead = forward_middle(index, feats, shorts, convs[:-1], projs[:-1], images, embed)
    last, mine, send = forward_last(feats, ahead, convs[-1], projs[-1], images, embed, member)
    blocks, projs = [first, *middle, last], [proj_own, *projs]
    blocks = [(*b, p) for b, p in zip(blocks, projs)]
    embeds = sum_of(F32, mine, swap(send, "fsdp", 1))
    ge, loss, odd = hsic(place, gather_slabs(embeds, slabs), proj_weight.shape[1], slabs, images, groups)

    first_rows = count * SPLIT // 8
    parts = [(0, first_rows), (first_rows, count - first_rows)]
    terms, done = [], ()
    for part, extra in zip(parts, ("pooled", "embed")):
        done = tuple(backward(feats, ge, blocks[1:], images, part, extra, done))
        terms.append(done)
    (own,) = backward(feats, ge, blocks[:1], images, (0, count), None, done)

    received = [[swap(m, "fsdp", 2 * j) for j, m in enumerate(term, 1)] for term in terms]
    total, tails = collect_grads(own, received[1], parts[1])
    if slabs == 4:
        merged = merge(parts[1][1], total, swap(total, "dp", 1))
        mine, other = sum_by_halves(own, blocks[0][2], odd, received[0], parts[0], (total,), (merged,))
        pieces = [mine, other, merged, swap(merged, "dp", 2)]
        order, above = [0, 2, 1, 3], parts[0][1] // 2
    else:
        pieces, order, above = [], list(range(slabs)), parts[0][1]
        for piece, part in zip((collect(own, blocks[0][2], received[0], parts[0], True, ()), total), parts):
            bit = 1
            while 2 * bit < slabs:
                piece = merge(part[1], piece, swap(piece, "dp", bit))
                bit *= 2
            pieces += [piece, swap(piece, "dp", bit)]
    grad_conv, grad_proj = small_call(
        functools.partial(last_sums_kernel, slabs, images, order, above),
        [((count, width), F32), (proj_weight.shape, F32)],
        "last_sums",
        *(ge, odd, pieces[2], pieces[3], pieces[0], pieces[1], tails, swap(tails, "fsdp", 1)),
    )
    return grad_conv, grad_proj, loss.reshape(1)


def solution(mesh):
    return jax.shard_map(
        local,
        mesh=mesh,
        in_specs=(
            P(("dp", "fsdp"), None),
            P(("dp", "fsdp"), None),
            P("fsdp", None),
            P("fsdp", None),
            P(("dp", "fsdp")),
        ),
        out_specs=(P("fsdp", None), P("fsdp", None), P("fsdp")),
        check_vma=False,
    )
```

```python
import functools

import jax
import jax.numpy as jnp
from jax import lax
from jax.experimental import pallas as pl
from jax.experimental.pallas import tpu as pltpu
from jax.sharding import PartitionSpec as P

POS = 49
GAMMA = 3.0
EPSILON = 1e-06
BF = jnp.bfloat16
F32 = jnp.float32
NT = (((1,), (1,)), ((), ()))
TN = (((0,), (0,)), ((), ()))
VMEM_LIMIT = 8 * 1024 * 1024
SPLIT = 4
ORDER = (0, 2, 3, 1)


def dot(a, b, dims=(((1,), (0,)), ((), ()))):
    return lax.dot_general(a, b, dims, preferred_element_type=F32)


def vspec():
    return pl.BlockSpec(memory_space=pltpu.VMEM)


def params(more=0):
    return pltpu.CompilerParams(vmem_limit_bytes=VMEM_LIMIT + more)


def tile_iota(width):
    return lax.broadcasted_iota(jnp.int32, (8, width), 0)


def pool_rows(hidden, images):
    width = hidden.shape[1]
    row = tile_iota(width)
    pooled = jnp.zeros((images, width), F32)
    for i in range(images):
        first, last = i * POS, i * POS + POS - 1
        total = jnp.zeros((8, width), F32)
        for t in range(first // 8, last // 8 + 1):
            tile = hidden[8 * t : 8 * t + 8]
            if 8 * t < first:
                tile = jnp.where(row >= first - 8 * t, tile, 0.0)
            if 8 * t + 7 > last:
                tile = jnp.where(row <= last - 8 * t, tile, 0.0)
            total = total + tile
        pooled = jnp.where(row == i, jnp.sum(total, axis=0, keepdims=True) / POS, pooled)
    return pooled


def spread_rows(values, images):
    width = values.shape[1]
    row = tile_iota(width)
    whole = [jnp.broadcast_to(values[i : i + 1], (8, width)) for i in range(images)]
    tiles = []
    for t in range(images * POS // 8):
        low, high = 8 * t // POS, (8 * t + 7) // POS
        tiles.append(whole[low] if low == high else jnp.where(row < high * POS - 8 * t, whole[low], whole[high]))
    return jnp.concatenate(tiles, axis=0)


def forward_block(feat, short, convs, images):
    preact = [dot(feat, conv[...], NT) for conv in convs]
    preact = preact[0] if len(preact) == 1 else jnp.concatenate(preact, axis=1)
    hidden = jnp.maximum(preact + short.astype(F32), 0.0)
    mask = jnp.where(hidden > 0, 1.0, 0.0).astype(BF)
    return mask, pool_rows(hidden, images)


def forward_blocks(picks, feats, shorts, convs, projs, embed, outs, ready=None):
    images = outs[2].shape[0] // 2
    for j in range(picks):
        pooled = [None, None]
        for side in (1, 0):
            if ready is not None:
                ready(j, side)
            mask, pooled[side] = forward_block(feats[side][...], shorts[2 * j + side][...], convs[j], images)
            outs[3 * j + side][...] = mask
        pooled = jnp.concatenate(pooled, axis=0).astype(BF)
        outs[3 * j + 2][...] = pooled
        embed = embed + dot(pooled, projs[j][...])
    return embed


def fetcher(sems):
    copies = []

    def fetch(source, target):
        copies.append(pltpu.make_async_copy(source, target, sems.at[len(copies)]))
        copies[-1].start()
        return copies[-1]

    return fetch


def columns(index_ref, pick, count):
    return pl.ds(pl.multiple_of((index_ref[0] ^ (2 * pick)) * count, count), count)


def first_kernel(images, index_ref, f_sib, partner_ref, f_own, s_own, s_sib, conv, proj, *refs):
    blocks, embed_ref, feat, proj_out, member_ref = refs[:3], refs[3], refs[4], refs[5], refs[6]
    short, conv_buf, partner, sems = refs[7:]
    fetch = fetcher(sems)
    at = columns(index_ref, 0, conv_buf.shape[0])
    shorts = [short.at[0], short.at[1]]
    waits = [
        [fetch(conv, conv_buf), fetch(s_sib.at[:, at], shorts[1])],
        [fetch(f_own, feat), fetch(s_own.at[:, at], shorts[0]), fetch(proj, proj_out)],
    ]
    partner_copy = fetch(partner_ref, partner)

    def ready(j, side):
        for copy in waits[1 - side]:
            copy.wait()

    embed = jnp.zeros(embed_ref.shape, F32)
    embed_ref[...] = forward_blocks(1, (feat, f_sib), shorts, [[conv_buf]], [proj_out], embed, blocks, ready)
    partner_copy.wait()
    member = lax.broadcasted_iota(jnp.int32, member_ref.shape, 0)
    whole = jnp.zeros(member_ref.shape, F32)
    for i in range(images):
        whole = jnp.where(member == i, partner[i].astype(F32), whole)
    member_ref[...] = whole


def middle_kernel(blocks, index_ref, f_own, f_sib, before, s_own, s_sib, *refs):
    convs, projs, refs = refs[:blocks], refs[blocks : 2 * blocks], refs[2 * blocks :]
    *outs, embed_ref, ahead_own, ahead_sib, short, sems = refs
    fetch = fetcher(sems)
    targets = [short.at[k] for k in range(2 * blocks)] + [ahead_own, ahead_sib]
    copies = [None] * len(targets)
    for j in range(blocks + 1):
        at = columns(index_ref, j + 1, short.shape[2])
        for side in (1, 0):
            copies[2 * j + side] = fetch((s_own, s_sib)[side].at[:, at], targets[2 * j + side])

    def ready(j, side):
        copies[2 * j + side].wait()

    feats, weights = (f_own, f_sib), [[c] for c in convs]
    embed_ref[...] = forward_blocks(blocks, feats, targets, weights, projs, before[...], outs, ready)
    ready(blocks, 1)
    ready(blocks, 0)


def last_kernel(images, f_own, f_sib, before, member, s_own, s_sib, proj, *refs):
    convs, outs = refs[:-5], refs[-5:]
    embed = forward_blocks(1, (f_own, f_sib), (s_own, s_sib), [convs], [proj], before[...], outs)
    mine_ref, send_ref = outs[-2:]
    lanes = member.shape[1]
    tiles = embed.shape[1] // lanes
    for g in (0, 1):
        for t in range(tiles):
            piece = embed[g * images : (g + 1) * images, t * lanes : (t + 1) * lanes]
            at = (g * tiles + t) * images
            mine_ref[at : at + images] = piece
            at = ((1 - g) * tiles + t) * images
            send_ref[at : at + images] = piece
    low = lax.broadcasted_iota(jnp.int32, (images, lanes), 1) < lanes // 2
    mine_ref[2 * tiles * images :] = jnp.where(low, member[...], 0.0)
    send_ref[2 * tiles * images :] = jnp.where(low, 0.0, member[...])


def forward_call(kernel, in_specs, shapes, scratch, busy, name, *arrays):
    rows, width, count = busy
    return pl.pallas_call(
        kernel,
        in_specs=in_specs,
        out_specs=[vspec()] * len(shapes),
        out_shape=[jax.ShapeDtypeStruct(shape, kind) for shape, kind in shapes],
        scratch_shapes=scratch,
        compiler_params=params(),
        cost_estimate=pl.CostEstimate(
            flops=16 * rows * width * count, bytes_accessed=8 * rows * count, transcendentals=0
        ),
        name=name,
    )(*arrays)


def block_shapes(rows, count, images):
    return [((rows, count), BF), ((rows, count), BF), ((2 * images, count), BF)]


def from_hbm(x):
    return pltpu.with_memory_space_constraint(x, pltpu.HBM)


def forward_first(index, partner, feats, shorts, conv, proj, images):
    rows, width = feats[0].shape
    count, embed = proj.shape
    shapes = block_shapes(rows, count, images)
    shapes += [((2 * images, embed), F32), ((rows, width), BF), ((count, embed), BF), ((images, 128), F32)]
    outs = forward_call(
        functools.partial(first_kernel, images),
        [pl.BlockSpec(memory_space=pltpu.SMEM)] + [vspec()] + [pl.BlockSpec(memory_space=pl.ANY)] * 6,
        shapes,
        [
            pltpu.VMEM((2, rows, count), BF),
            pltpu.VMEM((count, width), BF),
            pltpu.SMEM((images,), jnp.int32),
            pltpu.SemaphoreType.DMA((6,)),
        ],
        (rows, width, count),
        "forward_first",
        *(index, feats[1], from_hbm(partner), from_hbm(feats[0]), from_hbm(shorts[0]), from_hbm(shorts[1])),
        *(from_hbm(conv), from_hbm(proj)),
    )
    return outs[:3], outs[3], outs[4], outs[5], outs[6]


def forward_middle(index, feats, shorts, convs, projs, images, before):
    rows, width = feats[0].shape
    count, blocks = convs[0].shape[0], len(convs)
    outs = forward_call(
        functools.partial(middle_kernel, blocks),
        [pl.BlockSpec(memory_space=pltpu.SMEM)]
        + [vspec()] * 3
        + [pl.BlockSpec(memory_space=pl.ANY)] * 2
        + [vspec()] * (2 * blocks),
        block_shapes(rows, count, images) * blocks + [(before.shape, F32)] + [((rows, count), BF)] * 2,
        [pltpu.VMEM((2 * blocks, rows, count), BF), pltpu.SemaphoreType.DMA((2 * blocks + 2,))],
        (rows, width, blocks * count),
        "forward_middle",
        *(index, *feats, before, from_hbm(shorts[0]), from_hbm(shorts[1]), *convs, *projs),
    )
    return [outs[3 * j : 3 * j + 3] for j in range(blocks)], outs[-3], outs[-2:]


def forward_last(feats, shorts, convs, proj, images, before, member):
    rows, width = feats[0].shape
    count, embed = proj.shape
    arrays = (*feats, before, member, *shorts, proj, *convs)
    outs = forward_call(
        functools.partial(last_kernel, images),
        [vspec()] * len(arrays),
        block_shapes(rows, count, images) + [(((2 * embed // 128 + 1) * images, 128), F32)] * 2,
        [],
        (rows, width, count),
        "forward_last",
        *arrays,
    )
    return outs[:3], outs[3], outs[4]


def group_terms(z, inner, partner, groups):
    count = z.shape[0]
    squares = jnp.sum(z * z, axis=1, keepdims=True)
    spread = 2.0 * jnp.mean(squares)
    row = lax.broadcasted_iota(jnp.int32, (count, count), 0)
    col = lax.broadcasted_iota(jnp.int32, (count, count), 1)
    across = jnp.sum(jnp.where(row == col, squares, 0.0), axis=0, keepdims=True)
    kernel = jnp.exp(-(squares + across - 2.0 * inner) / (2.0 * spread))
    r_col = jnp.mean(kernel, axis=1, keepdims=True)
    r_row = jnp.mean(kernel, axis=0, keepdims=True)
    t = jnp.mean(r_col)
    centered = kernel - r_col - r_row + t
    scale_sq = float(count - 1) ** 2
    root = jnp.sqrt(jnp.sum(centered * centered, keepdims=True) / scale_sq + EPSILON)
    onehot = jnp.where(partner == col.astype(F32), 1.0, 0.0)
    positive = jnp.sum(kernel * onehot, keepdims=True) / count
    loss = -(positive - t) + GAMMA * root
    coeff = (-onehot / count + 1.0 / (count * count) + GAMMA * centered / (scale_sq * root)) / groups
    weighted = coeff * kernel
    moved = lax.dot_general(
        weighted, z, (((1,), (0,)), ((), ())), precision=lax.Precision.HIGHEST, preferred_element_type=F32
    )
    return loss, -(2.0 / spread) * (jnp.sum(weighted, axis=1, keepdims=True) * z - moved)


def hsic_kernel(slabs, images, groups, place_ref, *refs):
    chunks = refs[:-6]
    ge_ref, loss_ref, odd_ref, z_ref, p_ref, g_ref = refs[-6:]
    place = place_ref[0]
    odd_ref[...] = jnp.full(odd_ref.shape, (place & 1).astype(F32))
    tiles = z_ref.shape[2] // 128
    for j in range(slabs):
        block = chunks[0].at[j] if len(chunks) == 1 else chunks[ORDER.index(j)]
        at = pl.ds(pl.multiple_of((place ^ j) * images, images), images)
        for g in (0, 1):
            for t in range(tiles):
                row = (g * tiles + t) * images
                z_ref[g, at, t * 128 : (t + 1) * 128] = block[row : row + images]
        p_ref[at] = block[2 * tiles * images :]
    high_lane = lax.broadcasted_iota(jnp.int32, p_ref.shape, 1) >= 64
    count = slabs * images
    both = [z_ref[g] - jnp.mean(z_ref[g], axis=0, keepdims=True) for g in (0, 1)]
    pair = jnp.concatenate(both, axis=0)
    inner = lax.dot_general(pair, pair, NT, precision=lax.Precision.HIGHEST, preferred_element_type=F32)
    for g in (0, 1):
        part = inner[g * count : (g + 1) * count, g * count : (g + 1) * count]
        partner = jnp.max(jnp.where(high_lane == (g == 1), p_ref[...], -1.0), axis=1, keepdims=True)
        loss, grad = group_terms(both[g], part, partner, groups)
        if g == 0:
            loss_ref[...] = loss
        g_ref[g] = grad
    for j in range(slabs):
        at = pl.ds(pl.multiple_of((place ^ j) * images, images), images)
        for g in (0, 1):
            ge_ref[j, g * images : (g + 1) * images] = g_ref[g, at]


def hsic(place, chunks, embed, slabs, images, groups):
    return pl.pallas_call(
        functools.partial(hsic_kernel, slabs, images, groups),
        in_specs=[pl.BlockSpec(memory_space=pltpu.SMEM)] + [vspec()] * len(chunks),
        out_specs=[vspec()] * 3,
        out_shape=[
            jax.ShapeDtypeStruct((slabs, 2 * images, embed), F32),
            jax.ShapeDtypeStruct((1, 1), F32),
            jax.ShapeDtypeStruct((8, 128), F32),
        ],
        scratch_shapes=[
            pltpu.VMEM((2, slabs * images, embed), F32),
            pltpu.VMEM((slabs * images, 128), F32),
            pltpu.VMEM((2, slabs * images, embed), F32),
        ],
        compiler_params=params(80 * (slabs * images) ** 2),
        cost_estimate=pl.CostEstimate(flops=10**9, bytes_accessed=0, transcendentals=0),
        name="hsic_groups",
    )(place, *([chunks[j] for j in ORDER] if len(chunks) > 1 else chunks))


def backward_kernel(blocks, images, part, extra, after, f_own, f_sib, ge_ref, *refs):
    ins, outs = refs[: 4 * blocks], refs[4 * blocks + after :]
    mine = ge_ref[0].astype(BF)
    start, rows = part
    width = f_own.shape[1]
    grad_pool = [dot(mine, ins[4 * j + 3][start : start + rows], NT) / POS for j in range(blocks)]
    total = jnp.zeros((blocks * rows, width), F32)
    for side, feat in enumerate((f_own, f_sib)):
        grad_hidden = []
        for j in range(blocks):
            spread = spread_rows(grad_pool[j][side * images : (side + 1) * images], images)
            grad_hidden.append(spread.astype(BF) * ins[4 * j + side][:, start : start + rows])
        total = total + dot(jnp.concatenate(grad_hidden, axis=1), feat[...], TN)
    for j in range(blocks):
        out, pooled = outs[j], ins[4 * j + 2]
        out[0:rows] = total[j * rows : (j + 1) * rows].astype(out.dtype)
        if extra == "pooled":
            rest = jnp.zeros((2 * images, width - pooled.shape[1]), BF)
            out[rows:] = jnp.concatenate([pooled[...], rest], axis=1)
        if extra == "embed":
            half = ge_ref.shape[0] * images // 2
            flat = ge_ref[:, :images].reshape(2 * half, ge_ref.shape[2]).astype(BF)
            out[rows:] = jnp.concatenate([flat[:half], flat[half:]], axis=1)


def backward(feats, ge, blocks, images, part, extra=None, after=()):
    length, width = feats[0].shape
    rows = part[1]
    high = rows + {None: 0, "pooled": 2 * images, "embed": ge.shape[0] * images // 2}[extra]
    return pl.pallas_call(
        functools.partial(backward_kernel, len(blocks), images, part, extra, len(after)),
        in_specs=[vspec()] * (3 + 4 * len(blocks)) + [pl.BlockSpec(memory_space=pl.ANY)] * len(after),
        out_specs=[vspec()] * len(blocks),
        out_shape=[jax.ShapeDtypeStruct((high, width), BF if extra else F32)] * len(blocks),
        compiler_params=params(),
        cost_estimate=pl.CostEstimate(
            flops=16 * len(blocks) * length * width * rows,
            bytes_accessed=4 * len(blocks) * length * rows,
            transcendentals=0,
        ),
        name="backward_blocks",
    )(*feats, ge, *[a for block in blocks for a in block], *after)


def small_call(kernel, shapes, name, *arrays, tokens=()):
    return pl.pallas_call(
        kernel,
        in_specs=[vspec()] * len(arrays) + [pl.BlockSpec(memory_space=pl.ANY)] * len(tokens),
        out_specs=[vspec()] * len(shapes),
        out_shape=[jax.ShapeDtypeStruct(shape, kind) for shape, kind in shapes],
        compiler_params=params(),
        cost_estimate=pl.CostEstimate(flops=0, bytes_accessed=0, transcendentals=0),
        name=name,
    )(*arrays, *tokens)


def sum_kernel(*refs):
    total = refs[0][...].astype(F32)
    for ref in refs[1:-1]:
        total = total + ref[...].astype(F32)
    refs[-1][...] = total.astype(refs[-1].dtype)


def sum_of(kind, *arrays):
    return small_call(sum_kernel, [(arrays[0].shape, kind)], "sum_arrays", *arrays)[0]


def collect_kernel(start, rows, count_msgs, own, pooled, *refs):
    msgs, out = refs[:count_msgs], refs[-1]
    total = own[start : start + rows]
    for msg in msgs:
        total = total + msg[0:rows].astype(F32)
    out[0:rows] = total.astype(BF)
    if out.shape[0] == rows:
        return
    high, count = pooled.shape
    slab = [pooled[...]] + [msg[rows : rows + high, 0:count] for msg in msgs]
    tall = (out.shape[0] - rows) // high
    for k, piece in enumerate(slab):
        at = rows + k % tall * high
        out[at : at + high, k // tall * count : (k // tall + 1) * count] = piece


def collect(own, pooled, msgs, part, with_pooled, token):
    start, rows = part
    width = own.shape[1]
    more = (len(msgs) + 1) * pooled.size // width if with_pooled else 0
    kernel = functools.partial(collect_kernel, start, rows, len(msgs))
    return small_call(kernel, [((rows + more, width), BF)], "collect_terms", own, pooled, *msgs, tokens=token)[0]


def collect_grads_kernel(start, rows, own, *refs):
    msgs, (out, tails) = refs[:-2], refs[-2:]
    total = own[start : start + rows]
    for msg in msgs:
        total = total + msg[0:rows].astype(F32)
    out[...] = total.astype(BF)
    high = msgs[0].shape[0] - rows
    for k, msg in enumerate(msgs):
        tails[k * high : (k + 1) * high] = msg[rows:]


def collect_grads(own, msgs, part):
    start, rows = part
    width = own.shape[1]
    shapes = [((rows, width), BF), ((len(msgs) * (msgs[0].shape[0] - rows), width), BF)]
    return small_call(functools.partial(collect_grads_kernel, start, rows), shapes, "collect_terms", own, *msgs)


def merge_kernel(rows, mine, other, *refs):
    out = refs[-1]
    out[0:rows] = (mine[0:rows].astype(F32) + other[0:rows].astype(F32)).astype(BF)
    more = mine.shape[0] - rows
    if more:
        out[rows : rows + more] = mine[rows:]
        out[rows + more :] = other[rows:]


def merge(rows, mine, other, *token):
    high, width = mine.shape
    shape = (2 * high - rows, width)
    return small_call(functools.partial(merge_kernel, rows), [(shape, BF)], "merge_slabs", mine, other, tokens=token)[0]


def choose(odd, width):
    return jnp.broadcast_to(odd[0:1, 0:1], (1, width)) > 0.5


def collect_halves_kernel(start, rows, own, pooled, odd, *refs):
    msgs, (keep, send, slab_ref) = [refs[(2, 0, 1).index(i)] for i in range(len(refs) - 3)], refs[-3:]
    width, half = own.shape[1], rows // 2
    total = own[start : start + rows]
    for msg in msgs:
        total = total + msg[0:rows].astype(F32)
    total = total.astype(BF).astype(F32)
    pick = choose(odd, width)
    keep[...] = jnp.where(pick, total[half:], total[:half]).astype(BF)
    send[...] = jnp.where(pick, total[:half], total[half:]).astype(BF)
    high, count = pooled.shape
    slab = [pooled[...]] + [msg[rows : rows + high, 0:count] for msg in msgs]
    tall = slab_ref.shape[0] // high
    for k, piece in enumerate(slab):
        at = k % tall * high
        slab_ref[at : at + high, k // tall * count : (k // tall + 1) * count] = piece


def add_and_append_kernel(rows, count, mine, other, *refs):
    more, out = refs[:count], refs[-1]
    out[0:rows] = (mine[0:rows].astype(F32) + other[0:rows].astype(F32)).astype(BF)
    at = rows
    for ref in more:
        tail = ref[...] if ref.shape[0] < rows else ref[rows:]
        out[at : at + tail.shape[0]] = tail
        at += tail.shape[0]


def sum_by_halves(own, pooled, odd, msgs, part, token, late):
    start, rows = part
    width, half = own.shape[1], rows // 2
    slab_rows = (len(msgs) + 1) * pooled.size // width
    keep, send, slab = small_call(
        functools.partial(collect_halves_kernel, start, rows),
        [((half, width), BF), ((half, width), BF), ((slab_rows, width), BF)],
        "collect_terms",
        *(own, pooled, odd, *[msgs[i] for i in (2, 0, 1)]),
    )
    first = small_call(
        functools.partial(add_and_append_kernel, half, 1),
        [((half + slab_rows, width), BF)],
        "merge_slabs",
        *(keep, swap(send, "dp", 1), slab),
        tokens=token,
    )[0]
    far = swap(first, "dp", 2)
    mine = small_call(
        functools.partial(add_and_append_kernel, half, 2),
        [((half + 2 * slab_rows, width), BF)],
        "merge_slabs",
        *(first, far, first, far),
        tokens=late,
    )[0]
    return mine, swap(mine, "dp", 1)


def final_halves(odd, mine, other, pieces, out):
    tail = pieces[0].shape[0]
    head = out.shape[0] - tail
    half = head // 2
    pick = choose(odd, out.shape[1])
    left, right = mine[0:half].astype(F32), other[0:half].astype(F32)
    out[0:half] = jnp.where(pick, right, left)
    out[half:head] = jnp.where(pick, left, right)
    out[head:] = pieces[0][...].astype(F32) + pieces[1][...].astype(F32)


def final_whole(pieces, out):
    tail = pieces[2].shape[0]
    head = out.shape[0] - tail
    out[0:head] = pieces[0][0:head].astype(F32) + pieces[1][0:head].astype(F32)
    out[head:] = pieces[2][...].astype(F32) + pieces[3][...].astype(F32)


def proj_sum(slabs, images, order, rows, own_ge, mine, other, tails, out):
    count, embed = out.shape
    groups = mine.shape[1] // count
    half = slabs * images // 2
    per = (mine.shape[0] - rows) // (slabs // 2)
    together = per // (2 * images)
    parts = []
    for j in range(slabs):
        pieces = [own_ge[j].astype(BF)]
        start, left = j * images % half, j * images // half * embed
        base = start // 16 * 16
        for k in range(0, tails[0].shape[0], half):
            pair = [t[k + base : k + base + 16, left : left + embed].astype(F32) for t in tails]
            pieces.append(jnp.concatenate([p[start - base : start - base + images] for p in pair], axis=0).astype(BF))
        at = order.index(j)
        ref, at = (mine, at) if at < slabs // 2 else (other, at - slabs // 2)
        total = jnp.zeros((count, embed), F32)
        for g in range(groups):
            pooled = ref[rows + at * per : rows + (at + 1) * per, g * count : (g + 1) * count]
            grads = jnp.concatenate(pieces[g * together : (g + 1) * together], axis=0)
            total = total + dot(pooled, grads, TN)
        parts.append(total)
    while len(parts) > 1:
        parts = [parts[k] + parts[k + 1] for k in range(0, len(parts), 2)]
    out[...] = parts[0]


def gate_kernel(x, token, out):
    out[...] = x[...]


def after(x, token):
    return small_call(gate_kernel, [(x.shape, x.dtype)], "gate", x, tokens=(token,))[0]


def part_kernel(start, x, token, out):
    out[...] = x[start : start + out.shape[0]]


def half_of(start, x, token):
    shape = (x.shape[0] // 2, x.shape[1])
    return small_call(functools.partial(part_kernel, start), [(shape, x.dtype)], "half_of", x, tokens=(token,))[0]


def last_sums_kernel(slabs, images, order, rows, own_ge, odd, last_mine, last_other, mine, other, *refs):
    tails, (conv_out, proj_out) = refs[:-2], refs[-2:]
    proj_sum(slabs, images, order, rows, own_ge, mine, other, tails, proj_out)
    if slabs == 4:
        final_halves(odd, mine, other, (last_mine, last_other), conv_out)
    else:
        final_whole((mine, other, last_mine, last_other), conv_out)


def swap(x, axis, bit):
    size = lax.axis_size(axis)
    return lax.ppermute(x, axis, [(i, i ^ bit) for i in range(size)])


def gather_slabs(x, slabs):
    if slabs <= 4:
        return [x] + [swap(x, "dp", j) for j in range(1, slabs)]
    whole = lax.all_gather(x, "dp", axis=0, tiled=False)
    return [jnp.take(whole, lax.axis_index("dp") ^ jnp.arange(slabs), axis=0)]


def local(features, shortcut, conv_weight, proj_weight, partner):
    slabs, groups = lax.axis_size("dp"), lax.axis_size("fsdp")
    peers = groups // 2
    images = features.shape[0] // POS
    count, width = conv_weight.shape
    place = lax.axis_index("dp").astype(jnp.int32).reshape(1)
    index = lax.axis_index("fsdp").astype(jnp.int32).reshape(1)

    f_sib = swap(features, "fsdp", 1)
    s_sib = swap(shortcut, "fsdp", 1)
    shorts = (shortcut, s_sib)
    first, embed, f_own, proj_own, member = forward_first(
        index, partner, (features, f_sib), shorts, conv_weight, proj_weight, images
    )
    feats = (f_own, f_sib)
    projs = [swap(proj_weight, "fsdp", 2 * j) for j in range(1, peers)]
    if peers == 4:
        conv_y = swap(conv_weight, "fsdp", 4)
        conv_x = swap(conv_weight, "fsdp", 2)
        halves = [
            swap(half_of(0, conv_y, embed), "fsdp", 2),
            swap(half_of(count // 2, conv_x, embed), "fsdp", 4),
        ]
        convs = [conv_x, conv_y, halves]
    else:
        convs = [swap(conv_weight, "fsdp", 2 * j) for j in range(1, peers)]
        convs[-1] = [convs[-1]]
    middle, embed, ahead = forward_middle(index, feats, shorts, convs[:-1], projs[:-1], images, embed)
    last, mine, send = forward_last(feats, ahead, convs[-1], projs[-1], images, embed, member)
    blocks, projs = [first, *middle, last], [proj_own, *projs]
    blocks = [(*b, p) for b, p in zip(blocks, projs)]
    embeds = sum_of(F32, mine, swap(send, "fsdp", 1))
    ge, loss, odd = hsic(place, gather_slabs(embeds, slabs), proj_weight.shape[1], slabs, images, groups)

    first_rows = count * SPLIT // 8
    parts = [(0, first_rows), (first_rows, count - first_rows)]
    terms, done = [], ()
    for part, extra in zip(parts, ("pooled", "embed")):
        done = tuple(backward(feats, ge, blocks[1:], images, part, extra, done))
        terms.append(done)
    (own,) = backward(feats, ge, blocks[:1], images, (0, count), None, done)

    received = [[swap(m, "fsdp", 2 * j) for j, m in enumerate(term, 1)] for term in terms]
    total, tails = collect_grads(own, received[1], parts[1])
    if slabs == 4:
        merged = merge(parts[1][1], total, swap(total, "dp", 1))
        mine, other = sum_by_halves(own, blocks[0][2], odd, received[0], parts[0], (total,), (merged,))
        pieces = [mine, other, merged, swap(merged, "dp", 2)]
        order, above = [0, 2, 1, 3], parts[0][1] // 2
    else:
        pieces, order, above = [], list(range(slabs)), parts[0][1]
        for piece, part in zip((collect(own, blocks[0][2], received[0], parts[0], True, ()), total), parts):
            bit = 1
            while 2 * bit < slabs:
                piece = merge(part[1], piece, swap(piece, "dp", bit))
                bit *= 2
            pieces += [piece, swap(piece, "dp", bit)]
    grad_conv, grad_proj = small_call(
        functools.partial(last_sums_kernel, slabs, images, order, above),
        [((count, width), F32), (proj_weight.shape, F32)],
        "last_sums",
        *(ge, odd, pieces[2], pieces[3], pieces[0], pieces[1], tails, swap(tails, "fsdp", 1)),
    )
    return grad_conv, grad_proj, loss.reshape(1)


def solution(mesh):
    return jax.shard_map(
        local,
        mesh=mesh,
        in_specs=(
            P(("dp", "fsdp"), None),
            P(("dp", "fsdp"), None),
            P("fsdp", None),
            P("fsdp", None),
            P(("dp", "fsdp")),
        ),
        out_specs=(P("fsdp", None), P("fsdp", None), P("fsdp")),
        check_vma=False,
    )
```

```python
import functools

import jax
import jax.numpy as jnp
from jax import lax
from jax.experimental import pallas as pl
from jax.experimental.pallas import tpu as pltpu
from jax.sharding import PartitionSpec as P

POS = 49
GAMMA = 3.0
EPSILON = 1e-06
BF = jnp.bfloat16
F32 = jnp.float32
NT = (((1,), (1,)), ((), ()))
TN = (((0,), (0,)), ((), ()))
VMEM_LIMIT = 8 * 1024 * 1024
SPLIT = 4
ORDER = (0, 2, 3, 1)


def dot(a, b, dims=(((1,), (0,)), ((), ()))):
    return lax.dot_general(a, b, dims, preferred_element_type=F32)


def vspec():
    return pl.BlockSpec(memory_space=pltpu.VMEM)


def params(more=0):
    return pltpu.CompilerParams(vmem_limit_bytes=VMEM_LIMIT + more)


def tile_iota(width):
    return lax.broadcasted_iota(jnp.int32, (8, width), 0)


def pool_rows(hidden, images):
    width = hidden.shape[1]
    row = tile_iota(width)
    pooled = jnp.zeros((images, width), F32)
    for i in range(images):
        first, last = i * POS, i * POS + POS - 1
        total = jnp.zeros((8, width), F32)
        for t in range(first // 8, last // 8 + 1):
            tile = hidden[8 * t : 8 * t + 8]
            if 8 * t < first:
                tile = jnp.where(row >= first - 8 * t, tile, 0.0)
            if 8 * t + 7 > last:
                tile = jnp.where(row <= last - 8 * t, tile, 0.0)
            total = total + tile
        pooled = jnp.where(row == i, jnp.sum(total, axis=0, keepdims=True) / POS, pooled)
    return pooled


def spread_rows(values, images):
    width = values.shape[1]
    row = tile_iota(width)
    whole = [jnp.broadcast_to(values[i : i + 1], (8, width)) for i in range(images)]
    tiles = []
    for t in range(images * POS // 8):
        low, high = 8 * t // POS, (8 * t + 7) // POS
        tiles.append(whole[low] if low == high else jnp.where(row < high * POS - 8 * t, whole[low], whole[high]))
    return jnp.concatenate(tiles, axis=0)


def forward_block(feat, short, convs, images):
    preact = [dot(feat, conv[...], NT) for conv in convs]
    preact = preact[0] if len(preact) == 1 else jnp.concatenate(preact, axis=1)
    hidden = jnp.maximum(preact + short.astype(F32), 0.0)
    mask = jnp.where(hidden > 0, 1.0, 0.0).astype(BF)
    return mask, pool_rows(hidden, images)


def forward_blocks(picks, feats, shorts, convs, projs, embed, outs, ready=None):
    images = outs[2].shape[0] // 2
    for j in range(picks):
        pooled = [None, None]
        for side in (1, 0):
            if ready is not None:
                ready(j, side)
            mask, pooled[side] = forward_block(feats[side][...], shorts[2 * j + side][...], convs[j], images)
            outs[3 * j + side][...] = mask
        pooled = jnp.concatenate(pooled, axis=0).astype(BF)
        outs[3 * j + 2][...] = pooled
        embed = embed + dot(pooled, projs[j][...])
    return embed


def fetcher(sems):
    copies = []

    def fetch(source, target):
        copies.append(pltpu.make_async_copy(source, target, sems.at[len(copies)]))
        copies[-1].start()
        return copies[-1]

    return fetch


def columns(index_ref, pick, count):
    return pl.ds(pl.multiple_of((index_ref[0] ^ (2 * pick)) * count, count), count)


def first_kernel(images, index_ref, f_sib, partner_ref, f_own, s_own, s_sib, conv, proj, *refs):
    blocks, embed_ref, feat, proj_out, member_ref = refs[:3], refs[3], refs[4], refs[5], refs[6]
    short, conv_buf, partner, sems = refs[7:]
    fetch = fetcher(sems)
    at = columns(index_ref, 0, conv_buf.shape[0])
    shorts = [short.at[0], short.at[1]]
    waits = [
        [fetch(conv, conv_buf), fetch(s_sib.at[:, at], shorts[1])],
        [fetch(f_own, feat), fetch(s_own.at[:, at], shorts[0]), fetch(proj, proj_out)],
    ]
    partner_copy = fetch(partner_ref, partner)

    def ready(j, side):
        for copy in waits[1 - side]:
            copy.wait()

    embed = jnp.zeros(embed_ref.shape, F32)
    embed_ref[...] = forward_blocks(1, (feat, f_sib), shorts, [[conv_buf]], [proj_out], embed, blocks, ready)
    partner_copy.wait()
    member = lax.broadcasted_iota(jnp.int32, member_ref.shape, 0)
    whole = jnp.zeros(member_ref.shape, F32)
    for i in range(images):
        whole = jnp.where(member == i, partner[i].astype(F32), whole)
    member_ref[...] = whole


def middle_kernel(blocks, index_ref, f_own, f_sib, before, s_own, s_sib, *refs):
    convs, projs, refs = refs[:blocks], refs[blocks : 2 * blocks], refs[2 * blocks :]
    *outs, embed_ref, ahead_own, ahead_sib, short, sems = refs
    fetch = fetcher(sems)
    targets = [short.at[k] for k in range(2 * blocks)] + [ahead_own, ahead_sib]
    copies = [None] * len(targets)
    for j in range(blocks + 1):
        at = columns(index_ref, j + 1, short.shape[2])
        for side in (1, 0):
            copies[2 * j + side] = fetch((s_own, s_sib)[side].at[:, at], targets[2 * j + side])

    def ready(j, side):
        copies[2 * j + side].wait()

    feats, weights = (f_own, f_sib), [[c] for c in convs]
    embed_ref[...] = forward_blocks(blocks, feats, targets, weights, projs, before[...], outs, ready)
    ready(blocks, 1)
    ready(blocks, 0)


def last_kernel(images, f_own, f_sib, before, member, s_own, s_sib, proj, *refs):
    convs, outs = refs[:-5], refs[-5:]
    embed = forward_blocks(1, (f_own, f_sib), (s_own, s_sib), [convs], [proj], before[...], outs)
    mine_ref, send_ref = outs[-2:]
    lanes = member.shape[1]
    tiles = embed.shape[1] // lanes
    for g in (0, 1):
        for t in range(tiles):
            piece = embed[g * images : (g + 1) * images, t * lanes : (t + 1) * lanes]
            at = (g * tiles + t) * images
            mine_ref[at : at + images] = piece
            at = ((1 - g) * tiles + t) * images
            send_ref[at : at + images] = piece
    low = lax.broadcasted_iota(jnp.int32, (images, lanes), 1) < lanes // 2
    mine_ref[2 * tiles * images :] = jnp.where(low, member[...], 0.0)
    send_ref[2 * tiles * images :] = jnp.where(low, 0.0, member[...])


def forward_call(kernel, in_specs, shapes, scratch, busy, name, *arrays):
    rows, width, count = busy
    return pl.pallas_call(
        kernel,
        in_specs=in_specs,
        out_specs=[vspec()] * len(shapes),
        out_shape=[jax.ShapeDtypeStruct(shape, kind) for shape, kind in shapes],
        scratch_shapes=scratch,
        compiler_params=params(),
        cost_estimate=pl.CostEstimate(
            flops=16 * rows * width * count, bytes_accessed=8 * rows * count, transcendentals=0
        ),
        name=name,
    )(*arrays)


def block_shapes(rows, count, images):
    return [((rows, count), BF), ((rows, count), BF), ((2 * images, count), BF)]


def from_hbm(x):
    return pltpu.with_memory_space_constraint(x, pltpu.HBM)


def forward_first(index, partner, feats, shorts, conv, proj, images):
    rows, width = feats[0].shape
    count, embed = proj.shape
    shapes = block_shapes(rows, count, images)
    shapes += [((2 * images, embed), F32), ((rows, width), BF), ((count, embed), BF), ((images, 128), F32)]
    outs = forward_call(
        functools.partial(first_kernel, images),
        [pl.BlockSpec(memory_space=pltpu.SMEM)] + [vspec()] + [pl.BlockSpec(memory_space=pl.ANY)] * 6,
        shapes,
        [
            pltpu.VMEM((2, rows, count), BF),
            pltpu.VMEM((count, width), BF),
            pltpu.SMEM((images,), jnp.int32),
            pltpu.SemaphoreType.DMA((6,)),
        ],
        (rows, width, count),
        "forward_first",
        *(index, feats[1], from_hbm(partner), from_hbm(feats[0]), from_hbm(shorts[0]), from_hbm(shorts[1])),
        *(from_hbm(conv), from_hbm(proj)),
    )
    return outs[:3], outs[3], outs[4], outs[5], outs[6]


def forward_middle(index, feats, shorts, convs, projs, images, before):
    rows, width = feats[0].shape
    count, blocks = convs[0].shape[0], len(convs)
    outs = forward_call(
        functools.partial(middle_kernel, blocks),
        [pl.BlockSpec(memory_space=pltpu.SMEM)]
        + [vspec()] * 3
        + [pl.BlockSpec(memory_space=pl.ANY)] * 2
        + [vspec()] * (2 * blocks),
        block_shapes(rows, count, images) * blocks + [(before.shape, F32)] + [((rows, count), BF)] * 2,
        [pltpu.VMEM((2 * blocks, rows, count), BF), pltpu.SemaphoreType.DMA((2 * blocks + 2,))],
        (rows, width, blocks * count),
        "forward_middle",
        *(index, *feats, before, from_hbm(shorts[0]), from_hbm(shorts[1]), *convs, *projs),
    )
    return [outs[3 * j : 3 * j + 3] for j in range(blocks)], outs[-3], outs[-2:]


def forward_last(feats, shorts, convs, proj, images, before, member):
    rows, width = feats[0].shape
    count, embed = proj.shape
    arrays = (*feats, before, member, *shorts, proj, *convs)
    outs = forward_call(
        functools.partial(last_kernel, images),
        [vspec()] * len(arrays),
        block_shapes(rows, count, images) + [(((2 * embed // 128 + 1) * images, 128), F32)] * 2,
        [],
        (rows, width, count),
        "forward_last",
        *arrays,
    )
    return outs[:3], outs[3], outs[4]


def group_terms(z, inner, partner, groups):
    count = z.shape[0]
    squares = jnp.sum(z * z, axis=1, keepdims=True)
    spread = 2.0 * jnp.mean(squares)
    row = lax.broadcasted_iota(jnp.int32, (count, count), 0)
    col = lax.broadcasted_iota(jnp.int32, (count, count), 1)
    across = jnp.sum(jnp.where(row == col, squares, 0.0), axis=0, keepdims=True)
    kernel = jnp.exp(-(squares + across - 2.0 * inner) / (2.0 * spread))
    r_col = jnp.mean(kernel, axis=1, keepdims=True)
    r_row = jnp.mean(kernel, axis=0, keepdims=True)
    t = jnp.mean(r_col)
    centered = kernel - r_col - r_row + t
    scale_sq = float(count - 1) ** 2
    root = jnp.sqrt(jnp.sum(centered * centered, keepdims=True) / scale_sq + EPSILON)
    onehot = jnp.where(partner == col.astype(F32), 1.0, 0.0)
    positive = jnp.sum(kernel * onehot, keepdims=True) / count
    loss = -(positive - t) + GAMMA * root
    coeff = (-onehot / count + 1.0 / (count * count) + GAMMA * centered / (scale_sq * root)) / groups
    weighted = coeff * kernel
    moved = lax.dot_general(
        weighted, z, (((1,), (0,)), ((), ())), precision=lax.Precision.HIGHEST, preferred_element_type=F32
    )
    return loss, -(2.0 / spread) * (jnp.sum(weighted, axis=1, keepdims=True) * z - moved)


def hsic_kernel(slabs, images, groups, place_ref, *refs):
    chunks = refs[:-6]
    ge_ref, loss_ref, odd_ref, z_ref, p_ref, g_ref = refs[-6:]
    place = place_ref[0]
    odd_ref[...] = jnp.full(odd_ref.shape, (place & 1).astype(F32))
    tiles = z_ref.shape[2] // 128
    for j in range(slabs):
        block = chunks[0].at[j] if len(chunks) == 1 else chunks[ORDER.index(j)]
        at = pl.ds(pl.multiple_of((place ^ j) * images, images), images)
        for g in (0, 1):
            for t in range(tiles):
                row = (g * tiles + t) * images
                z_ref[g, at, t * 128 : (t + 1) * 128] = block[row : row + images]
        p_ref[at] = block[2 * tiles * images :]
    high_lane = lax.broadcasted_iota(jnp.int32, p_ref.shape, 1) >= 64
    count = slabs * images
    both = [z_ref[g] - jnp.mean(z_ref[g], axis=0, keepdims=True) for g in (0, 1)]
    pair = jnp.concatenate(both, axis=0)
    inner = lax.dot_general(pair, pair, NT, precision=lax.Precision.HIGHEST, preferred_element_type=F32)
    for g in (0, 1):
        part = inner[g * count : (g + 1) * count, g * count : (g + 1) * count]
        partner = jnp.max(jnp.where(high_lane == (g == 1), p_ref[...], -1.0), axis=1, keepdims=True)
        loss, grad = group_terms(both[g], part, partner, groups)
        if g == 0:
            loss_ref[...] = loss
        g_ref[g] = grad
    for j in range(slabs):
        at = pl.ds(pl.multiple_of((place ^ j) * images, images), images)
        for g in (0, 1):
            ge_ref[j, g * images : (g + 1) * images] = g_ref[g, at]


def hsic(place, chunks, embed, slabs, images, groups):
    return pl.pallas_call(
        functools.partial(hsic_kernel, slabs, images, groups),
        in_specs=[pl.BlockSpec(memory_space=pltpu.SMEM)] + [vspec()] * len(chunks),
        out_specs=[vspec()] * 3,
        out_shape=[
            jax.ShapeDtypeStruct((slabs, 2 * images, embed), F32),
            jax.ShapeDtypeStruct((1, 1), F32),
            jax.ShapeDtypeStruct((8, 128), F32),
        ],
        scratch_shapes=[
            pltpu.VMEM((2, slabs * images, embed), F32),
            pltpu.VMEM((slabs * images, 128), F32),
            pltpu.VMEM((2, slabs * images, embed), F32),
        ],
        compiler_params=params(80 * (slabs * images) ** 2),
        cost_estimate=pl.CostEstimate(flops=10**9, bytes_accessed=0, transcendentals=0),
        name="hsic_groups",
    )(place, *([chunks[j] for j in ORDER] if len(chunks) > 1 else chunks))


def backward_kernel(blocks, images, part, extra, after, f_own, f_sib, ge_ref, *refs):
    ins, outs = refs[: 4 * blocks], refs[4 * blocks + after :]
    mine = ge_ref[0].astype(BF)
    start, rows = part
    width = f_own.shape[1]
    grad_pool = [dot(mine, ins[4 * j + 3][start : start + rows], NT) / POS for j in range(blocks)]
    total = jnp.zeros((blocks * rows, width), F32)
    for side, feat in enumerate((f_own, f_sib)):
        grad_hidden = []
        for j in range(blocks):
            spread = spread_rows(grad_pool[j][side * images : (side + 1) * images], images)
            grad_hidden.append(spread.astype(BF) * ins[4 * j + side][:, start : start + rows])
        total = total + dot(jnp.concatenate(grad_hidden, axis=1), feat[...], TN)
    for j in range(blocks):
        out, pooled = outs[j], ins[4 * j + 2]
        out[0:rows] = total[j * rows : (j + 1) * rows].astype(out.dtype)
        if extra == "pooled":
            rest = jnp.zeros((2 * images, width - pooled.shape[1]), BF)
            out[rows:] = jnp.concatenate([pooled[...], rest], axis=1)
        if extra == "embed":
            half = ge_ref.shape[0] * images // 2
            flat = ge_ref[:, :images].reshape(2 * half, ge_ref.shape[2]).astype(BF)
            out[rows:] = jnp.concatenate([flat[:half], flat[half:]], axis=1)


def backward(feats, ge, blocks, images, part, extra=None, after=()):
    length, width = feats[0].shape
    rows = part[1]
    high = rows + {None: 0, "pooled": 2 * images, "embed": ge.shape[0] * images // 2}[extra]
    return pl.pallas_call(
        functools.partial(backward_kernel, len(blocks), images, part, extra, len(after)),
        in_specs=[vspec()] * (3 + 4 * len(blocks)) + [pl.BlockSpec(memory_space=pl.ANY)] * len(after),
        out_specs=[vspec()] * len(blocks),
        out_shape=[jax.ShapeDtypeStruct((high, width), BF if extra else F32)] * len(blocks),
        compiler_params=params(),
        cost_estimate=pl.CostEstimate(
            flops=16 * len(blocks) * length * width * rows,
            bytes_accessed=4 * len(blocks) * length * rows,
            transcendentals=0,
        ),
        name="backward_blocks",
    )(*feats, ge, *[a for block in blocks for a in block], *after)


def small_call(kernel, shapes, name, *arrays, tokens=()):
    return pl.pallas_call(
        kernel,
        in_specs=[vspec()] * len(arrays) + [pl.BlockSpec(memory_space=pl.ANY)] * len(tokens),
        out_specs=[vspec()] * len(shapes),
        out_shape=[jax.ShapeDtypeStruct(shape, kind) for shape, kind in shapes],
        compiler_params=params(),
        cost_estimate=pl.CostEstimate(flops=0, bytes_accessed=0, transcendentals=0),
        name=name,
    )(*arrays, *tokens)


def sum_kernel(*refs):
    total = refs[0][...].astype(F32)
    for ref in refs[1:-1]:
        total = total + ref[...].astype(F32)
    refs[-1][...] = total.astype(refs[-1].dtype)


def sum_of(kind, *arrays):
    return small_call(sum_kernel, [(arrays[0].shape, kind)], "sum_arrays", *arrays)[0]


def collect_kernel(start, rows, count_msgs, own, pooled, *refs):
    msgs, out = refs[:count_msgs], refs[-1]
    total = own[start : start + rows]
    for msg in msgs:
        total = total + msg[0:rows].astype(F32)
    out[0:rows] = total.astype(BF)
    if out.shape[0] == rows:
        return
    high, count = pooled.shape
    slab = [pooled[...]] + [msg[rows : rows + high, 0:count] for msg in msgs]
    tall = (out.shape[0] - rows) // high
    for k, piece in enumerate(slab):
        at = rows + k % tall * high
        out[at : at + high, k // tall * count : (k // tall + 1) * count] = piece


def collect(own, pooled, msgs, part, with_pooled, token):
    start, rows = part
    width = own.shape[1]
    more = (len(msgs) + 1) * pooled.size // width if with_pooled else 0
    kernel = functools.partial(collect_kernel, start, rows, len(msgs))
    return small_call(kernel, [((rows + more, width), BF)], "collect_terms", own, pooled, *msgs, tokens=token)[0]


def collect_grads_kernel(start, rows, own, *refs):
    msgs, (out, tails) = refs[:-2], refs[-2:]
    total = own[start : start + rows]
    for msg in msgs:
        total = total + msg[0:rows].astype(F32)
    out[...] = total.astype(BF)
    high = msgs[0].shape[0] - rows
    for k, msg in enumerate(msgs):
        tails[k * high : (k + 1) * high] = msg[rows:]


def collect_grads(own, msgs, part):
    start, rows = part
    width = own.shape[1]
    shapes = [((rows, width), BF), ((len(msgs) * (msgs[0].shape[0] - rows), width), BF)]
    return small_call(functools.partial(collect_grads_kernel, start, rows), shapes, "collect_terms", own, *msgs)


def merge_kernel(rows, mine, other, *refs):
    out = refs[-1]
    out[0:rows] = (mine[0:rows].astype(F32) + other[0:rows].astype(F32)).astype(BF)
    more = mine.shape[0] - rows
    if more:
        out[rows : rows + more] = mine[rows:]
        out[rows + more :] = other[rows:]


def merge(rows, mine, other, *token):
    high, width = mine.shape
    shape = (2 * high - rows, width)
    return small_call(functools.partial(merge_kernel, rows), [(shape, BF)], "merge_slabs", mine, other, tokens=token)[0]


def choose(odd, width):
    return jnp.broadcast_to(odd[0:1, 0:1], (1, width)) > 0.5


def collect_halves_kernel(start, rows, own, pooled, odd, *refs):
    msgs, (keep, send, slab_ref) = [refs[(2, 0, 1).index(i)] for i in range(len(refs) - 3)], refs[-3:]
    width, half = own.shape[1], rows // 2
    total = own[start : start + rows]
    for msg in msgs:
        total = total + msg[0:rows].astype(F32)
    total = total.astype(BF).astype(F32)
    pick = choose(odd, width)
    keep[...] = jnp.where(pick, total[half:], total[:half]).astype(BF)
    send[...] = jnp.where(pick, total[:half], total[half:]).astype(BF)
    high, count = pooled.shape
    slab = [pooled[...]] + [msg[rows : rows + high, 0:count] for msg in msgs]
    tall = slab_ref.shape[0] // high
    for k, piece in enumerate(slab):
        at = k % tall * high
        slab_ref[at : at + high, k // tall * count : (k // tall + 1) * count] = piece


def add_and_append_kernel(rows, count, mine, other, *refs):
    more, out = refs[:count], refs[-1]
    out[0:rows] = (mine[0:rows].astype(F32) + other[0:rows].astype(F32)).astype(BF)
    at = rows
    for ref in more:
        tail = ref[...] if ref.shape[0] < rows else ref[rows:]
        out[at : at + tail.shape[0]] = tail
        at += tail.shape[0]


def sum_by_halves(own, pooled, odd, msgs, part, token, late):
    start, rows = part
    width, half = own.shape[1], rows // 2
    slab_rows = (len(msgs) + 1) * pooled.size // width
    keep, send, slab = small_call(
        functools.partial(collect_halves_kernel, start, rows),
        [((half, width), BF), ((half, width), BF), ((slab_rows, width), BF)],
        "collect_terms",
        *(own, pooled, odd, *[msgs[i] for i in (2, 0, 1)]),
    )
    first = small_call(
        functools.partial(add_and_append_kernel, half, 1),
        [((half + slab_rows, width), BF)],
        "merge_slabs",
        *(keep, swap(send, "dp", 1), slab),
        tokens=token,
    )[0]
    far = swap(first, "dp", 2)
    mine = small_call(
        functools.partial(add_and_append_kernel, half, 2),
        [((half + 2 * slab_rows, width), BF)],
        "merge_slabs",
        *(first, far, first, far),
        tokens=late,
    )[0]
    return mine, swap(mine, "dp", 1)


def final_halves(odd, mine, other, pieces, out):
    tail = pieces[0].shape[0]
    head = out.shape[0] - tail
    half = head // 2
    pick = choose(odd, out.shape[1])
    left, right = mine[0:half].astype(F32), other[0:half].astype(F32)
    out[0:half] = jnp.where(pick, right, left)
    out[half:head] = jnp.where(pick, left, right)
    out[head:] = pieces[0][...].astype(F32) + pieces[1][...].astype(F32)


def final_whole(pieces, out):
    tail = pieces[2].shape[0]
    head = out.shape[0] - tail
    out[0:head] = pieces[0][0:head].astype(F32) + pieces[1][0:head].astype(F32)
    out[head:] = pieces[2][...].astype(F32) + pieces[3][...].astype(F32)


def proj_sum(slabs, images, order, rows, own_ge, mine, other, tails, out):
    count, embed = out.shape
    groups = mine.shape[1] // count
    half = slabs * images // 2
    per = (mine.shape[0] - rows) // (slabs // 2)
    together = per // (2 * images)
    parts = []
    for j in range(slabs):
        pieces = [own_ge[j].astype(BF)]
        start, left = j * images % half, j * images // half * embed
        base = start // 16 * 16
        for k in range(0, tails[0].shape[0], half):
            pair = [t[k + base : k + base + 16, left : left + embed].astype(F32) for t in tails]
            pieces.append(jnp.concatenate([p[start - base : start - base + images] for p in pair], axis=0).astype(BF))
        at = order.index(j)
        ref, at = (mine, at) if at < slabs // 2 else (other, at - slabs // 2)
        total = jnp.zeros((count, embed), F32)
        for g in range(groups):
            pooled = ref[rows + at * per : rows + (at + 1) * per, g * count : (g + 1) * count]
            grads = jnp.concatenate(pieces[g * together : (g + 1) * together], axis=0)
            total = total + dot(pooled, grads, TN)
        parts.append(total)
    while len(parts) > 1:
        parts = [parts[k] + parts[k + 1] for k in range(0, len(parts), 2)]
    out[...] = parts[0]


def gate_kernel(x, token, out):
    out[...] = x[...]


def after(x, token):
    return small_call(gate_kernel, [(x.shape, x.dtype)], "gate", x, tokens=(token,))[0]


def part_kernel(start, x, token, out):
    out[...] = x[start : start + out.shape[0]]


def half_of(start, x, token):
    shape = (x.shape[0] // 2, x.shape[1])
    return small_call(functools.partial(part_kernel, start), [(shape, x.dtype)], "half_of", x, tokens=(token,))[0]


def last_sums_kernel(slabs, images, order, rows, own_ge, odd, last_mine, last_other, mine, other, *refs):
    tails, (conv_out, proj_out) = refs[:-2], refs[-2:]
    proj_sum(slabs, images, order, rows, own_ge, mine, other, tails, proj_out)
    if slabs == 4:
        final_halves(odd, mine, other, (last_mine, last_other), conv_out)
    else:
        final_whole((mine, other, last_mine, last_other), conv_out)


def swap(x, axis, bit):
    size = lax.axis_size(axis)
    return lax.ppermute(x, axis, [(i, i ^ bit) for i in range(size)])


def gather_slabs(x, slabs):
    if slabs <= 4:
        return [x] + [swap(x, "dp", j) for j in range(1, slabs)]
    whole = lax.all_gather(x, "dp", axis=0, tiled=False)
    return [jnp.take(whole, lax.axis_index("dp") ^ jnp.arange(slabs), axis=0)]


def local(features, shortcut, conv_weight, proj_weight, partner):
    slabs, groups = lax.axis_size("dp"), lax.axis_size("fsdp")
    peers = groups // 2
    images = features.shape[0] // POS
    count, width = conv_weight.shape
    place = lax.axis_index("dp").astype(jnp.int32).reshape(1)
    index = lax.axis_index("fsdp").astype(jnp.int32).reshape(1)

    f_sib = swap(features, "fsdp", 1)
    s_sib = swap(shortcut, "fsdp", 1)
    shorts = (shortcut, s_sib)
    first, embed, f_own, proj_own, member = forward_first(
        index, partner, (features, f_sib), shorts, conv_weight, proj_weight, images
    )
    feats = (f_own, f_sib)
    projs = [swap(proj_weight, "fsdp", 2 * j) for j in range(1, peers)]
    if peers == 4:
        conv_y = swap(conv_weight, "fsdp", 4)
        conv_x = swap(conv_weight, "fsdp", 2)
        halves = [
            swap(half_of(0, conv_y, embed), "fsdp", 2),
            swap(half_of(count // 2, conv_x, embed), "fsdp", 4),
        ]
        convs = [conv_x, conv_y, halves]
    else:
        convs = [swap(conv_weight, "fsdp", 2 * j) for j in range(1, peers)]
        convs[-1] = [convs[-1]]
    middle, embed, ahead = forward_middle(index, feats, shorts, convs[:-1], projs[:-1], images, embed)
    last, mine, send = forward_last(feats, ahead, convs[-1], projs[-1], images, embed, member)
    blocks, projs = [first, *middle, last], [proj_own, *projs]
    blocks = [(*b, p) for b, p in zip(blocks, projs)]
    embeds = sum_of(F32, mine, swap(send, "fsdp", 1))
    ge, loss, odd = hsic(place, gather_slabs(embeds, slabs), proj_weight.shape[1], slabs, images, groups)

    first_rows = count * SPLIT // 8
    parts = [(0, first_rows), (first_rows, count - first_rows)]
    terms, done = [], ()
    for part, extra in zip(parts, ("pooled", "embed")):
        if terms:
            (own,) = backward(feats, ge, blocks[:1], images, (0, count), None, done)
            done = (own,)
        done = tuple(backward(feats, ge, blocks[1:], images, part, extra, done))
        terms.append(done)

    received = [[swap(m, "fsdp", 2 * j) for j, m in enumerate(term, 1)] for term in terms]
    total, tails = collect_grads(own, received[1], parts[1])
    if slabs == 4:
        merged = merge(parts[1][1], total, swap(total, "dp", 1))
        mine, other = sum_by_halves(own, blocks[0][2], odd, received[0], parts[0], (total,), (merged,))
        pieces = [mine, other, merged, swap(merged, "dp", 2)]
        order, above = [0, 2, 1, 3], parts[0][1] // 2
    else:
        pieces, order, above = [], list(range(slabs)), parts[0][1]
        for piece, part in zip((collect(own, blocks[0][2], received[0], parts[0], True, ()), total), parts):
            bit = 1
            while 2 * bit < slabs:
                piece = merge(part[1], piece, swap(piece, "dp", bit))
                bit *= 2
            pieces += [piece, swap(piece, "dp", bit)]
    grad_conv, grad_proj = small_call(
        functools.partial(last_sums_kernel, slabs, images, order, above),
        [((count, width), F32), (proj_weight.shape, F32)],
        "last_sums",
        *(ge, odd, pieces[2], pieces[3], pieces[0], pieces[1], tails, swap(tails, "fsdp", 1)),
    )
    return grad_conv, grad_proj, loss.reshape(1)


def solution(mesh):
    return jax.shard_map(
        local,
        mesh=mesh,
        in_specs=(
            P(("dp", "fsdp"), None),
            P(("dp", "fsdp"), None),
            P("fsdp", None),
            P("fsdp", None),
            P(("dp", "fsdp")),
        ),
        out_specs=(P("fsdp", None), P("fsdp", None), P("fsdp")),
        check_vma=False,
    )
```

```python
import functools

import jax
import jax.numpy as jnp
from jax import lax
from jax.experimental import pallas as pl
from jax.experimental.pallas import tpu as pltpu
from jax.sharding import PartitionSpec as P

POS = 49
GAMMA = 3.0
EPSILON = 1e-06
BF = jnp.bfloat16
F32 = jnp.float32
NT = (((1,), (1,)), ((), ()))
TN = (((0,), (0,)), ((), ()))
VMEM_LIMIT = 8 * 1024 * 1024
SPLIT = 4
ORDER = (0, 2, 3, 1)


def dot(a, b, dims=(((1,), (0,)), ((), ()))):
    return lax.dot_general(a, b, dims, preferred_element_type=F32)


def vspec():
    return pl.BlockSpec(memory_space=pltpu.VMEM)


def params(more=0):
    return pltpu.CompilerParams(vmem_limit_bytes=VMEM_LIMIT + more)


def tile_iota(width):
    return lax.broadcasted_iota(jnp.int32, (8, width), 0)


def pool_rows(hidden, images):
    width = hidden.shape[1]
    row = tile_iota(width)
    pooled = jnp.zeros((images, width), F32)
    for i in range(images):
        first, last = i * POS, i * POS + POS - 1
        total = jnp.zeros((8, width), F32)
        for t in range(first // 8, last // 8 + 1):
            tile = hidden[8 * t : 8 * t + 8]
            if 8 * t < first:
                tile = jnp.where(row >= first - 8 * t, tile, 0.0)
            if 8 * t + 7 > last:
                tile = jnp.where(row <= last - 8 * t, tile, 0.0)
            total = total + tile
        pooled = jnp.where(row == i, jnp.sum(total, axis=0, keepdims=True) / POS, pooled)
    return pooled


def spread_rows(values, images):
    width = values.shape[1]
    row = tile_iota(width)
    whole = [jnp.broadcast_to(values[i : i + 1], (8, width)) for i in range(images)]
    tiles = []
    for t in range(images * POS // 8):
        low, high = 8 * t // POS, (8 * t + 7) // POS
        tiles.append(whole[low] if low == high else jnp.where(row < high * POS - 8 * t, whole[low], whole[high]))
    return jnp.concatenate(tiles, axis=0)


def forward_block(feat, short, convs, images):
    preact = [dot(feat, conv[...], NT) for conv in convs]
    preact = preact[0] if len(preact) == 1 else jnp.concatenate(preact, axis=1)
    hidden = jnp.maximum(preact + short.astype(F32), 0.0)
    mask = jnp.where(hidden > 0, 1.0, 0.0).astype(BF)
    return mask, pool_rows(hidden, images)


def forward_blocks(picks, feats, shorts, convs, projs, embed, outs, ready=None):
    images = outs[2].shape[0] // 2
    for j in range(picks):
        pooled = [None, None]
        for side in (1, 0):
            if ready is not None:
                ready(j, side)
            mask, pooled[side] = forward_block(feats[side][...], shorts[2 * j + side][...], convs[j], images)
            outs[3 * j + side][...] = mask
        pooled = jnp.concatenate(pooled, axis=0).astype(BF)
        outs[3 * j + 2][...] = pooled
        embed = embed + dot(pooled, projs[j][...])
    return embed


def fetcher(sems):
    copies = []

    def fetch(source, target):
        copies.append(pltpu.make_async_copy(source, target, sems.at[len(copies)]))
        copies[-1].start()
        return copies[-1]

    return fetch


def columns(index_ref, pick, count):
    return pl.ds(pl.multiple_of((index_ref[0] ^ (2 * pick)) * count, count), count)


def first_kernel(images, index_ref, f_sib, partner_ref, f_own, s_own, s_sib, conv, proj, *refs):
    blocks, embed_ref, feat, proj_out, member_ref = refs[:3], refs[3], refs[4], refs[5], refs[6]
    short, conv_buf, partner, sems = refs[7:]
    fetch = fetcher(sems)
    at = columns(index_ref, 0, conv_buf.shape[0])
    shorts = [short.at[0], short.at[1]]
    waits = [
        [fetch(conv, conv_buf), fetch(s_sib.at[:, at], shorts[1])],
        [fetch(f_own, feat), fetch(s_own.at[:, at], shorts[0]), fetch(proj, proj_out)],
    ]
    partner_copy = fetch(partner_ref, partner)

    def ready(j, side):
        for copy in waits[1 - side]:
            copy.wait()

    embed = jnp.zeros(embed_ref.shape, F32)
    embed_ref[...] = forward_blocks(1, (feat, f_sib), shorts, [[conv_buf]], [proj_out], embed, blocks, ready)
    partner_copy.wait()
    member = lax.broadcasted_iota(jnp.int32, member_ref.shape, 0)
    whole = jnp.zeros(member_ref.shape, F32)
    for i in range(images):
        whole = jnp.where(member == i, partner[i].astype(F32), whole)
    member_ref[...] = whole


def middle_kernel(blocks, index_ref, f_own, f_sib, before, s_own, s_sib, *refs):
    convs, projs, refs = refs[:blocks], refs[blocks : 2 * blocks], refs[2 * blocks :]
    *outs, embed_ref, ahead_own, ahead_sib, short, sems = refs
    fetch = fetcher(sems)
    targets = [short.at[k] for k in range(2 * blocks)] + [ahead_own, ahead_sib]
    copies = [None] * len(targets)
    for j in range(blocks + 1):
        at = columns(index_ref, j + 1, short.shape[2])
        for side in (1, 0):
            copies[2 * j + side] = fetch((s_own, s_sib)[side].at[:, at], targets[2 * j + side])

    def ready(j, side):
        copies[2 * j + side].wait()

    feats, weights = (f_own, f_sib), [[c] for c in convs]
    embed_ref[...] = forward_blocks(blocks, feats, targets, weights, projs, before[...], outs, ready)
    ready(blocks, 1)
    ready(blocks, 0)


def last_kernel(images, f_own, f_sib, before, member, s_own, s_sib, proj, *refs):
    convs, outs = refs[:-5], refs[-5:]
    embed = forward_blocks(1, (f_own, f_sib), (s_own, s_sib), [convs], [proj], before[...], outs)
    mine_ref, send_ref = outs[-2:]
    lanes = member.shape[1]
    tiles = embed.shape[1] // lanes
    for g in (0, 1):
        for t in range(tiles):
            piece = embed[g * images : (g + 1) * images, t * lanes : (t + 1) * lanes]
            at = (g * tiles + t) * images
            mine_ref[at : at + images] = piece
            at = ((1 - g) * tiles + t) * images
            send_ref[at : at + images] = piece
    low = lax.broadcasted_iota(jnp.int32, (images, lanes), 1) < lanes // 2
    mine_ref[2 * tiles * images :] = jnp.where(low, member[...], 0.0)
    send_ref[2 * tiles * images :] = jnp.where(low, 0.0, member[...])


def forward_call(kernel, in_specs, shapes, scratch, busy, name, *arrays):
    rows, width, count = busy
    return pl.pallas_call(
        kernel,
        in_specs=in_specs,
        out_specs=[vspec()] * len(shapes),
        out_shape=[jax.ShapeDtypeStruct(shape, kind) for shape, kind in shapes],
        scratch_shapes=scratch,
        compiler_params=params(),
        cost_estimate=pl.CostEstimate(
            flops=16 * rows * width * count, bytes_accessed=8 * rows * count, transcendentals=0
        ),
        name=name,
    )(*arrays)


def block_shapes(rows, count, images):
    return [((rows, count), BF), ((rows, count), BF), ((2 * images, count), BF)]


def from_hbm(x):
    return pltpu.with_memory_space_constraint(x, pltpu.HBM)


def forward_first(index, partner, feats, shorts, conv, proj, images):
    rows, width = feats[0].shape
    count, embed = proj.shape
    shapes = block_shapes(rows, count, images)
    shapes += [((2 * images, embed), F32), ((rows, width), BF), ((count, embed), BF), ((images, 128), F32)]
    outs = forward_call(
        functools.partial(first_kernel, images),
        [pl.BlockSpec(memory_space=pltpu.SMEM)] + [vspec()] + [pl.BlockSpec(memory_space=pl.ANY)] * 6,
        shapes,
        [
            pltpu.VMEM((2, rows, count), BF),
            pltpu.VMEM((count, width), BF),
            pltpu.SMEM((images,), jnp.int32),
            pltpu.SemaphoreType.DMA((6,)),
        ],
        (rows, width, count),
        "forward_first",
        *(index, feats[1], from_hbm(partner), from_hbm(feats[0]), from_hbm(shorts[0]), from_hbm(shorts[1])),
        *(from_hbm(conv), from_hbm(proj)),
    )
    return outs[:3], outs[3], outs[4], outs[5], outs[6]


def forward_middle(index, feats, shorts, convs, projs, images, before):
    rows, width = feats[0].shape
    count, blocks = convs[0].shape[0], len(convs)
    outs = forward_call(
        functools.partial(middle_kernel, blocks),
        [pl.BlockSpec(memory_space=pltpu.SMEM)]
        + [vspec()] * 3
        + [pl.BlockSpec(memory_space=pl.ANY)] * 2
        + [vspec()] * (2 * blocks),
        block_shapes(rows, count, images) * blocks + [(before.shape, F32)] + [((rows, count), BF)] * 2,
        [pltpu.VMEM((2 * blocks, rows, count), BF), pltpu.SemaphoreType.DMA((2 * blocks + 2,))],
        (rows, width, blocks * count),
        "forward_middle",
        *(index, *feats, before, from_hbm(shorts[0]), from_hbm(shorts[1]), *convs, *projs),
    )
    return [outs[3 * j : 3 * j + 3] for j in range(blocks)], outs[-3], outs[-2:]


def forward_last(feats, shorts, convs, proj, images, before, member):
    rows, width = feats[0].shape
    count, embed = proj.shape
    arrays = (*feats, before, member, *shorts, proj, *convs)
    outs = forward_call(
        functools.partial(last_kernel, images),
        [vspec()] * len(arrays),
        block_shapes(rows, count, images) + [(((2 * embed // 128 + 1) * images, 128), F32)] * 2,
        [],
        (rows, width, count),
        "forward_last",
        *arrays,
    )
    return outs[:3], outs[3], outs[4]


def group_terms(z, inner, partner, groups):
    count = z.shape[0]
    squares = jnp.sum(z * z, axis=1, keepdims=True)
    spread = 2.0 * jnp.mean(squares)
    row = lax.broadcasted_iota(jnp.int32, (count, count), 0)
    col = lax.broadcasted_iota(jnp.int32, (count, count), 1)
    across = jnp.sum(jnp.where(row == col, squares, 0.0), axis=0, keepdims=True)
    kernel = jnp.exp(-(squares + across - 2.0 * inner) / (2.0 * spread))
    r_col = jnp.mean(kernel, axis=1, keepdims=True)
    r_row = jnp.mean(kernel, axis=0, keepdims=True)
    t = jnp.mean(r_col)
    centered = kernel - r_col - r_row + t
    scale_sq = float(count - 1) ** 2
    root = jnp.sqrt(jnp.sum(centered * centered, keepdims=True) / scale_sq + EPSILON)
    onehot = jnp.where(partner == col.astype(F32), 1.0, 0.0)
    positive = jnp.sum(kernel * onehot, keepdims=True) / count
    loss = -(positive - t) + GAMMA * root
    coeff = (-onehot / count + 1.0 / (count * count) + GAMMA * centered / (scale_sq * root)) / groups
    weighted = coeff * kernel
    moved = lax.dot_general(
        weighted, z, (((1,), (0,)), ((), ())), precision=lax.Precision.HIGHEST, preferred_element_type=F32
    )
    return loss, -(2.0 / spread) * (jnp.sum(weighted, axis=1, keepdims=True) * z - moved)


def hsic_kernel(slabs, images, groups, place_ref, *refs):
    chunks = refs[:-6]
    ge_ref, loss_ref, odd_ref, z_ref, p_ref, g_ref = refs[-6:]
    place = place_ref[0]
    odd_ref[...] = jnp.full(odd_ref.shape, (place & 1).astype(F32))
    tiles = z_ref.shape[2] // 128
    for j in range(slabs):
        block = chunks[0].at[j] if len(chunks) == 1 else chunks[ORDER.index(j)]
        at = pl.ds(pl.multiple_of((place ^ j) * images, images), images)
        for g in (0, 1):
            for t in range(tiles):
                row = (g * tiles + t) * images
                z_ref[g, at, t * 128 : (t + 1) * 128] = block[row : row + images]
        p_ref[at] = block[2 * tiles * images :]
    high_lane = lax.broadcasted_iota(jnp.int32, p_ref.shape, 1) >= 64
    count = slabs * images
    both = [z_ref[g] - jnp.mean(z_ref[g], axis=0, keepdims=True) for g in (0, 1)]
    pair = jnp.concatenate(both, axis=0)
    inner = lax.dot_general(pair, pair, NT, precision=lax.Precision.HIGHEST, preferred_element_type=F32)
    for g in (0, 1):
        part = inner[g * count : (g + 1) * count, g * count : (g + 1) * count]
        partner = jnp.max(jnp.where(high_lane == (g == 1), p_ref[...], -1.0), axis=1, keepdims=True)
        loss, grad = group_terms(both[g], part, partner, groups)
        if g == 0:
            loss_ref[...] = loss
        g_ref[g] = grad
    for j in range(slabs):
        at = pl.ds(pl.multiple_of((place ^ j) * images, images), images)
        for g in (0, 1):
            ge_ref[j, g * images : (g + 1) * images] = g_ref[g, at]


def hsic(place, chunks, embed, slabs, images, groups):
    return pl.pallas_call(
        functools.partial(hsic_kernel, slabs, images, groups),
        in_specs=[pl.BlockSpec(memory_space=pltpu.SMEM)] + [vspec()] * len(chunks),
        out_specs=[vspec()] * 3,
        out_shape=[
            jax.ShapeDtypeStruct((slabs, 2 * images, embed), F32),
            jax.ShapeDtypeStruct((1, 1), F32),
            jax.ShapeDtypeStruct((8, 128), F32),
        ],
        scratch_shapes=[
            pltpu.VMEM((2, slabs * images, embed), F32),
            pltpu.VMEM((slabs * images, 128), F32),
            pltpu.VMEM((2, slabs * images, embed), F32),
        ],
        compiler_params=params(80 * (slabs * images) ** 2),
        cost_estimate=pl.CostEstimate(flops=10**9, bytes_accessed=0, transcendentals=0),
        name="hsic_groups",
    )(place, *([chunks[j] for j in ORDER] if len(chunks) > 1 else chunks))


def backward_kernel(blocks, images, part, extra, after, f_own, f_sib, ge_ref, *refs):
    ins, outs = refs[: 4 * blocks], refs[4 * blocks + after :]
    mine = ge_ref[0].astype(BF)
    start, rows = part
    width = f_own.shape[1]
    grad_pool = [dot(mine, ins[4 * j + 3][start : start + rows], NT) / POS for j in range(blocks)]
    total = jnp.zeros((blocks * rows, width), F32)
    for side, feat in enumerate((f_own, f_sib)):
        grad_hidden = []
        for j in range(blocks):
            spread = spread_rows(grad_pool[j][side * images : (side + 1) * images], images)
            grad_hidden.append(spread.astype(BF) * ins[4 * j + side][:, start : start + rows])
        total = total + dot(jnp.concatenate(grad_hidden, axis=1), feat[...], TN)
    for j in range(blocks):
        out, pooled = outs[j], ins[4 * j + 2]
        out[0:rows] = total[j * rows : (j + 1) * rows].astype(out.dtype)
        if extra == "pooled":
            rest = jnp.zeros((2 * images, width - pooled.shape[1]), BF)
            out[rows:] = jnp.concatenate([pooled[...], rest], axis=1)
        if extra == "embed":
            half = ge_ref.shape[0] * images // 2
            flat = ge_ref[:, :images].reshape(2 * half, ge_ref.shape[2]).astype(BF)
            out[rows:] = jnp.concatenate([flat[:half], flat[half:]], axis=1)


def backward(feats, ge, blocks, images, part, extra=None, after=()):
    length, width = feats[0].shape
    rows = part[1]
    high = rows + {None: 0, "pooled": 2 * images, "embed": ge.shape[0] * images // 2}[extra]
    return pl.pallas_call(
        functools.partial(backward_kernel, len(blocks), images, part, extra, len(after)),
        in_specs=[vspec()] * (3 + 4 * len(blocks)) + [pl.BlockSpec(memory_space=pl.ANY)] * len(after),
        out_specs=[vspec()] * len(blocks),
        out_shape=[jax.ShapeDtypeStruct((high, width), BF if extra else F32)] * len(blocks),
        compiler_params=params(),
        cost_estimate=pl.CostEstimate(
            flops=16 * len(blocks) * length * width * rows,
            bytes_accessed=4 * len(blocks) * length * rows,
            transcendentals=0,
        ),
        name="backward_blocks",
    )(*feats, ge, *[a for block in blocks for a in block], *after)


def small_call(kernel, shapes, name, *arrays, tokens=()):
    return pl.pallas_call(
        kernel,
        in_specs=[vspec()] * len(arrays) + [pl.BlockSpec(memory_space=pl.ANY)] * len(tokens),
        out_specs=[vspec()] * len(shapes),
        out_shape=[jax.ShapeDtypeStruct(shape, kind) for shape, kind in shapes],
        compiler_params=params(),
        cost_estimate=pl.CostEstimate(flops=0, bytes_accessed=0, transcendentals=0),
        name=name,
    )(*arrays, *tokens)


def sum_kernel(*refs):
    total = refs[0][...].astype(F32)
    for ref in refs[1:-1]:
        total = total + ref[...].astype(F32)
    refs[-1][...] = total.astype(refs[-1].dtype)


def sum_of(kind, *arrays):
    return small_call(sum_kernel, [(arrays[0].shape, kind)], "sum_arrays", *arrays)[0]


def collect_kernel(start, rows, count_msgs, own, pooled, *refs):
    msgs, out = refs[:count_msgs], refs[-1]
    total = own[start : start + rows]
    for msg in msgs:
        total = total + msg[0:rows].astype(F32)
    out[0:rows] = total.astype(BF)
    if out.shape[0] == rows:
        return
    high, count = pooled.shape
    slab = [pooled[...]] + [msg[rows : rows + high, 0:count] for msg in msgs]
    tall = (out.shape[0] - rows) // high
    for k, piece in enumerate(slab):
        at = rows + k % tall * high
        out[at : at + high, k // tall * count : (k // tall + 1) * count] = piece


def collect(own, pooled, msgs, part, with_pooled, token):
    start, rows = part
    width = own.shape[1]
    more = (len(msgs) + 1) * pooled.size // width if with_pooled else 0
    kernel = functools.partial(collect_kernel, start, rows, len(msgs))
    return small_call(kernel, [((rows + more, width), BF)], "collect_terms", own, pooled, *msgs, tokens=token)[0]


def collect_grads_kernel(start, rows, own, *refs):
    msgs, (out, tails) = refs[:-2], refs[-2:]
    total = own[start : start + rows]
    for msg in msgs:
        total = total + msg[0:rows].astype(F32)
    out[...] = total.astype(BF)
    high = msgs[0].shape[0] - rows
    for k, msg in enumerate(msgs):
        tails[k * high : (k + 1) * high] = msg[rows:]


def collect_grads(own, msgs, part):
    start, rows = part
    width = own.shape[1]
    shapes = [((rows, width), BF), ((len(msgs) * (msgs[0].shape[0] - rows), width), BF)]
    return small_call(functools.partial(collect_grads_kernel, start, rows), shapes, "collect_terms", own, *msgs)


def merge_kernel(rows, mine, other, *refs):
    out = refs[-1]
    out[0:rows] = (mine[0:rows].astype(F32) + other[0:rows].astype(F32)).astype(BF)
    more = mine.shape[0] - rows
    if more:
        out[rows : rows + more] = mine[rows:]
        out[rows + more :] = other[rows:]


def merge(rows, mine, other, *token):
    high, width = mine.shape
    shape = (2 * high - rows, width)
    return small_call(functools.partial(merge_kernel, rows), [(shape, BF)], "merge_slabs", mine, other, tokens=token)[0]


def choose(odd, width):
    return jnp.broadcast_to(odd[0:1, 0:1], (1, width)) > 0.5


def collect_halves_kernel(start, rows, own, pooled, odd, *refs):
    msgs, (keep, send, slab_ref) = [refs[(2, 0, 1).index(i)] for i in range(len(refs) - 3)], refs[-3:]
    width, half = own.shape[1], rows // 2
    total = own[start : start + rows]
    for msg in msgs:
        total = total + msg[0:rows].astype(F32)
    total = total.astype(BF).astype(F32)
    pick = choose(odd, width)
    keep[...] = jnp.where(pick, total[half:], total[:half]).astype(BF)
    send[...] = jnp.where(pick, total[:half], total[half:]).astype(BF)
    high, count = pooled.shape
    slab = [pooled[...]] + [msg[rows : rows + high, 0:count] for msg in msgs]
    tall = slab_ref.shape[0] // high
    for k, piece in enumerate(slab):
        at = k % tall * high
        slab_ref[at : at + high, k // tall * count : (k // tall + 1) * count] = piece


def add_and_append_kernel(rows, count, mine, other, *refs):
    more, out = refs[:count], refs[-1]
    out[0:rows] = (mine[0:rows].astype(F32) + other[0:rows].astype(F32)).astype(BF)
    at = rows
    for ref in more:
        tail = ref[...] if ref.shape[0] < rows else ref[rows:]
        out[at : at + tail.shape[0]] = tail
        at += tail.shape[0]


def sum_by_halves(own, pooled, odd, msgs, part, token, late):
    start, rows = part
    width, half = own.shape[1], rows // 2
    slab_rows = (len(msgs) + 1) * pooled.size // width
    keep, send, slab = small_call(
        functools.partial(collect_halves_kernel, start, rows),
        [((half, width), BF), ((half, width), BF), ((slab_rows, width), BF)],
        "collect_terms",
        *(own, pooled, odd, *[msgs[i] for i in (2, 0, 1)]),
    )
    first = small_call(
        functools.partial(add_and_append_kernel, half, 1),
        [((half + slab_rows, width), BF)],
        "merge_slabs",
        *(keep, swap(send, "dp", 1), slab),
        tokens=token,
    )[0]
    far = swap(first, "dp", 2)
    mine = small_call(
        functools.partial(add_and_append_kernel, half, 2),
        [((half + 2 * slab_rows, width), BF)],
        "merge_slabs",
        *(first, far, first, far),
        tokens=late,
    )[0]
    return mine, swap(mine, "dp", 1)


def final_halves(odd, mine, other, pieces, out):
    tail = pieces[0].shape[0]
    head = out.shape[0] - tail
    half = head // 2
    pick = choose(odd, out.shape[1])
    left, right = mine[0:half].astype(F32), other[0:half].astype(F32)
    out[0:half] = jnp.where(pick, right, left)
    out[half:head] = jnp.where(pick, left, right)
    out[head:] = pieces[0][...].astype(F32) + pieces[1][...].astype(F32)


def final_whole(pieces, out):
    tail = pieces[2].shape[0]
    head = out.shape[0] - tail
    out[0:head] = pieces[0][0:head].astype(F32) + pieces[1][0:head].astype(F32)
    out[head:] = pieces[2][...].astype(F32) + pieces[3][...].astype(F32)


def proj_sum(slabs, images, order, rows, own_ge, mine, other, tails, out):
    count, embed = out.shape
    groups = mine.shape[1] // count
    half = slabs * images // 2
    per = (mine.shape[0] - rows) // (slabs // 2)
    together = per // (2 * images)
    parts = []
    for j in range(slabs):
        pieces = [own_ge[j].astype(BF)]
        start, left = j * images % half, j * images // half * embed
        base = start // 16 * 16
        for k in range(0, tails[0].shape[0], half):
            pair = [t[k + base : k + base + 16, left : left + embed].astype(F32) for t in tails]
            pieces.append(jnp.concatenate([p[start - base : start - base + images] for p in pair], axis=0).astype(BF))
        at = order.index(j)
        ref, at = (mine, at) if at < slabs // 2 else (other, at - slabs // 2)
        total = jnp.zeros((count, embed), F32)
        for g in range(groups):
            pooled = ref[rows + at * per : rows + (at + 1) * per, g * count : (g + 1) * count]
            grads = jnp.concatenate(pieces[g * together : (g + 1) * together], axis=0)
            total = total + dot(pooled, grads, TN)
        parts.append(total)
    while len(parts) > 1:
        parts = [parts[k] + parts[k + 1] for k in range(0, len(parts), 2)]
    out[...] = parts[0]


def gate_kernel(x, token, out):
    out[...] = x[...]


def after(x, token):
    return small_call(gate_kernel, [(x.shape, x.dtype)], "gate", x, tokens=(token,))[0]


def part_kernel(start, x, token, out):
    out[...] = x[start : start + out.shape[0]]


def half_of(start, x, token):
    shape = (x.shape[0] // 2, x.shape[1])
    return small_call(functools.partial(part_kernel, start), [(shape, x.dtype)], "half_of", x, tokens=(token,))[0]


def last_sums_kernel(slabs, images, order, rows, own_ge, odd, last_mine, last_other, mine, other, *refs):
    tails, (conv_out, proj_out, conv, proj, sems) = refs[:-5], refs[-5:]
    if slabs == 4:
        final_halves(odd, mine, other, (last_mine, last_other), conv)
    else:
        final_whole((mine, other, last_mine, last_other), conv)
    conv_copy = pltpu.make_async_copy(conv, conv_out, sems.at[0])
    conv_copy.start()
    proj_sum(slabs, images, order, rows, own_ge, mine, other, tails, proj)
    proj_copy = pltpu.make_async_copy(proj, proj_out, sems.at[1])
    proj_copy.start()
    conv_copy.wait()
    proj_copy.wait()


def swap(x, axis, bit):
    size = lax.axis_size(axis)
    return lax.ppermute(x, axis, [(i, i ^ bit) for i in range(size)])


def gather_slabs(x, slabs):
    if slabs <= 4:
        return [x] + [swap(x, "dp", j) for j in range(1, slabs)]
    whole = lax.all_gather(x, "dp", axis=0, tiled=False)
    return [jnp.take(whole, lax.axis_index("dp") ^ jnp.arange(slabs), axis=0)]


def local(features, shortcut, conv_weight, proj_weight, partner):
    slabs, groups = lax.axis_size("dp"), lax.axis_size("fsdp")
    peers = groups // 2
    images = features.shape[0] // POS
    count, width = conv_weight.shape
    place = lax.axis_index("dp").astype(jnp.int32).reshape(1)
    index = lax.axis_index("fsdp").astype(jnp.int32).reshape(1)

    f_sib = swap(features, "fsdp", 1)
    s_sib = swap(shortcut, "fsdp", 1)
    shorts = (shortcut, s_sib)
    first, embed, f_own, proj_own, member = forward_first(
        index, partner, (features, f_sib), shorts, conv_weight, proj_weight, images
    )
    feats = (f_own, f_sib)
    projs = [swap(proj_weight, "fsdp", 2 * j) for j in range(1, peers)]
    if peers == 4:
        conv_y = swap(conv_weight, "fsdp", 4)
        conv_x = swap(conv_weight, "fsdp", 2)
        halves = [
            swap(half_of(0, conv_y, embed), "fsdp", 2),
            swap(half_of(count // 2, conv_x, embed), "fsdp", 4),
        ]
        convs = [conv_x, conv_y, halves]
    else:
        convs = [swap(conv_weight, "fsdp", 2 * j) for j in range(1, peers)]
        convs[-1] = [convs[-1]]
    middle, embed, ahead = forward_middle(index, feats, shorts, convs[:-1], projs[:-1], images, embed)
    last, mine, send = forward_last(feats, ahead, convs[-1], projs[-1], images, embed, member)
    blocks, projs = [first, *middle, last], [proj_own, *projs]
    blocks = [(*b, p) for b, p in zip(blocks, projs)]
    embeds = sum_of(F32, mine, swap(send, "fsdp", 1))
    ge, loss, odd = hsic(place, gather_slabs(embeds, slabs), proj_weight.shape[1], slabs, images, groups)

    first_rows = count * SPLIT // 8
    parts = [(0, first_rows), (first_rows, count - first_rows)]
    terms, done = [], ()
    for part, extra in zip(parts, ("pooled", "embed")):
        if terms:
            (own,) = backward(feats, ge, blocks[:1], images, (0, count), None, done)
            done = (own,)
        done = tuple(backward(feats, ge, blocks[1:], images, part, extra, done))
        terms.append(done)

    received = [[swap(m, "fsdp", 2 * j) for j, m in enumerate(term, 1)] for term in terms]
    total, tails = collect_grads(own, received[1], parts[1])
    if slabs == 4:
        merged = merge(parts[1][1], total, swap(total, "dp", 1))
        mine, other = sum_by_halves(own, blocks[0][2], odd, received[0], parts[0], (total,), (merged,))
        pieces = [mine, other, merged, swap(merged, "dp", 2)]
        order, above = [0, 2, 1, 3], parts[0][1] // 2
    else:
        pieces, order, above = [], list(range(slabs)), parts[0][1]
        for piece, part in zip((collect(own, blocks[0][2], received[0], parts[0], True, ()), total), parts):
            bit = 1
            while 2 * bit < slabs:
                piece = merge(part[1], piece, swap(piece, "dp", bit))
                bit *= 2
            pieces += [piece, swap(piece, "dp", bit)]
    arrays = (ge, odd, pieces[2], pieces[3], pieces[0], pieces[1], tails, swap(tails, "fsdp", 1))
    shapes = [(count, width), proj_weight.shape]
    grad_conv, grad_proj = pl.pallas_call(
        functools.partial(last_sums_kernel, slabs, images, order, above),
        in_specs=[vspec()] * len(arrays),
        out_specs=[pl.BlockSpec(memory_space=pl.ANY)] * 2,
        out_shape=[jax.ShapeDtypeStruct(shape, F32) for shape in shapes],
        scratch_shapes=[pltpu.VMEM(shape, F32) for shape in shapes] + [pltpu.SemaphoreType.DMA((2,))],
        compiler_params=params(),
        cost_estimate=pl.CostEstimate(flops=0, bytes_accessed=0, transcendentals=0),
        name="last_sums",
    )(*arrays)
    return grad_conv, grad_proj, loss.reshape(1)


def solution(mesh):
    return jax.shard_map(
        local,
        mesh=mesh,
        in_specs=(
            P(("dp", "fsdp"), None),
            P(("dp", "fsdp"), None),
            P("fsdp", None),
            P("fsdp", None),
            P(("dp", "fsdp")),
        ),
        out_specs=(P("fsdp", None), P("fsdp", None), P("fsdp")),
        check_vma=False,
    )
```
